256 devices in a mesh: section: 4 (over x_hi, core), lat: 8 (over z), lon: 8 (over x_lo, y).
Axes of the slice: x: 4 (x_hi: 2, x_lo: 2; x = x_hi * 2 + x_lo), y: 4, z: 8, core: 2. Of those that a mesh axis runs over, the one named last changes fastest.
Arguments:
- states: bfloat16 [4, 1, 192, 96, 192], P('section', None, 'lat', 'lon'), may hold values from -60 to 60
- loss_grads: bfloat16 [4, 1, 192, 96, 192], P('section', None, 'lat', 'lon'), may hold values from -6 to 6
- land_sea: int32 [192, 96], P('lat', 'lon'), may hold values 0 or 1
- land_embed: float32 [192], replicated, may hold values from -4 to 4
- gain_attn: float32 [192], replicated, may hold values from 0.5 to 1.5
- gain_mlp: float32 [192], replicated, may hold values from 0.5 to 1.5
- w_qkv: bfloat16 [192, 576], replicated, may hold values from -0.4375 to 0.4375
- w_out: bfloat16 [192, 192], replicated, may hold values from -0.4375 to 0.4375
- w_up: bfloat16 [192, 768], replicated, may hold values from -0.4375 to 0.4375
- w_down: bfloat16 [768, 192], replicated, may hold values from -0.21875 to 0.21875
Outputs:
- state_grads: float32 [4, 1, 192, 96, 192], P('section', None, 'lat', 'lon')
- grad_qkv: float32 [192, 576], replicated
- grad_out: float32 [192, 192], replicated
- grad_up: float32 [192, 768], replicated
- grad_down: float32 [768, 192], replicated
- grad_land: float32 [192], replicated
- grad_gain_attn: float32 [192], replicated
- grad_gain_mlp: float32 [192], replicated
The draws below stay inside these ranges and needn't reach their ends.
All inputs are finite; a program needn't handle non-finite values. No bound on the sum of `land_sea` on one device may be relied on, other than what follows from the above.
Results may differ from the reference program's by a relative error of at most 0.015.
Values may be sent and summed in bfloat16 or wider, within the bound.
No kernel may reach another device: no remote copies, remote signals or barrier semaphores. Data moves between devices by JAX's collectives and lax.ppermute only.
A program may use at most 64 MiB of HBM per device.

```python
import math
import jax
import jax.numpy as jnp
from jax import lax

CHANNELS = 192
HEADS = 6
MLP_WIDTH = 768
HEAD_DIM = 32
LEVELS = 1
WIN_LAT = 6
WIN_LON = 12
SECTIONS = 4
LAT_ALL = 192
LON_ALL = 96


def draw_states(key, part):
    key = jax.random.fold_in(key, 11)
    chan_key, token_key, base_key = jax.random.split(key, 3)
    shape = (SECTIONS, LEVELS, LAT_ALL, LON_ALL, CHANNELS)
    channel_scale = jnp.exp(jax.random.uniform(chan_key, (CHANNELS,), jnp.float32, math.log(0.3), math.log(3.0)))
    token_scale = jnp.exp(jax.random.uniform(token_key, (SECTIONS, LEVELS, LAT_ALL, LON_ALL, 1), jnp.float32, math.log(0.5), math.log(5.0)))
    base = jnp.clip(jax.random.normal(base_key, shape, jnp.float32), -4.0, 4.0)
    return (base * channel_scale * token_scale).astype(jnp.bfloat16)


def place_ends(drawn, rng, least, high):
    index_at = [jax.random.randint(jax.random.fold_in(rng, axis), (), 0, length) for axis, length in enumerate(drawn.shape)]
    longest = drawn.shape.index(max(drawn.shape))
    next_to = index_at[:longest] + [(index_at[longest] + 1) % drawn.shape[longest]] + index_at[longest + 1:]
    return drawn.at[tuple(index_at)].set(least).at[tuple(next_to)].set(high)


def levels(rng, dims, shards, smallest, top_value):
    level = 1.0
    for dim, parts in shards:
        heights = jax.random.uniform(jax.random.fold_in(jax.random.fold_in(rng, 6), dim), (parts,), jnp.float32, smallest / len(shards), top_value / len(shards))
        level = level * jnp.repeat(jnp.exp(heights), dims[dim] // parts).reshape((-1,) + (1,) * (len(dims) - 1 - dim))
    return level


def normal_values(stream_key, dims, deviation, limit, pieces=(), kind=jnp.bfloat16):
    entries = deviation * jax.random.normal(stream_key, dims, jnp.float32)
    if pieces:
        entries = entries * levels(stream_key, dims, pieces, -0.22, 0.18)
    return jnp.clip(entries, -limit, limit).astype(kind)


def setup_inputs(seed: int = 0) -> dict:
    splits = jax.random.split(jax.random.key(seed), 11)
    return {
        "states": draw_states(jax.random.fold_in(splits[10], 71), 0),
        "loss_grads": normal_values(splits[1], (SECTIONS, LEVELS, LAT_ALL, LON_ALL, CHANNELS), 1.0, 6.0, ((0, 4), (2, 8), (3, 8))),
        "land_sea": place_ends((jax.random.randint(splits[2], (LAT_ALL, LON_ALL), 0, 10) < 3).astype(jnp.int32), jax.random.fold_in(splits[2], 1), 0, 1),
        "land_embed": normal_values(splits[3], (CHANNELS,), 1.0, 4.0, (), jnp.float32),
        "gain_attn": jnp.clip(1.0 + 0.1 * jax.random.normal(splits[4], (CHANNELS,), jnp.float32), 0.5, 1.5),
        "gain_mlp": jnp.clip(1.0 + 0.1 * jax.random.normal(splits[5], (CHANNELS,), jnp.float32), 0.5, 1.5),
        "w_qkv": normal_values(splits[6], (CHANNELS, 3 * CHANNELS), CHANNELS ** -0.5, 0.4375),
        "w_out": normal_values(splits[7], (CHANNELS, CHANNELS), CHANNELS ** -0.5, 0.4375),
        "w_up": normal_values(splits[8], (CHANNELS, MLP_WIDTH), CHANNELS ** -0.5, 0.4375),
        "w_down": normal_values(splits[9], (MLP_WIDTH, CHANNELS), MLP_WIDTH ** -0.5, 0.21875),
    }


EPS = 1e-05

def normalize(field, gain):
    centre = lax.optimization_barrier(jnp.mean(field, axis=-1, keepdims=True))
    offset = field - centre
    spread = lax.optimization_barrier(jnp.mean(offset * offset, axis=-1, keepdims=True))
    return offset * lax.rsqrt(spread + EPS) * gain

def exact_gelu(values):
    return jax.nn.gelu(values, approximate=False)

def to_windows(field):
    depth, height, breadth, width = field.shape
    grid = field.reshape(depth, height // WIN_LAT, WIN_LAT, breadth // WIN_LON, WIN_LON, width)
    grid = grid.transpose(1, 3, 0, 2, 4, 5)
    return grid.reshape(height // WIN_LAT, breadth // WIN_LON, depth * WIN_LAT * WIN_LON, width)

def from_windows(blocks, depth):
    band_count, cell_count, tokens, width = blocks.shape
    grid = blocks.reshape(band_count, cell_count, depth, WIN_LAT, WIN_LON, width)
    grid = grid.transpose(2, 0, 3, 1, 4, 5)
    return grid.reshape(depth, band_count * WIN_LAT, cell_count * WIN_LON, width)

def allowed_pairs(first_row, total_rows, band_count, depth):
    row_ids = first_row + jnp.arange(band_count * WIN_LAT, dtype=jnp.int32)
    source = (row_ids + WIN_LAT // 2) % total_rows
    labels = (source < WIN_LAT // 2).astype(jnp.int32).reshape(band_count, 1, WIN_LAT, 1)
    labels = jnp.broadcast_to(labels, (band_count, depth, WIN_LAT, WIN_LON))
    labels = labels.reshape(band_count, depth * WIN_LAT * WIN_LON)
    return (labels[:, :, None] == labels[:, None, :]).astype(jnp.float32)

def heads_of(block):
    band_count, cell_count, tokens, width = block.shape
    return block.reshape(band_count, cell_count, tokens, HEADS, width // HEADS)

def merge_heads(block):
    band_count, cell_count, tokens, heads, size = block.shape
    return block.reshape(band_count, cell_count, tokens, heads * size)

def attend(qkv_win, allow):
    width = qkv_win.shape[-1] // 3
    query = heads_of(qkv_win[..., :width]).astype(jnp.float32)
    keys = heads_of(qkv_win[..., width:2 * width]).astype(jnp.float32)
    values = heads_of(qkv_win[..., 2 * width:]).astype(jnp.float32)
    scores = jnp.einsum('abqhd,abkhd->abhqk', query, keys) * HEAD_DIM ** (-0.5)
    weights = jnp.exp(scores) * allow[:, None, None]
    probs = weights / lax.optimization_barrier(jnp.sum(weights, axis=-1, keepdims=True))
    rounded = lax.optimization_barrier(probs.astype(jnp.bfloat16)).astype(jnp.float32)
    mixed = jnp.einsum('abhqk,abkhd->abqhd', rounded, values)
    return (probs, merge_heads(mixed).astype(jnp.bfloat16))

def attend_back(qkv_win, probs, d_mixed):
    width = qkv_win.shape[-1] // 3
    query = heads_of(qkv_win[..., :width]).astype(jnp.float32)
    keys = heads_of(qkv_win[..., width:2 * width]).astype(jnp.float32)
    values = heads_of(qkv_win[..., 2 * width:]).astype(jnp.float32)
    d_heads = heads_of(d_mixed).astype(jnp.float32)
    rounded = lax.optimization_barrier(probs.astype(jnp.bfloat16)).astype(jnp.float32)
    d_probs = jnp.einsum('abqhd,abkhd->abhqk', d_heads, values)
    d_values = jnp.einsum('abhqk,abqhd->abkhd', rounded, d_heads)
    d_scores = probs * (d_probs - lax.optimization_barrier(jnp.sum(probs * d_probs, axis=-1, keepdims=True))) * HEAD_DIM ** (-0.5)
    d_scores = lax.optimization_barrier(d_scores.astype(jnp.bfloat16)).astype(jnp.float32)
    d_query = jnp.einsum('abhqk,abkhd->abqhd', d_scores, keys)
    d_keys = jnp.einsum('abhqk,abqhd->abkhd', d_scores, query)
    joined = jnp.concatenate([merge_heads(d_query), merge_heads(d_keys), merge_heads(d_values)], axis=-1)
    return joined.astype(jnp.bfloat16)

def attend_bands(qkv_win, allow):

    def one_band(item):
        probs, mixed = attend(item[0][None], item[1][None])
        return (probs[0], mixed[0])
    return lax.map(one_band, (qkv_win, allow))

def attend_back_bands(qkv_win, probs, d_mixed):

    def one_band(item):
        return attend_back(item[0][None], item[1][None], item[2][None])[0]
    return lax.map(one_band, (qkv_win, probs, d_mixed))

def roll_ahead(field):
    return jnp.roll(field, (-(WIN_LAT // 2), -(WIN_LON // 2)), axis=(1, 2))

def roll_behind(field):
    return jnp.roll(field, (WIN_LAT // 2, WIN_LON // 2), axis=(1, 2))

def section_backward(state, cotangent, land, land_embed, gain_attn, gain_mlp, w_qkv, w_out, w_up, w_down):
    depth, height, breadth, width = state.shape
    embedded = state.astype(jnp.float32) + land * land_embed
    normed, attn_back = jax.vjp(normalize, embedded, gain_attn)
    normed = normed.astype(jnp.bfloat16)
    rolled = roll_ahead(normed).reshape(-1, width)
    qkv = jnp.dot(rolled, w_qkv, preferred_element_type=jnp.float32).astype(jnp.bfloat16)
    qkv_win = to_windows(qkv.reshape(depth, height, breadth, 3 * width))
    allow = allowed_pairs(0, height, height // WIN_LAT, depth)
    probs, mixed_win = attend_bands(qkv_win, allow)
    mixed = from_windows(mixed_win, depth).reshape(-1, width)
    projected = jnp.dot(mixed, w_out, preferred_element_type=jnp.float32).astype(jnp.bfloat16)
    hidden_in = embedded + roll_behind(projected.reshape(depth, height, breadth, width)).astype(jnp.float32)
    normed_mlp, mlp_back = jax.vjp(normalize, hidden_in, gain_mlp)
    normed_mlp = normed_mlp.astype(jnp.bfloat16).reshape(-1, width)
    pre_act = jnp.dot(normed_mlp, w_up, preferred_element_type=jnp.float32)
    activated, gelu_back = jax.vjp(exact_gelu, pre_act)
    activated = activated.astype(jnp.bfloat16)
    cot_round = cotangent.astype(jnp.bfloat16).reshape(-1, width)
    grad_down = jnp.dot(activated.T, cot_round, preferred_element_type=jnp.float32)
    d_act = jnp.dot(cot_round, w_down.T, preferred_element_type=jnp.float32)
    d_pre = gelu_back(d_act)[0].astype(jnp.bfloat16)
    grad_up = jnp.dot(normed_mlp.T, d_pre, preferred_element_type=jnp.float32)
    d_normed_mlp = jnp.dot(d_pre, w_up.T, preferred_element_type=jnp.float32).reshape(depth, height, breadth, width)
    d_hidden, grad_gain_mlp = mlp_back(d_normed_mlp)
    d_hidden = cotangent + d_hidden
    d_projected = roll_ahead(d_hidden.astype(jnp.bfloat16)).reshape(-1, width)
    grad_out = jnp.dot(mixed.T, d_projected, preferred_element_type=jnp.float32)
    d_mixed = jnp.dot(d_projected, w_out.T, preferred_element_type=jnp.float32).astype(jnp.bfloat16)
    d_qkv_win = attend_back_bands(qkv_win, probs, to_windows(d_mixed.reshape(depth, height, breadth, width)))
    d_qkv = from_windows(d_qkv_win, depth).reshape(-1, 3 * width)
    grad_qkv = jnp.dot(rolled.T, d_qkv, preferred_element_type=jnp.float32)
    d_rolled = jnp.dot(d_qkv, w_qkv.T, preferred_element_type=jnp.float32).astype(jnp.bfloat16)
    d_normed = roll_behind(d_rolled.reshape(depth, height, breadth, width)).astype(jnp.float32)
    d_embedded, grad_gain_attn = attn_back(d_normed)
    d_state = d_hidden + d_embedded
    grad_land = lax.optimization_barrier(jnp.sum(d_state * land, axis=(0, 1, 2)))
    return (d_state, (grad_qkv, grad_out, grad_up, grad_down, grad_land, grad_gain_attn, grad_gain_mlp))

def reference(states, loss_grads, land_sea, land_embed, gain_attn, gain_mlp, w_qkv, w_out, w_up, w_down):
    land = land_sea.astype(jnp.float32)[None, :, :, None]
    incoming = jnp.zeros(states.shape[1:], jnp.float32)
    results = []
    totals = None
    for section_number in range(SECTIONS - 1, -1, -1):
        cotangent = loss_grads[section_number].astype(jnp.float32) + incoming
        d_state, grads = section_backward(states[section_number], cotangent, land, land_embed, gain_attn, gain_mlp, w_qkv, w_out, w_up, w_down)
        results.append(d_state)
        totals = grads if totals is None else jax.tree.map(jnp.add, totals, grads)
        incoming = lax.optimization_barrier(d_state.astype(jnp.bfloat16)).astype(jnp.float32)
    state_grads = jnp.stack(results[::-1])
    factor = float(SECTIONS * LEVELS * LAT_ALL * LON_ALL) ** (-0.5)
    return (state_grads, totals[0] * factor, totals[1] * factor, totals[2] * factor, totals[3] * factor, totals[4] * factor, totals[5] * factor, totals[6] * factor)
```

```python
import jax
import jax.numpy as jnp
from jax import lax
from jax.experimental import pallas as pl
from jax.experimental.pallas import tpu as pltpu
from jax.sharding import PartitionSpec as P

CH = 192
HEADS = 6
HEAD_DIM = 32
MLP = 768
HALF_LAT = 3
HALF_LON = 6
QUAD = HALF_LAT * HALF_LON
WIN = 4 * QUAD
STEPS = 4
TOK = STEPS * WIN
MSG = 512
GROUPS = 64
UNIT = 16
USED = 55
PART = USED * UNIT
SCALE = HEAD_DIM ** (-0.5)
EPS = 1e-05
F32 = jnp.float32
BF16 = jnp.bfloat16
VMEM_LIMIT = 60 * 1024 * 1024


def nn(a, b):
    return lax.dot_general(a, b, (((1,), (0,)), ((), ())), preferred_element_type=F32)


def nt(a, b):
    return lax.dot_general(a, b, (((1,), (1,)), ((), ())), preferred_element_type=F32)


def tn(a, b):
    return lax.dot_general(a, b, (((0,), (0,)), ((), ())), preferred_element_type=F32)


def mean_of(v):
    return jnp.sum(v, axis=-1, keepdims=True) * (1.0 / CH)


def pack_kernel(states, loss, land, out, cells):
    for k in range(4):
        for rh in range(2):
            for r in range(HALF_LAT):
                row = 6 * k + 3 * rh + r
                st = states[row].astype(F32)
                lo = loss[row].astype(F32)
                la = land[row].astype(F32)
                for ch in range(2):
                    q = 2 * rh + ch
                    here = slice(6 * r, 6 * r + 6)
                    cols = slice(6 * ch, 6 * ch + 6)
                    wide = jnp.broadcast_to(la[cols], (6, 64))
                    cells[k, q, here, 0:192] = st[cols]
                    cells[k, q, here, 192:256] = wide
                    cells[k, q, here, 256:448] = lo[cols]
                    cells[k, q, here, 448:512] = wide
    out[...] = cells[...].astype(BF16)


def main_kernel(
    own, right, below, corner, embed, gain_a, gain_m, wqkv, wout, wup, wdown,
    grads_out, msg_out,
    x, qkv, probs, qm_all, emb, xh1, r1, hid_xh, r2, gp, act, normed_s, mixed_s, nm_s,
    cot_s, dpre_s, dproj_s, dqkv_s, dstate, small,
):
    last = jnp.logical_and(lax.axis_index("lat") == 7, lax.axis_index("section") == 3)
    closed = jnp.where(last, 0.0, 1.0).astype(F32)
    for s in range(STEPS):
        for q, piece in enumerate((own, right, below, corner)):
            at = WIN * s + QUAD * q
            x[at : at + QUAD, :] = piece[s].astype(F32)
    land_full = lambda rows: jnp.concatenate([x[rows, 448:512]] * 3, axis=1)
    le = embed[...]
    ga = gain_a[...]
    gm = gain_m[...]
    col_head = lax.broadcasted_iota(jnp.int32, (1, CH), 1) // HEAD_DIM
    masks = [(col_head == h).astype(F32) for h in range(HEADS)]
    row_half = lax.broadcasted_iota(jnp.int32, (WIN, WIN), 0) // (2 * QUAD)
    key_half = lax.broadcasted_iota(jnp.int32, (WIN, WIN), 1) // (2 * QUAD)
    allow1 = jnp.where(row_half == key_half, 1.0, closed).astype(F32)
    allow = jnp.concatenate([allow1] * HEADS, axis=0)

    def spread(v):
        return jnp.concatenate([v * m for m in masks], axis=0).astype(BF16)

    def gathered(v):
        total = v[0:WIN] * masks[0]
        for h in range(1, HEADS):
            total = total + v[WIN * h : WIN * h + WIN] * masks[h]
        return total

    for s in range(STEPS):
        rows = slice(WIN * s, WIN * s + WIN)
        land = x[rows, 192:256][:, 0:1]
        e = x[rows, 0:CH] + land * le
        emb[rows, :] = e
        off = e - mean_of(e)
        r = lax.rsqrt(mean_of(off * off) + EPS)
        xh = off * r
        xh1[rows, :] = xh
        r1[rows, :] = r
        normed_s[rows, :] = (xh * ga)
    normed = normed_s[...].astype(BF16)
    qkv[...] = nn(normed, wqkv[...]).astype(BF16).astype(F32)
    for s in range(STEPS):
        rows = slice(WIN * s, WIN * s + WIN)
        qm = spread(qkv[rows, 0:CH])
        qm_all[s] = qm
        keys = qkv[rows, CH : 2 * CH].astype(BF16)
        values = qkv[rows, 2 * CH : 3 * CH].astype(BF16)
        weights = jnp.exp(nt(qm, keys) * SCALE) * allow
        p = weights / jnp.sum(weights, axis=-1, keepdims=True)
        probs[s] = p
        mixed_s[rows, :] = gathered(nn(p.astype(BF16), values))
    mixed = mixed_s[...].astype(BF16)
    projected = nn(mixed, wout[...]).astype(BF16).astype(F32)
    hid = emb[...] + projected
    off = hid - mean_of(hid)
    r = lax.rsqrt(mean_of(off * off) + EPS)
    xh = off * r
    hid_xh[...] = xh
    r2[...] = r
    nm = (xh * gm).astype(BF16)
    nm_s[...] = nm
    for j in range(MLP // 256):
        cols = slice(256 * j, 256 * j + 256)
        pre = nn(nm_s[...], wup[:, cols])
        cdf = 0.5 * (1.0 + lax.erf(pre * (0.5 ** 0.5)))
        pdf = jnp.exp(pre * pre * -0.5) * 0.3989422804014327
        act[:, cols] = (pre * cdf).astype(BF16)
        gp[:, cols] = cdf + pre * pdf

    gain_m_sum = jnp.zeros((1, CH), F32)
    gain_a_sum = jnp.zeros((1, CH), F32)
    land_sum = jnp.zeros((1, CH), F32)
    incoming = None
    wq = wqkv[:, 0:CH]
    wk = wqkv[:, CH : 2 * CH]
    wv = wqkv[:, 2 * CH : 3 * CH]
    for s in range(STEPS - 1, -1, -1):
        rows = slice(WIN * s, WIN * s + WIN)
        cot = x[rows, 256:448]
        if incoming is not None:
            cot = cot + incoming
        cotb = cot.astype(BF16)
        cot_s[rows, :] = cotb.astype(F32)
        d_pre = gp[rows, :] * nt(cotb, wdown[...])
        dpre_b = d_pre.astype(BF16)
        dpre_s[rows, :] = dpre_b.astype(F32)
        dy = nt(dpre_b, wup[...])
        xh = hid_xh[rows, :]
        gain_m_sum = gain_m_sum + jnp.sum(dy * xh, axis=0, keepdims=True)
        dxh = dy * gm
        d_hid = cot + r2[rows, :] * (dxh - mean_of(dxh) - xh * mean_of(dxh * xh))
        dproj = d_hid.astype(BF16)
        dproj_s[rows, :] = dproj.astype(F32)
        d_mixed = nt(dproj, wout[...]).astype(BF16).astype(F32)
        dm = spread(d_mixed)
        keys = qkv[rows, CH : 2 * CH].astype(BF16)
        values = qkv[rows, 2 * CH : 3 * CH].astype(BF16)
        p = probs[s]
        dp = nt(dm, values)
        dv = tn(p.astype(BF16), dm).astype(BF16)
        ds = (p * (dp - jnp.sum(p * dp, axis=-1, keepdims=True)) * SCALE).astype(BF16)
        dq = gathered(nn(ds, keys)).astype(BF16)
        dk = tn(ds, qm_all[s]).astype(BF16)
        dqkv_s[rows, 0:CH] = dq.astype(F32)
        dqkv_s[rows, CH : 2 * CH] = dk.astype(F32)
        dqkv_s[rows, 2 * CH : 3 * CH] = dv.astype(F32)
        d_rolled = nt(dq, wq) + nt(dk, wk) + nt(dv, wv)
        dy = d_rolled.astype(BF16).astype(F32)
        xh = xh1[rows, :]
        gain_a_sum = gain_a_sum + jnp.sum(dy * xh, axis=0, keepdims=True)
        dxh = dy * ga
        d_state = d_hid + r1[rows, :] * (dxh - mean_of(dxh) - xh * mean_of(dxh * xh))
        land = x[rows, 192:256][:, 0:1]
        land_sum = land_sum + jnp.sum(d_state * land, axis=0, keepdims=True)
        d_round = d_state.astype(BF16)
        incoming = d_round.astype(F32)
        dstate[...] = incoming
        for q in range(4):
            grads_out[q, s] = dstate[QUAD * q : QUAD * q + QUAD, :].astype(BF16)

    factor = float(STEPS * 192 * 96) ** (-0.5)

    def put(tile, value):
        for j in range(value.shape[1] // 128):
            at = (tile + j) * CH
            left = at
            done = 0
            while done < CH:
                part, row = divmod(left, PART)
                n = min(CH - done, PART - row)
                msg_out[part, row : row + n, :] = value[done : done + n, 128 * j : 128 * j + 128]
                done += n
                left += n

    cot_all = cot_s[...].astype(BF16)
    put(12, (tn(cot_all, act[...]) * factor).astype(BF16))
    put(6, (tn(nm_s[...], dpre_s[...].astype(BF16)) * factor).astype(BF16))
    g_qkv = tn(normed_s[...].astype(BF16), dqkv_s[...].astype(BF16)) * factor
    g_out = tn(mixed_s[...].astype(BF16), dproj_s[...].astype(BF16)) * factor
    put(0, jnp.concatenate([g_qkv, g_out], axis=1).astype(BF16))
    small[...] = jnp.zeros_like(small)
    for i, total in enumerate((land_sum, gain_a_sum, gain_m_sum)):
        total = total * factor
        small[2 * i : 2 * i + 1, :] = total[:, 0:128]
        small[2 * i + 1 : 2 * i + 2, 0:64] = total[:, 128:192]
    at = 18 * CH - 3 * PART
    msg_out[3, at:PART, :] = small[...].astype(BF16)


SMALL_ROWS = 4 * PART - 18 * CH


def unpack_kernel(msg, grads, state_out, g_qkv, g_out, g_up, g_down, g_land, g_ga, g_gm, cells):
    def rows_of(at, count):
        pieces = []
        done = 0
        while done < count:
            part, row = divmod(at + done, PART)
            n = min(count - done, PART - row)
            pieces.append(msg[part, row : row + n, :].astype(F32))
            done += n
        return pieces[0] if len(pieces) == 1 else jnp.concatenate(pieces, axis=0)

    for j in range(4):
        g_qkv[:, 128 * j : 128 * j + 128] = rows_of(j * CH, CH)
    mid = rows_of(4 * CH, CH)
    tail = rows_of(5 * CH, CH)
    g_qkv[:, 512:576] = mid[:, 0:64]
    g_out[...] = jnp.concatenate([mid[:, 64:128], tail], axis=1)
    for j in range(6):
        g_up[:, 128 * j : 128 * j + 128] = rows_of((6 + j) * CH, CH)
    for j in range(6):
        g_down[128 * j : 128 * j + 128, :] = rows_of((12 + j) * CH, CH).T
    small = rows_of(18 * CH, 16)
    for i, out in enumerate((g_land, g_ga, g_gm)):
        out[...] = jnp.concatenate([small[2 * i : 2 * i + 1, :], small[2 * i + 1 : 2 * i + 2, 0:64]], axis=1)
    cells[...] = grads[...].astype(F32)
    for k in range(4):
        for rh in range(2):
            for r in range(HALF_LAT):
                for ch in range(2):
                    state_out[6 * k + 3 * rh + r, 6 * ch : 6 * ch + 6, :] = cells[
                        k, 2 * rh + ch, 6 * r : 6 * r + 6, :
                    ]


def hop(value, rows, cols):
    pairs = []
    for k in range(4):
        for a in range(8):
            for b in range(8):
                band = (4 * a + k + rows) % 32
                to = ((band % 4) * 8 + band // 4) * 8 + (b + cols) % 8
                pairs.append(((k * 8 + a) * 8 + b, to))
    return lax.ppermute(value, ("section", "lat", "lon"), pairs)


def exchange(value, axis):
    return lax.all_to_all(value, axis, 0, 0, tiled=True)


def local(
    states, loss_grads, land_sea, land_embed, gain_attn, gain_mlp, w_qkv, w_out, w_up, w_down
):
    params = pltpu.CompilerParams(vmem_limit_bytes=VMEM_LIMIT)
    shape = jax.ShapeDtypeStruct
    packed = pl.pallas_call(
        pack_kernel,
        out_shape=shape((4, 4, QUAD, MSG), BF16),
        scratch_shapes=[pltpu.VMEM((4, 4, QUAD, MSG), F32)],
        compiler_params=params,
        name="pack_cells",
    )(states[0, 0], loss_grads[0, 0], land_sea[..., None])
    cells = exchange(packed, "section")
    right = hop(cells[:, 2], 0, -1)
    below = hop(cells[:, 1], -1, 0)
    corner = hop(cells[:, 0], -1, -1)
    vm = pltpu.VMEM
    grads, msg = pl.pallas_call(
        main_kernel,
        out_shape=(
            shape((4, STEPS, QUAD, CH), BF16),
            shape((4, PART, 128), BF16),
        ),
        scratch_shapes=[
            vm((TOK, MSG), F32),
            vm((TOK, 3 * CH), F32),
            vm((STEPS, HEADS * WIN, WIN), F32),
            vm((STEPS, HEADS * WIN, CH), BF16),
            vm((TOK, CH), F32),
            vm((TOK, CH), F32),
            vm((TOK, 1), F32),
            vm((TOK, CH), F32),
            vm((TOK, 1), F32),
            vm((TOK, MLP), F32),
            vm((TOK, MLP), BF16),
            vm((TOK, CH), F32),
            vm((TOK, CH), F32),
            vm((TOK, CH), BF16),
            vm((TOK, CH), F32),
            vm((TOK, MLP), F32),
            vm((TOK, CH), F32),
            vm((TOK, 3 * CH), F32),
            vm((WIN, CH), F32),
            vm((SMALL_ROWS, 128), F32),
        ],
        compiler_params=params,
        name="window_steps",
    )(
        cells[:, 3], right, below, corner,
        land_embed[None], gain_attn[None], gain_mlp[None], w_qkv, w_out, w_up, w_down,
    )

    home = jnp.stack([hop(grads[3], 1, 1), hop(grads[2], 1, 0), hop(grads[1], 0, 1), grads[0]], axis=1)
    home = exchange(home, "section")

    parts = exchange(msg, "section")
    part = jnp.sum(parts.astype(F32), axis=0).astype(BF16)
    part = jnp.pad(part, ((0, (GROUPS - USED) * UNIT), (0, 0))).reshape(GROUPS, UNIT, 128)
    mine = exchange(part, ("lat", "lon"))
    mine = jnp.sum(mine.astype(F32), axis=0).astype(BF16)
    whole = exchange(jnp.broadcast_to(mine[None], (GROUPS, UNIT, 128)), ("lat", "lon"))
    whole = whole.reshape(GROUPS * UNIT, 128)[:PART]
    msg = exchange(jnp.broadcast_to(whole[None], (4, PART, 128)), "section")

    outs = pl.pallas_call(
        unpack_kernel,
        out_shape=(
            shape((24, 12, CH), F32),
            shape((CH, 3 * CH), F32),
            shape((CH, CH), F32),
            shape((CH, MLP), F32),
            shape((MLP, CH), F32),
            shape((1, CH), F32),
            shape((1, CH), F32),
            shape((1, CH), F32),
        ),
        scratch_shapes=[pltpu.VMEM((4, 4, QUAD, CH), F32)],
        compiler_params=params,
        name="unpack_sums",
    )(msg, home)
    return (
        outs[0][None, None], outs[1], outs[2], outs[3], outs[4], outs[5][0], outs[6][0], outs[7][0],
    )


def solution(mesh):
    cell = P("section", None, "lat", "lon", None)
    return jax.shard_map(
        local,
        mesh=mesh,
        in_specs=(cell, cell, P("lat", "lon"), P(), P(), P(), P(), P(), P(), P()),
        out_specs=(cell, P(), P(), P(), P(), P(), P(), P()),
        check_vma=False,
    )
```

```python
import jax
import jax.numpy as jnp
from jax import lax
from jax.experimental import pallas as pl
from jax.experimental.pallas import tpu as pltpu
from jax.sharding import Mesh
from jax.sharding import PartitionSpec as P

CH = 192
HEADS = 6
HEAD_DIM = 32
MLP = 768
ROWS = 24
WIN_LAT = 6
WIN_LON = 12
WIN = WIN_LAT * WIN_LON
HALF = WIN // 2
STEPS = 4
TOK = STEPS * WIN
MSG = 512
EDGE = 8
GROUP = 16
UNIT = 112
SUMS = GROUP * UNIT
BLOCK = 48
QUARTER = 4 * BLOCK
SENT = SUMS + 2 * QUARTER
SCALE = HEAD_DIM ** (-0.5)
EPS = 1e-05
F32 = jnp.float32
BF16 = jnp.bfloat16
AXES = ("xh", "core", "lat", "lon")
MIB = 1024 * 1024


def nn(a, b):
    return lax.dot_general(a, b, (((1,), (0,)), ((), ())), preferred_element_type=F32)


def nt(a, b):
    return lax.dot_general(a, b, (((1,), (1,)), ((), ())), preferred_element_type=F32)


def tn(a, b):
    return lax.dot_general(a, b, (((0,), (0,)), ((), ())), preferred_element_type=F32)


def mean_of(v):
    return jnp.sum(v, axis=-1, keepdims=True) * (1.0 / CH)


def pack_kernel(states, loss, land, kept, to_lon, to_lat, to_both):
    mask = land[...].astype(F32)
    for c in range(WIN_LON):
        column = jnp.broadcast_to(mask[c : c + 1, :], (64, ROWS)).T
        cell = jnp.concatenate(
            [states[c].astype(F32), column, loss[c].astype(F32), column], axis=1
        )
        wide, edge = (to_lon, to_both) if c < 6 else (kept, to_lat)
        wide[c % 6] = cell.astype(BF16)
        edge[c % 6] = cell[0:EDGE].astype(BF16)


def window_kernel(kept, from_lon, from_lat, from_both, out, cells):
    for c in range(WIN_LON):
        wide, edge = (kept, from_lat) if c < 6 else (from_lon, from_both)
        column = wide[c % 6].astype(F32)
        after = edge[c % 6].astype(F32)
        for k in range(3):
            cells[k, 6 * c : 6 * c + 6, :] = column[6 * k + 3 : 6 * k + 9]
        cells[3, 6 * c : 6 * c + 3, :] = column[21:24]
        cells[3, 6 * c + 3 : 6 * c + 6, :] = after[0:3]
    out[...] = cells[...].astype(BF16)


def main_kernel(
    cells, embed, gain_a, gain_m, wqkv, wout, wup, wdown_t,
    send_out, keep_out,
    x, qkv, probs, qm_all, emb, xh1, r1, hid_xh, r2, gp, act, normed_s, mixed_s, nm_s,
    cot_s, dpre_s, dproj_s, dqkv_s, dstate, small, msg,
):
    core = lax.axis_index("core")
    third = jnp.logical_and(lax.axis_index("xh") == 1, core == 1)
    last = jnp.logical_and(lax.axis_index("lat") == 7, third)
    closed = jnp.where(last, 0.0, 1.0).astype(F32)
    for s in range(STEPS):
        x[WIN * s : WIN * s + WIN, :] = cells[s].astype(F32)
    le = embed[...]
    ga = gain_a[...]
    gm = gain_m[...]
    col_head = lax.broadcasted_iota(jnp.int32, (1, CH), 1) // HEAD_DIM
    masks = [(col_head == h).astype(F32) for h in range(HEADS)]
    row_half = lax.rem(lax.broadcasted_iota(jnp.int32, (WIN, WIN), 0), WIN_LAT) // 3
    key_half = lax.rem(lax.broadcasted_iota(jnp.int32, (WIN, WIN), 1), WIN_LAT) // 3
    allow1 = jnp.where(row_half == key_half, 1.0, closed).astype(F32)
    allow = jnp.concatenate([allow1] * HEADS, axis=0)

    def spread(v):
        return jnp.concatenate([v * m for m in masks], axis=0).astype(BF16)

    def gathered(v):
        total = v[0:WIN] * masks[0]
        for h in range(1, HEADS):
            total = total + v[WIN * h : WIN * h + WIN] * masks[h]
        return total

    for s in range(STEPS):
        rows = slice(WIN * s, WIN * s + WIN)
        land = x[rows, 192:256][:, 0:1]
        e = x[rows, 0:CH] + land * le
        emb[rows, :] = e
        off = e - mean_of(e)
        r = lax.rsqrt(mean_of(off * off) + EPS)
        xh = off * r
        xh1[rows, :] = xh
        r1[rows, :] = r
        normed_s[rows, :] = xh * ga
    normed = normed_s[...].astype(BF16)
    qkv[...] = nn(normed, wqkv[...]).astype(BF16).astype(F32)
    for s in range(STEPS):
        rows = slice(WIN * s, WIN * s + WIN)
        qm = spread(qkv[rows, 0:CH])
        qm_all[s] = qm
        keys = qkv[rows, CH : 2 * CH].astype(BF16)
        values = qkv[rows, 2 * CH : 3 * CH].astype(BF16)
        weights = jnp.exp(nt(qm, keys) * SCALE) * allow
        p = weights / jnp.sum(weights, axis=-1, keepdims=True)
        probs[s] = p
        mixed_s[rows, :] = gathered(nn(p.astype(BF16), values))
    mixed = mixed_s[...].astype(BF16)
    projected = nn(mixed, wout[...]).astype(BF16).astype(F32)
    hid = emb[...] + projected
    off = hid - mean_of(hid)
    r = lax.rsqrt(mean_of(off * off) + EPS)
    xh = off * r
    hid_xh[...] = xh
    r2[...] = r
    nm_s[...] = (xh * gm).astype(BF16)
    for j in range(MLP // 256):
        cols = slice(256 * j, 256 * j + 256)
        pre = nn(nm_s[...], wup[:, cols])
        cdf = 0.5 * (1.0 + lax.erf(pre * (0.5 ** 0.5)))
        pdf = jnp.exp(pre * pre * -0.5) * 0.3989422804014327
        act[:, cols] = (pre * cdf).astype(BF16)
        gp[:, cols] = cdf + pre * pdf

    gain_m_sum = jnp.zeros((1, CH), F32)
    gain_a_sum = jnp.zeros((1, CH), F32)
    land_sum = jnp.zeros((1, CH), F32)
    incoming = None
    wq = wqkv[:, 0:CH]
    wk = wqkv[:, CH : 2 * CH]
    wv = wqkv[:, 2 * CH : 3 * CH]
    zero_rows = jnp.zeros((BLOCK - HALF, 128), F32)
    dstate[...] = jnp.zeros_like(dstate)
    for s in range(STEPS - 1, -1, -1):
        rows = slice(WIN * s, WIN * s + WIN)
        cot = x[rows, 256:448]
        if incoming is not None:
            cot = cot + incoming
        cotb = cot.astype(BF16)
        cot_s[rows, :] = cotb.astype(F32)
        d_pre = gp[rows, :] * nn(cotb, wdown_t[...])
        dpre_b = d_pre.astype(BF16)
        dpre_s[rows, :] = dpre_b.astype(F32)
        dy = nt(dpre_b, wup[...])
        xh = hid_xh[rows, :]
        gain_m_sum = gain_m_sum + jnp.sum(dy * xh, axis=0, keepdims=True)
        dxh = dy * gm
        d_hid = cot + r2[rows, :] * (dxh - mean_of(dxh) - xh * mean_of(dxh * xh))
        dproj = d_hid.astype(BF16)
        dproj_s[rows, :] = dproj.astype(F32)
        d_mixed = nt(dproj, wout[...]).astype(BF16).astype(F32)
        dm = spread(d_mixed)
        keys = qkv[rows, CH : 2 * CH].astype(BF16)
        values = qkv[rows, 2 * CH : 3 * CH].astype(BF16)
        p = probs[s]
        dp = nt(dm, values)
        dv = tn(p.astype(BF16), dm).astype(BF16)
        ds = (p * (dp - jnp.sum(p * dp, axis=-1, keepdims=True)) * SCALE).astype(BF16)
        dq = gathered(nn(ds, keys)).astype(BF16)
        dk = tn(ds, qm_all[s]).astype(BF16)
        dqkv_s[rows, 0:CH] = dq.astype(F32)
        dqkv_s[rows, CH : 2 * CH] = dk.astype(F32)
        dqkv_s[rows, 2 * CH : 3 * CH] = dv.astype(F32)
        d_rolled = nt(dq, wq) + nt(dk, wk) + nt(dv, wv)
        dy = d_rolled.astype(BF16).astype(F32)
        xh = xh1[rows, :]
        gain_a_sum = gain_a_sum + jnp.sum(dy * xh, axis=0, keepdims=True)
        dxh = dy * ga
        d_state = d_hid + r1[rows, :] * (dxh - mean_of(dxh) - xh * mean_of(dxh * xh))
        land = x[rows, 192:256][:, 0:1]
        land_sum = land_sum + jnp.sum(d_state * land, axis=0, keepdims=True)
        incoming = d_state.astype(BF16).astype(F32)
        dstate[:, 0:CH] = incoming
        for half in range(2):
            piece = dstate[HALF * half : HALF * half + HALF, :]
            for tile in range(2):
                at = SUMS + QUARTER * (s // 2) + BLOCK * (2 * half + tile)
                block = jnp.concatenate([piece[:, 128 * tile : 128 * tile + 128], zero_rows], axis=0)
                msg[s % 2, at : at + BLOCK, :] = block.astype(BF16)

    factor = float(STEPS * 192 * 96) ** (-0.5)

    def put(tile, value):
        for j in range(value.shape[1] // 128):
            start = (tile + j) * CH
            done = 0
            while done < CH:
                part, row = divmod(start + done, SUMS)
                n = min(CH - done, SUMS - row)
                msg[part, row : row + n, :] = value[done : done + n, 128 * j : 128 * j + 128]
                done += n

    cot_all = cot_s[...].astype(BF16)
    put(12, (tn(cot_all, act[...]) * factor).astype(BF16))
    put(6, (tn(nm_s[...], dpre_s[...].astype(BF16)) * factor).astype(BF16))
    g_qkv = tn(normed_s[...].astype(BF16), dqkv_s[...].astype(BF16)) * factor
    g_out = tn(mixed_s[...].astype(BF16), dproj_s[...].astype(BF16)) * factor
    put(0, jnp.concatenate([g_qkv, g_out], axis=1).astype(BF16))
    small[...] = jnp.zeros_like(small)
    for i, total in enumerate((land_sum, gain_a_sum, gain_m_sum)):
        total = total * factor
        small[2 * i : 2 * i + 1, :] = total[:, 0:128]
        small[2 * i + 1 : 2 * i + 2, 0:64] = total[:, 128:192]
    msg[1, 18 * CH - SUMS : SUMS, :] = small[...].astype(BF16)
    send_out[...] = msg[1 - core]
    keep_out[...] = msg[core]


SMALL_ROWS = 2 * SUMS - 18 * CH


def pair_kernel(kept, arrived, chunks, x_send, x_keep):
    core = lax.axis_index("core")
    here = lax.axis_index("xh")
    for g in range(GROUP):
        at = UNIT * g
        total = kept[at : at + UNIT, :].astype(F32) + arrived[at : at + UNIT, :].astype(F32)
        chunks[g] = total.astype(BF16)
    own = pl.ds(pl.multiple_of(SUMS + QUARTER * here, 64), QUARTER)
    other = pl.ds(pl.multiple_of(SUMS + QUARTER * (1 - here), 64), QUARTER)
    x_send[core] = kept[other, :]
    x_send[1 - core] = arrived[other, :]
    x_keep[core] = kept[own, :]
    x_keep[1 - core] = arrived[own, :]


def group_kernel(terms, kept, arrived, total_out, near, to_lon, to_lat, to_both):
    here = lax.axis_index("xh")
    total = terms[0].astype(F32)
    for g in range(1, GROUP):
        total = total + terms[g].astype(F32)
    total = total.astype(BF16)
    for g in range(8):
        total_out[g] = total
    half = QUARTER // 2
    for c in range(2):
        near[2 * here + c] = kept[c, 0:half, :]
        near[2 * (1 - here) + c] = arrived[c, 0:half, :]
        to_lon[2 * here + c] = kept[c, half:QUARTER, :]
        to_lon[2 * (1 - here) + c] = arrived[c, half:QUARTER, :]
    to_lat[...] = near[3]
    to_both[...] = to_lon[3]


def column_kernel(terms, total_out):
    total = terms[0].astype(F32)
    for g in range(1, 8):
        total = total + terms[g].astype(F32)
    total = total.astype(BF16)
    for g in range(GROUP):
        total_out[g] = total


def unpack_kernel(
    own, other, near, from_lon, from_lat, from_both,
    state_out, g_qkv, g_out, g_up, g_down, g_land, g_ga, g_gm, msg,
):
    core = lax.axis_index("core")
    for g in range(GROUP):
        msg[core, UNIT * g : UNIT * g + UNIT, :] = own[g]
        msg[1 - core, UNIT * g : UNIT * g + UNIT, :] = other[g]

    def rows_of(start, count):
        pieces = []
        done = 0
        while done < count:
            part, row = divmod(start + done, SUMS)
            n = min(count - done, SUMS - row)
            pieces.append(msg[part, row : row + n, :].astype(F32))
            done += n
        return pieces[0] if len(pieces) == 1 else jnp.concatenate(pieces, axis=0)

    for j in range(4):
        g_qkv[:, 128 * j : 128 * j + 128] = rows_of(j * CH, CH)
    mid = rows_of(4 * CH, CH)
    tail = rows_of(5 * CH, CH)
    g_qkv[:, 512:576] = mid[:, 0:64]
    g_out[...] = jnp.concatenate([mid[:, 64:128], tail], axis=1)
    for j in range(6):
        g_up[:, 128 * j : 128 * j + 128] = rows_of((6 + j) * CH, CH)
        g_down[:, 128 * j : 128 * j + 128] = rows_of((12 + j) * CH, CH)
    little = rows_of(18 * CH, 16)
    for i, out in enumerate((g_land, g_ga, g_gm)):
        out[...] = jnp.concatenate(
            [little[2 * i : 2 * i + 1, :], little[2 * i + 1 : 2 * i + 2, 0:64]], axis=1
        )
    for first, wide, edge in ((6, near, from_lat), (0, from_lon, from_both)):
        for tile, lanes in ((0, slice(0, 128)), (1, slice(128, 192))):
            n = lanes.stop - lanes.start
            at = slice(BLOCK * tile, BLOCK * tile + BLOCK)
            before = edge[at, :].astype(F32)
            for c in range(6):
                state_out[first + c, 0:3, lanes] = before[6 * c + 3 : 6 * c + 6, 0:n]
            for k in range(4):
                block = wide[k, at, :].astype(F32)
                tall = 6 if k < 3 else 3
                for c in range(6):
                    state_out[first + c, 6 * k + 3 : 6 * k + 3 + tall, lanes] = block[
                        6 * c : 6 * c + tall, 0:n
                    ]


def hop(value, rows, cols):
    pairs = []
    for k in range(4):
        for a in range(8):
            for b in range(8):
                to = (k * 8 + (a + rows) % 8) * 8 + (b + cols) % 8
                pairs.append(((k * 8 + a) * 8 + b, to))
    return lax.ppermute(value, AXES, pairs)


def swap(value, axis):
    return lax.ppermute(value, axis, [(0, 1), (1, 0)])


def exchange(value, axis):
    return lax.all_to_all(value, axis, 0, 0, tiled=True)


def call(kernel, name, outs, scratch=(), mib=8):
    return pl.pallas_call(
        kernel,
        out_shape=tuple(jax.ShapeDtypeStruct(dims, kind) for dims, kind in outs),
        scratch_shapes=[pltpu.VMEM(dims, kind) for dims, kind in scratch],
        compiler_params=pltpu.CompilerParams(vmem_limit_bytes=mib * MIB),
        name=name,
    )


def local(
    states, loss_grads, land_sea, land_embed, gain_attn, gain_mlp, w_qkv, w_out, w_up, w_down
):
    kept, to_lon, to_lat, to_both = call(
        pack_kernel,
        "pack_cells",
        [((6, ROWS, MSG), BF16)] * 2 + [((6, EDGE, MSG), BF16)] * 2,
    )(states[0, 0].transpose(1, 0, 2), loss_grads[0, 0].transpose(1, 0, 2), land_sea.T)
    from_lon = hop(to_lon, 0, -1)
    from_lat = hop(to_lat, -1, 0)
    from_both = hop(to_both, -1, -1)
    (packed,) = call(
        window_kernel, "cut_windows", [((4, WIN, MSG), BF16)], [((4, WIN, MSG), F32)]
    )(kept, from_lon, from_lat, from_both)
    cells = exchange(packed, ("xh", "core"))
    send, keep = call(
        main_kernel,
        "window_steps",
        [((SENT, 128), BF16)] * 2,
        [
            ((TOK, MSG), F32),
            ((TOK, 3 * CH), F32),
            ((STEPS, HEADS * WIN, WIN), F32),
            ((STEPS, HEADS * WIN, CH), BF16),
            ((TOK, CH), F32),
            ((TOK, CH), F32),
            ((TOK, 1), F32),
            ((TOK, CH), F32),
            ((TOK, 1), F32),
            ((TOK, MLP), F32),
            ((TOK, MLP), BF16),
            ((TOK, CH), F32),
            ((TOK, CH), F32),
            ((TOK, CH), BF16),
            ((TOK, CH), F32),
            ((TOK, MLP), F32),
            ((TOK, CH), F32),
            ((TOK, 3 * CH), F32),
            ((WIN, 256), F32),
            ((SMALL_ROWS, 128), F32),
            ((2, SENT, 128), BF16),
        ],
        mib=24,
    )(
        cells, land_embed[None], gain_attn[None], gain_mlp[None], w_qkv, w_out, w_up, w_down.T
    )

    chunks, x_send, x_keep = call(
        pair_kernel,
        "sum_cores",
        [((GROUP, UNIT, 128), BF16)] + [((2, QUARTER, 128), BF16)] * 2,
    )(keep, swap(send, "core"))
    x_arrived = swap(x_send, "xh")
    terms = exchange(chunks, ("xh", "lon"))
    partial, near, to_lon, to_lat, to_both = call(
        group_kernel,
        "sum_group",
        [((8, UNIT, 128), BF16)]
        + [((4, QUARTER // 2, 128), BF16)] * 2
        + [((QUARTER // 2, 128), BF16)] * 2,
    )(terms, x_keep, x_arrived)
    from_lon = hop(to_lon, 0, 1)
    from_lat = hop(to_lat, 1, 0)
    from_both = hop(to_both, 1, 1)
    terms, from_lon, from_lat, from_both = lax.optimization_barrier(
        (exchange(partial, "lat"), from_lon, from_lat, from_both)
    )
    (total,) = call(column_kernel, "sum_column", [((GROUP, UNIT, 128), BF16)])(terms)
    own = exchange(total, ("xh", "lon"))
    outs = call(
        unpack_kernel,
        "unpack_sums",
        [
            ((WIN_LON, ROWS, CH), F32),
            ((CH, 3 * CH), F32),
            ((CH, CH), F32),
            ((CH, MLP), F32),
            ((CH, MLP), F32),
            ((1, CH), F32),
            ((1, CH), F32),
            ((1, CH), F32),
        ],
        [((2, SUMS, 128), BF16)],
        mib=16,
    )(own, swap(own, "core"), near, from_lon, from_lat, from_both)
    return (
        outs[0].transpose(1, 0, 2)[None, None],
        outs[1], outs[2], outs[3], outs[4].T, outs[5][0], outs[6][0], outs[7][0],
    )


def solution(mesh):
    halves = Mesh(mesh.devices.reshape(2, 2, *mesh.devices.shape[1:]), AXES)
    cell = P(("xh", "core"), None, "lat", "lon", None)
    return jax.shard_map(
        local,
        mesh=halves,
        in_specs=(cell, cell, P("lat", "lon"), P(), P(), P(), P(), P(), P(), P()),
        out_specs=(cell, P(), P(), P(), P(), P(), P(), P()),
        check_vma=False,
    )
```

```python
import jax
import jax.numpy as jnp
from jax import lax
from jax.experimental import pallas as pl
from jax.experimental.pallas import tpu as pltpu
from jax.sharding import Mesh
from jax.sharding import PartitionSpec as P

CH = 192
HEADS = 6
HEAD_DIM = 32
MLP = 768
ROWS = 24
WIN_LAT = 6
WIN_LON = 12
WIN = WIN_LAT * WIN_LON
HALF = WIN // 2
STEPS = 4
TOK = STEPS * WIN
MSG = 512
GROUP = 16
UNIT = 112
SUMS = GROUP * UNIT
BLOCK = 48
QUARTER = 4 * BLOCK
SENT = SUMS + 2 * QUARTER
SCALE = HEAD_DIM ** (-0.5)
EPS = 1e-05
F32 = jnp.float32
BF16 = jnp.bfloat16
AXES = ("xh", "core", "lat", "lon")
MIB = 1024 * 1024


def nn(a, b):
    return lax.dot_general(a, b, (((1,), (0,)), ((), ())), preferred_element_type=F32)


def nt(a, b):
    return lax.dot_general(a, b, (((1,), (1,)), ((), ())), preferred_element_type=F32)


def tn(a, b):
    return lax.dot_general(a, b, (((0,), (0,)), ((), ())), preferred_element_type=F32)


def mean_of(v):
    return jnp.sum(v, axis=-1, keepdims=True) * (1.0 / CH)


def pack_kernel(
    states_in, loss_in, land_in, embed_in, gain_a_in, gain_m_in,
    keep_out, send_out, edge_out, vectors_out,
    states, loss, land, vectors, cells, edges, sems,
):
    pairs = (
        (states_in, states), (loss_in, loss), (land_in, land),
        (embed_in, vectors.at[0:1]), (gain_a_in, vectors.at[1:2]), (gain_m_in, vectors.at[2:3]),
    )
    copies = [
        pltpu.make_async_copy(source, target, sems.at[i])
        for i, (source, target) in enumerate(pairs)
    ]
    for copy in copies:
        copy.start()
    for copy in copies:
        copy.wait()
    core = lax.axis_index("core")
    mask = land[...].astype(F32)
    nothing = jnp.zeros((3, MSG), F32)
    for c in range(WIN_LON):
        column = jnp.broadcast_to(mask[c : c + 1, :], (64, ROWS)).T
        cell = jnp.concatenate(
            [states[c].astype(F32), column, loss[c].astype(F32), column], axis=1
        )
        part, at = (1, 6 * c) if c < 6 else (0, 6 * (c - 6))
        for k in range(3):
            cells[k % 2, k // 2, part, at : at + 6, :] = cell[6 * k + 3 : 6 * k + 9]
        cells[1, 1, part, at : at + 3, :] = cell[21:24]
        cells[1, 1, part, at + 3 : at + 6, :] = nothing
        edges[part, at // 2 : at // 2 + 3, :] = cell[0:3]
    keep_out[...] = cells[core].astype(BF16)
    send_out[...] = cells[1 - core].astype(BF16)
    edge_out[...] = edges[...].astype(BF16)
    vectors_out[...] = vectors[...]


def sort_kernel(kept, arrived, edge0, edge1, near_own, near_x, lon_own, lon_x, cells):
    core = lax.axis_index("core")
    here = lax.axis_index("xh")
    cells[core] = kept[...].astype(F32)
    cells[1 - core] = arrived[...].astype(F32)

    @pl.when(core == 1)
    def _():
        for step, edge in enumerate((edge0, edge1)):
            for part in range(2):
                rows = edge[part].astype(F32)
                for c in range(6):
                    cells[step, 1, part, 6 * c + 3 : 6 * c + 6, :] = rows[3 * c : 3 * c + 3]

    for step in range(2):
        near_own[step] = cells[step, here, 0].astype(BF16)
        near_x[step] = cells[step, 1 - here, 0].astype(BF16)
        lon_own[step] = cells[step, here, 1].astype(BF16)
        lon_x[step] = cells[step, 1 - here, 1].astype(BF16)


def main_kernel(
    near_own, near_x, lon_own, lon_x, vectors, wqkv, wout, wup, wdown_t,
    send_out, keep_out,
    x, qkv, probs, qm_all, emb, xh1, r1, hid_xh, r2, gp, act, normed_s, mixed_s, nm_s,
    cot_s, dpre_s, dproj_s, dqkv_s, dstate, small, msg,
):
    core = lax.axis_index("core")
    here = lax.axis_index("xh")
    last = jnp.logical_and(lax.axis_index("lat") == 7, jnp.logical_and(here == 1, core == 1))
    closed = jnp.where(last, 0.0, 1.0).astype(F32)
    for step in range(2):
        x[2 * here + step, 0:HALF, :] = near_own[step].astype(F32)
        x[2 * here + step, HALF:WIN, :] = lon_own[step].astype(F32)
        x[2 * (1 - here) + step, 0:HALF, :] = near_x[step].astype(F32)
        x[2 * (1 - here) + step, HALF:WIN, :] = lon_x[step].astype(F32)
    le = vectors[0:1, :]
    ga = vectors[1:2, :]
    gm = vectors[2:3, :]
    col_head = lax.broadcasted_iota(jnp.int32, (1, CH), 1) // HEAD_DIM
    masks = [(col_head == h).astype(F32) for h in range(HEADS)]
    row_half = lax.rem(lax.broadcasted_iota(jnp.int32, (WIN, WIN), 0), WIN_LAT) // 3
    key_half = lax.rem(lax.broadcasted_iota(jnp.int32, (WIN, WIN), 1), WIN_LAT) // 3
    allow1 = jnp.where(row_half == key_half, 1.0, closed).astype(F32)
    allow = jnp.concatenate([allow1] * HEADS, axis=0)

    def spread(v):
        return jnp.concatenate([v * m for m in masks], axis=0).astype(BF16)

    def gathered(v):
        total = v[0:WIN] * masks[0]
        for h in range(1, HEADS):
            total = total + v[WIN * h : WIN * h + WIN] * masks[h]
        return total

    for s in range(STEPS):
        rows = slice(WIN * s, WIN * s + WIN)
        land = x[s, :, 192:256][:, 0:1]
        e = x[s, :, 0:CH] + land * le
        emb[rows, :] = e
        off = e - mean_of(e)
        r = lax.rsqrt(mean_of(off * off) + EPS)
        xh = off * r
        xh1[rows, :] = xh
        r1[rows, :] = r
        normed_s[rows, :] = xh * ga
    normed = normed_s[...].astype(BF16)
    qkv[...] = nn(normed, wqkv[...]).astype(BF16).astype(F32)
    for s in range(STEPS):
        rows = slice(WIN * s, WIN * s + WIN)
        qm = spread(qkv[rows, 0:CH])
        qm_all[s] = qm
        keys = qkv[rows, CH : 2 * CH].astype(BF16)
        values = qkv[rows, 2 * CH : 3 * CH].astype(BF16)
        weights = jnp.exp(nt(qm, keys) * SCALE) * allow
        p = weights / jnp.sum(weights, axis=-1, keepdims=True)
        probs[s] = p
        mixed_s[rows, :] = gathered(nn(p.astype(BF16), values))
    mixed = mixed_s[...].astype(BF16)
    projected = nn(mixed, wout[...]).astype(BF16).astype(F32)
    hid = emb[...] + projected
    off = hid - mean_of(hid)
    r = lax.rsqrt(mean_of(off * off) + EPS)
    xh = off * r
    hid_xh[...] = xh
    r2[...] = r
    nm_s[...] = (xh * gm).astype(BF16)
    for j in range(MLP // 256):
        cols = slice(256 * j, 256 * j + 256)
        pre = nn(nm_s[...], wup[:, cols])
        cdf = 0.5 * (1.0 + lax.erf(pre * (0.5 ** 0.5)))
        pdf = jnp.exp(pre * pre * -0.5) * 0.3989422804014327
        act[:, cols] = (pre * cdf).astype(BF16)
        gp[:, cols] = cdf + pre * pdf

    gain_m_sum = jnp.zeros((1, CH), F32)
    gain_a_sum = jnp.zeros((1, CH), F32)
    land_sum = jnp.zeros((1, CH), F32)
    incoming = None
    wq = wqkv[:, 0:CH]
    wk = wqkv[:, CH : 2 * CH]
    wv = wqkv[:, 2 * CH : 3 * CH]
    zero_rows = jnp.zeros((BLOCK - HALF, 128), F32)
    dstate[...] = jnp.zeros_like(dstate)
    for s in range(STEPS - 1, -1, -1):
        rows = slice(WIN * s, WIN * s + WIN)
        cot = x[s, :, 256:448]
        if incoming is not None:
            cot = cot + incoming
        cotb = cot.astype(BF16)
        cot_s[rows, :] = cotb.astype(F32)
        d_pre = gp[rows, :] * nn(cotb, wdown_t[...])
        dpre_b = d_pre.astype(BF16)
        dpre_s[rows, :] = dpre_b.astype(F32)
        dy = nt(dpre_b, wup[...])
        xh = hid_xh[rows, :]
        gain_m_sum = gain_m_sum + jnp.sum(dy * xh, axis=0, keepdims=True)
        dxh = dy * gm
        d_hid = cot + r2[rows, :] * (dxh - mean_of(dxh) - xh * mean_of(dxh * xh))
        dproj = d_hid.astype(BF16)
        dproj_s[rows, :] = dproj.astype(F32)
        d_mixed = nt(dproj, wout[...]).astype(BF16).astype(F32)
        dm = spread(d_mixed)
        keys = qkv[rows, CH : 2 * CH].astype(BF16)
        values = qkv[rows, 2 * CH : 3 * CH].astype(BF16)
        p = probs[s]
        dp = nt(dm, values)
        dv = tn(p.astype(BF16), dm).astype(BF16)
        ds = (p * (dp - jnp.sum(p * dp, axis=-1, keepdims=True)) * SCALE).astype(BF16)
        dq = gathered(nn(ds, keys)).astype(BF16)
        dk = tn(ds, qm_all[s]).astype(BF16)
        dqkv_s[rows, 0:CH] = dq.astype(F32)
        dqkv_s[rows, CH : 2 * CH] = dk.astype(F32)
        dqkv_s[rows, 2 * CH : 3 * CH] = dv.astype(F32)
        d_rolled = nt(dq, wq) + nt(dk, wk) + nt(dv, wv)
        dy = d_rolled.astype(BF16).astype(F32)
        xh = xh1[rows, :]
        gain_a_sum = gain_a_sum + jnp.sum(dy * xh, axis=0, keepdims=True)
        dxh = dy * ga
        d_state = d_hid + r1[rows, :] * (dxh - mean_of(dxh) - xh * mean_of(dxh * xh))
        land = x[s, :, 192:256][:, 0:1]
        land_sum = land_sum + jnp.sum(d_state * land, axis=0, keepdims=True)
        incoming = d_state.astype(BF16).astype(F32)
        dstate[:, 0:CH] = incoming
        for half in range(2):
            piece = dstate[HALF * half : HALF * half + HALF, :]
            for tile in range(2):
                at = SUMS + QUARTER * (s // 2) + BLOCK * (2 * half + tile)
                block = jnp.concatenate([piece[:, 128 * tile : 128 * tile + 128], zero_rows], axis=0)
                msg[s % 2, at : at + BLOCK, :] = block.astype(BF16)

    factor = float(STEPS * 192 * 96) ** (-0.5)

    def put(tile, value):
        for j in range(value.shape[1] // 128):
            start = (tile + j) * CH
            done = 0
            while done < CH:
                part, row = divmod(start + done, SUMS)
                n = min(CH - done, SUMS - row)
                msg[part, row : row + n, :] = value[done : done + n, 128 * j : 128 * j + 128]
                done += n

    cot_all = cot_s[...].astype(BF16)
    put(12, (tn(cot_all, act[...]) * factor).astype(BF16))
    put(6, (tn(nm_s[...], dpre_s[...].astype(BF16)) * factor).astype(BF16))
    g_qkv = tn(normed_s[...].astype(BF16), dqkv_s[...].astype(BF16)) * factor
    g_out = tn(mixed_s[...].astype(BF16), dproj_s[...].astype(BF16)) * factor
    put(0, jnp.concatenate([g_qkv, g_out], axis=1).astype(BF16))
    small[...] = jnp.zeros_like(small)
    for i, total in enumerate((land_sum, gain_a_sum, gain_m_sum)):
        total = total * factor
        small[2 * i : 2 * i + 1, :] = total[:, 0:128]
        small[2 * i + 1 : 2 * i + 2, 0:64] = total[:, 128:192]
    msg[1, 18 * CH - SUMS : SUMS, :] = small[...].astype(BF16)
    send_out[...] = msg[1 - core]
    keep_out[...] = msg[core]


SMALL_ROWS = 2 * SUMS - 18 * CH


def pair_kernel(kept, arrived, chunks, x_send, x_keep):
    core = lax.axis_index("core")
    here = lax.axis_index("xh")
    for g in range(GROUP):
        at = UNIT * g
        total = kept[at : at + UNIT, :].astype(F32) + arrived[at : at + UNIT, :].astype(F32)
        chunks[g] = total.astype(BF16)
    own = pl.ds(pl.multiple_of(SUMS + QUARTER * here, 64), QUARTER)
    other = pl.ds(pl.multiple_of(SUMS + QUARTER * (1 - here), 64), QUARTER)
    x_send[core] = kept[other, :]
    x_send[1 - core] = arrived[other, :]
    x_keep[core] = kept[own, :]
    x_keep[1 - core] = arrived[own, :]


def group_kernel(terms, total_out):
    total = terms[0].astype(F32)
    for g in range(1, GROUP):
        total = total + terms[g].astype(F32)
    total = total.astype(BF16)
    for g in range(8):
        total_out[g] = total


def column_kernel(terms, kept, arrived, total_out, near, to_lon, to_lat, to_both):
    here = lax.axis_index("xh")
    half = QUARTER // 2
    for c in range(2):
        near[2 * here + c] = kept[c, 0:half, :]
        near[2 * (1 - here) + c] = arrived[c, 0:half, :]
        to_lon[2 * here + c] = kept[c, half:QUARTER, :]
        to_lon[2 * (1 - here) + c] = arrived[c, half:QUARTER, :]
    to_lat[...] = near[3]
    to_both[...] = to_lon[3]
    total = terms[0].astype(F32)
    for g in range(1, 8):
        total = total + terms[g].astype(F32)
    total = total.astype(BF16)
    for g in range(GROUP):
        total_out[g] = total


def unpack_kernel(
    own, other, near, from_lon, from_lat, from_both,
    state_out, g_qkv, g_out, g_up, g_down, g_land, g_ga, g_gm, msg,
):
    core = lax.axis_index("core")
    for g in range(GROUP):
        msg[core, UNIT * g : UNIT * g + UNIT, :] = own[g]
        msg[1 - core, UNIT * g : UNIT * g + UNIT, :] = other[g]

    def rows_of(start, count):
        pieces = []
        done = 0
        while done < count:
            part, row = divmod(start + done, SUMS)
            n = min(count - done, SUMS - row)
            pieces.append(msg[part, row : row + n, :].astype(F32))
            done += n
        return pieces[0] if len(pieces) == 1 else jnp.concatenate(pieces, axis=0)

    for j in range(4):
        g_qkv[:, 128 * j : 128 * j + 128] = rows_of(j * CH, CH)
    mid = rows_of(4 * CH, CH)
    tail = rows_of(5 * CH, CH)
    g_qkv[:, 512:576] = mid[:, 0:64]
    g_out[...] = jnp.concatenate([mid[:, 64:128], tail], axis=1)
    for j in range(6):
        g_up[:, 128 * j : 128 * j + 128] = rows_of((6 + j) * CH, CH)
        g_down[:, 128 * j : 128 * j + 128] = rows_of((12 + j) * CH, CH)
    little = rows_of(18 * CH, 16)
    for i, out in enumerate((g_land, g_ga, g_gm)):
        out[...] = jnp.concatenate(
            [little[2 * i : 2 * i + 1, :], little[2 * i + 1 : 2 * i + 2, 0:64]], axis=1
        )
    for first, wide, edge in ((6, near, from_lat), (0, from_lon, from_both)):
        for tile, lanes in ((0, slice(0, 128)), (1, slice(128, 192))):
            n = lanes.stop - lanes.start
            at = slice(BLOCK * tile, BLOCK * tile + BLOCK)
            before = edge[at, :].astype(F32)
            for c in range(6):
                state_out[first + c, 0:3, lanes] = before[6 * c + 3 : 6 * c + 6, 0:n]
            for k in range(4):
                block = wide[k, at, :].astype(F32)
                tall = 6 if k < 3 else 3
                for c in range(6):
                    state_out[first + c, 6 * k + 3 : 6 * k + 3 + tall, lanes] = block[
                        6 * c : 6 * c + tall, 0:n
                    ]


def hop(value, rows, cols, xh=0, cores=((0, 0), (1, 1))):
    pairs = []
    for h in range(2):
        for source, target in cores:
            for a in range(8):
                for b in range(8):
                    k = 2 * ((h + xh) % 2) + target
                    to = (k * 8 + (a + rows) % 8) * 8 + (b + cols) % 8
                    pairs.append((((2 * h + source) * 8 + a) * 8 + b, to))
    return lax.ppermute(value, AXES, pairs)


def swap(value, axis):
    return lax.ppermute(value, axis, [(0, 1), (1, 0)])


def exchange(value, axis):
    return lax.all_to_all(value, axis, 0, 0, tiled=True)


def call(kernel, name, outs, scratch=(), mib=8, from_hbm=0):
    specs = {}
    if from_hbm:
        specs["in_specs"] = [pl.BlockSpec(memory_space=pltpu.HBM)] * from_hbm
    return pl.pallas_call(
        kernel,
        out_shape=tuple(jax.ShapeDtypeStruct(dims, kind) for dims, kind in outs),
        scratch_shapes=[pltpu.VMEM(dims, kind) if kind else dims for dims, kind in scratch],
        compiler_params=pltpu.CompilerParams(vmem_limit_bytes=mib * MIB),
        name=name,
        **specs,
    )


def local(
    states, loss_grads, land_sea, land_embed, gain_attn, gain_mlp, w_qkv, w_out, w_up, w_down
):
    keep, send, edge, vectors = call(
        pack_kernel,
        "pack_cells",
        [((2, 2, HALF, MSG), BF16)] * 2 + [((2, HALF // 2, MSG), BF16), ((8, CH), F32)],
        [
            ((WIN_LON, ROWS, CH), BF16),
            ((WIN_LON, ROWS, CH), BF16),
            ((WIN_LON, ROWS), jnp.int32),
            ((8, CH), F32),
            ((2, 2, 2, HALF, MSG), F32),
            ((2, HALF // 2, MSG), F32),
            (pltpu.SemaphoreType.DMA((6,)), None),
        ],
        from_hbm=6,
    )(
        states[0, 0].transpose(1, 0, 2), loss_grads[0, 0].transpose(1, 0, 2), land_sea.T,
        land_embed[None], gain_attn[None], gain_mlp[None],
    )
    near_own, near_x, lon_own, lon_x = call(
        sort_kernel,
        "sort_windows",
        [((2, HALF, MSG), BF16)] * 4,
        [((2, 2, 2, HALF, MSG), F32)],
    )(
        keep, swap(send, "core"),
        hop(edge, -1, 0, cores=((0, 1),)), hop(edge, -1, 0, cores=((1, 1),)),
    )
    near_x = hop(near_x, 0, 0, 1)
    lon_own = hop(lon_own, 0, -1)
    lon_x = hop(lon_x, 0, -1, 1)
    send, keep = call(
        main_kernel,
        "window_steps",
        [((SENT, 128), BF16)] * 2,
        [
            ((STEPS, WIN, MSG), F32),
            ((TOK, 3 * CH), F32),
            ((STEPS, HEADS * WIN, WIN), F32),
            ((STEPS, HEADS * WIN, CH), BF16),
            ((TOK, CH), F32),
            ((TOK, CH), F32),
            ((TOK, 1), F32),
            ((TOK, CH), F32),
            ((TOK, 1), F32),
            ((TOK, MLP), F32),
            ((TOK, MLP), BF16),
            ((TOK, CH), F32),
            ((TOK, CH), F32),
            ((TOK, CH), BF16),
            ((TOK, CH), F32),
            ((TOK, MLP), F32),
            ((TOK, CH), F32),
            ((TOK, 3 * CH), F32),
            ((WIN, 256), F32),
            ((SMALL_ROWS, 128), F32),
            ((2, SENT, 128), BF16),
        ],
        mib=24,
    )(near_own, near_x, lon_own, lon_x, vectors, w_qkv, w_out, w_up, w_down.T)

    chunks, x_send, x_keep = call(
        pair_kernel,
        "sum_cores",
        [((GROUP, UNIT, 128), BF16)] + [((2, QUARTER, 128), BF16)] * 2,
    )(keep, swap(send, "core"))
    x_arrived = swap(x_send, "xh")
    (partial,) = call(group_kernel, "sum_group", [((8, UNIT, 128), BF16)])(
        exchange(chunks, ("xh", "lon"))
    )
    total, near, to_lon, to_lat, to_both = call(
        column_kernel,
        "sum_column",
        [((GROUP, UNIT, 128), BF16)]
        + [((4, QUARTER // 2, 128), BF16)] * 2
        + [((QUARTER // 2, 128), BF16)] * 2,
    )(exchange(partial, "lat"), x_keep, x_arrived)
    from_lon = hop(to_lon, 0, 1)
    from_lat = hop(to_lat, 1, 0)
    from_both = hop(to_both, 1, 1)
    own, from_lon, from_lat, from_both = lax.optimization_barrier(
        (exchange(total, ("xh", "lon")), from_lon, from_lat, from_both)
    )
    outs = call(
        unpack_kernel,
        "unpack_sums",
        [
            ((WIN_LON, ROWS, CH), F32),
            ((CH, 3 * CH), F32),
            ((CH, CH), F32),
            ((CH, MLP), F32),
            ((CH, MLP), F32),
            ((1, CH), F32),
            ((1, CH), F32),
            ((1, CH), F32),
        ],
        [((2, SUMS, 128), BF16)],
        mib=16,
    )(own, swap(own, "core"), near, from_lon, from_lat, from_both)
    return (
        outs[0].transpose(1, 0, 2)[None, None],
        outs[1], outs[2], outs[3], outs[4].T, outs[5][0], outs[6][0], outs[7][0],
    )


def solution(mesh):
    halves = Mesh(mesh.devices.reshape(2, 2, *mesh.devices.shape[1:]), AXES)
    cell = P(("xh", "core"), None, "lat", "lon", None)
    return jax.shard_map(
        local,
        mesh=halves,
        in_specs=(cell, cell, P("lat", "lon"), P(), P(), P(), P(), P(), P(), P()),
        out_specs=(cell, P(), P(), P(), P(), P(), P(), P()),
        check_vma=False,
    )
```

```python
import jax
import jax.numpy as jnp
from jax import lax
from jax.experimental import pallas as pl
from jax.experimental.pallas import tpu as pltpu
from jax.sharding import Mesh
from jax.sharding import PartitionSpec as P

CH = 192
HEADS = 6
HEAD_DIM = 32
MLP = 768
ROWS = 24
WIN_LAT = 6
WIN_LON = 12
WIN = WIN_LAT * WIN_LON
HALF = WIN // 2
STEPS = 4
TOK = STEPS * WIN
MSG = 512
GROUP = 16
UNIT = 112
SUMS = GROUP * UNIT
BLOCK = 48
QUARTER = 4 * BLOCK
SENT = SUMS + 2 * QUARTER
SCALE = HEAD_DIM ** (-0.5)
EPS = 1e-05
F32 = jnp.float32
BF16 = jnp.bfloat16
AXES = ("xh", "core", "lat", "lon")
MIB = 1024 * 1024


def nn(a, b):
    return lax.dot_general(a, b, (((1,), (0,)), ((), ())), preferred_element_type=F32)


def nt(a, b):
    return lax.dot_general(a, b, (((1,), (1,)), ((), ())), preferred_element_type=F32)


def tn(a, b):
    return lax.dot_general(a, b, (((0,), (0,)), ((), ())), preferred_element_type=F32)


def mean_of(v):
    return jnp.sum(v, axis=-1, keepdims=True) * (1.0 / CH)


def pack_kernel(
    states_in, loss_in, land_in, embed_in, gain_a_in, gain_m_in, wqkv_in,
    keep_out, send_out, edge_out, vectors_out, wqkv_out,
    states, loss, land, vectors, cells, edges, sems,
):
    pairs = (
        (states_in, states), (loss_in, loss), (land_in, land),
        (embed_in, vectors.at[0:1]), (gain_a_in, vectors.at[1:2]), (gain_m_in, vectors.at[2:3]),
    )
    copies = [
        pltpu.make_async_copy(source, target, sems.at[i])
        for i, (source, target) in enumerate(pairs)
    ]
    weights = pltpu.make_async_copy(wqkv_in, wqkv_out, sems.at[6])
    for copy in copies:
        copy.start()
    weights.start()
    for copy in copies:
        copy.wait()
    core = lax.axis_index("core")
    mask = land[...].astype(F32)
    nothing = jnp.zeros((3, MSG), F32)
    for c in range(WIN_LON):
        column = jnp.broadcast_to(mask[c : c + 1, :], (64, ROWS)).T
        cell = jnp.concatenate(
            [states[c].astype(F32), column, loss[c].astype(F32), column], axis=1
        )
        part, at = (1, 6 * c) if c < 6 else (0, 6 * (c - 6))
        for k in range(3):
            cells[k % 2, k // 2, part, at : at + 6, :] = cell[6 * k + 3 : 6 * k + 9]
        cells[1, 1, part, at : at + 3, :] = cell[21:24]
        cells[1, 1, part, at + 3 : at + 6, :] = nothing
        edges[part, at // 2 : at // 2 + 3, :] = cell[0:3]
    keep_out[...] = cells[core].astype(BF16)
    send_out[...] = cells[1 - core].astype(BF16)
    edge_out[...] = edges[...].astype(BF16)
    vectors_out[...] = vectors[...]
    weights.wait()


def sort_kernel(kept, arrived, edge0, edge1, near_own, near_x, lon_own, lon_x, cells):
    core = lax.axis_index("core")
    here = lax.axis_index("xh")
    cells[core] = kept[...].astype(F32)
    cells[1 - core] = arrived[...].astype(F32)

    @pl.when(core == 1)
    def _():
        for step, edge in enumerate((edge0, edge1)):
            for part in range(2):
                rows = edge[part].astype(F32)
                for c in range(6):
                    cells[step, 1, part, 6 * c + 3 : 6 * c + 6, :] = rows[3 * c : 3 * c + 3]

    for step in range(2):
        near_own[step] = cells[step, here, 0].astype(BF16)
        near_x[step] = cells[step, 1 - here, 0].astype(BF16)
        lon_own[step] = cells[step, here, 1].astype(BF16)
        lon_x[step] = cells[step, 1 - here, 1].astype(BF16)


def main_kernel(
    near_own, near_x, lon_own, lon_x, vectors, wqkv, wout, wup, wdown_t,
    send_out, keep_out,
    x, qkv, probs, qm_all, emb, xh1, r1, hid_xh, r2, gp, act, normed_s, mixed_s, nm_s,
    cot_s, dpre_s, dproj_s, dqkv_s, dstate, small, msg, sems,
):
    core = lax.axis_index("core")
    here = lax.axis_index("xh")
    last = jnp.logical_and(lax.axis_index("lat") == 7, jnp.logical_and(here == 1, core == 1))
    closed = jnp.where(last, 0.0, 1.0).astype(F32)
    for step in range(2):
        x[2 * here + step, 0:HALF, :] = near_own[step].astype(F32)
        x[2 * here + step, HALF:WIN, :] = lon_own[step].astype(F32)
        x[2 * (1 - here) + step, 0:HALF, :] = near_x[step].astype(F32)
        x[2 * (1 - here) + step, HALF:WIN, :] = lon_x[step].astype(F32)
    le = vectors[0:1, :]
    ga = vectors[1:2, :]
    gm = vectors[2:3, :]
    col_head = lax.broadcasted_iota(jnp.int32, (1, CH), 1) // HEAD_DIM
    masks = [(col_head == h).astype(F32) for h in range(HEADS)]
    row_half = lax.rem(lax.broadcasted_iota(jnp.int32, (WIN, WIN), 0), WIN_LAT) // 3
    key_half = lax.rem(lax.broadcasted_iota(jnp.int32, (WIN, WIN), 1), WIN_LAT) // 3
    allow1 = jnp.where(row_half == key_half, 1.0, closed).astype(F32)
    allow = jnp.concatenate([allow1] * HEADS, axis=1)

    def spread(v):
        return jnp.concatenate([v * m for m in masks], axis=0).astype(BF16)

    def gathered(v):
        total = v[0:WIN] * masks[0]
        for h in range(1, HEADS):
            total = total + v[WIN * h : WIN * h + WIN] * masks[h]
        return total

    for s in range(STEPS):
        rows = slice(WIN * s, WIN * s + WIN)
        land = x[s, :, 192:256][:, 0:1]
        e = x[s, :, 0:CH] + land * le
        emb[rows, :] = e
        off = e - mean_of(e)
        r = lax.rsqrt(mean_of(off * off) + EPS)
        xh = off * r
        xh1[rows, :] = xh
        r1[rows, :] = r
        normed_s[rows, :] = xh * ga
    normed = normed_s[...].astype(BF16)
    qkv[...] = nn(normed, wqkv[...]).astype(BF16).astype(F32)
    for s in range(STEPS):
        rows = slice(WIN * s, WIN * s + WIN)
        qm = spread(qkv[rows, 0:CH])
        qm_all[s] = qm
        keys = qkv[rows, CH : 2 * CH].astype(BF16)
        values = qkv[rows, 2 * CH : 3 * CH].astype(BF16)
        weights = jnp.exp(nt(keys, qm) * SCALE) * allow
        p = weights / jnp.sum(weights, axis=0, keepdims=True)
        probs[s] = p
        mixed_s[rows, :] = gathered(tn(p.astype(BF16), values))
    mixed = mixed_s[...].astype(BF16)
    projected = nn(mixed, wout[...]).astype(BF16).astype(F32)
    hid = emb[...] + projected
    off = hid - mean_of(hid)
    r = lax.rsqrt(mean_of(off * off) + EPS)
    xh = off * r
    hid_xh[...] = xh
    r2[...] = r
    nm_s[...] = (xh * gm).astype(BF16)
    for j in range(MLP // 256):
        cols = slice(256 * j, 256 * j + 256)
        pre = nn(nm_s[...], wup[:, cols])
        cdf = 0.5 * (1.0 + lax.erf(pre * (0.5 ** 0.5)))
        pdf = jnp.exp(pre * pre * -0.5) * 0.3989422804014327
        act[:, cols] = (pre * cdf).astype(BF16)
        gp[:, cols] = cdf + pre * pdf

    gain_m_sum = jnp.zeros((1, CH), F32)
    gain_a_sum = jnp.zeros((1, CH), F32)
    land_sum = jnp.zeros((1, CH), F32)
    incoming = None
    wq = wqkv[:, 0:CH]
    wk = wqkv[:, CH : 2 * CH]
    wv = wqkv[:, 2 * CH : 3 * CH]
    zero_rows = jnp.zeros((BLOCK - HALF, 128), F32)
    dstate[...] = jnp.zeros_like(dstate)
    for s in range(STEPS - 1, -1, -1):
        rows = slice(WIN * s, WIN * s + WIN)
        cot = x[s, :, 256:448]
        if incoming is not None:
            cot = cot + incoming
        cotb = cot.astype(BF16)
        cot_s[rows, :] = cotb.astype(F32)
        d_pre = gp[rows, :] * nn(cotb, wdown_t[...])
        dpre_b = d_pre.astype(BF16)
        dpre_s[rows, :] = dpre_b.astype(F32)
        dy = nt(dpre_b, wup[...])
        xh = hid_xh[rows, :]
        gain_m_sum = gain_m_sum + jnp.sum(dy * xh, axis=0, keepdims=True)
        dxh = dy * gm
        d_hid = cot + r2[rows, :] * (dxh - mean_of(dxh) - xh * mean_of(dxh * xh))
        dproj = d_hid.astype(BF16)
        dproj_s[rows, :] = dproj.astype(F32)
        d_mixed = nt(dproj, wout[...]).astype(BF16).astype(F32)
        dm = spread(d_mixed)
        keys = qkv[rows, CH : 2 * CH].astype(BF16)
        values = qkv[rows, 2 * CH : 3 * CH].astype(BF16)
        p = probs[s]
        dp = nt(values, dm)
        dv = nn(p.astype(BF16), dm).astype(BF16)
        ds = (p * (dp - jnp.sum(p * dp, axis=0, keepdims=True)) * SCALE).astype(BF16)
        dq = gathered(tn(ds, keys)).astype(BF16)
        dk = nn(ds, qm_all[s]).astype(BF16)
        dqkv_s[rows, 0:CH] = dq.astype(F32)
        dqkv_s[rows, CH : 2 * CH] = dk.astype(F32)
        dqkv_s[rows, 2 * CH : 3 * CH] = dv.astype(F32)
        d_rolled = nt(dq, wq) + nt(dk, wk) + nt(dv, wv)
        dy = d_rolled.astype(BF16).astype(F32)
        xh = xh1[rows, :]
        gain_a_sum = gain_a_sum + jnp.sum(dy * xh, axis=0, keepdims=True)
        dxh = dy * ga
        d_state = d_hid + r1[rows, :] * (dxh - mean_of(dxh) - xh * mean_of(dxh * xh))
        land = x[s, :, 192:256][:, 0:1]
        land_sum = land_sum + jnp.sum(d_state * land, axis=0, keepdims=True)
        incoming = d_state.astype(BF16).astype(F32)
        dstate[:, 0:CH] = incoming
        for half in range(2):
            piece = dstate[HALF * half : HALF * half + HALF, :]
            for tile in range(2):
                at = SUMS + QUARTER * (s // 2) + BLOCK * (2 * half + tile)
                block = jnp.concatenate([piece[:, 128 * tile : 128 * tile + 128], zero_rows], axis=0)
                msg[s % 2, at : at + BLOCK, :] = block.astype(BF16)

    factor = float(STEPS * 192 * 96) ** (-0.5)

    def put(tile, value):
        for j in range(value.shape[1] // 128):
            start = (tile + j) * CH
            done = 0
            while done < CH:
                part, row = divmod(start + done, SUMS)
                n = min(CH - done, SUMS - row)
                msg[part, row : row + n, :] = value[done : done + n, 128 * j : 128 * j + 128]
                done += n

    cot_all = cot_s[...].astype(BF16)
    put(12, (tn(cot_all, act[...]) * factor).astype(BF16))
    put(6, (tn(nm_s[...], dpre_s[...].astype(BF16)) * factor).astype(BF16))
    g_qkv = tn(normed_s[...].astype(BF16), dqkv_s[...].astype(BF16)) * factor
    g_out = tn(mixed_s[...].astype(BF16), dproj_s[...].astype(BF16)) * factor
    put(0, jnp.concatenate([g_qkv, g_out], axis=1).astype(BF16))
    small[...] = jnp.zeros_like(small)
    for i, total in enumerate((land_sum, gain_a_sum, gain_m_sum)):
        total = total * factor
        small[2 * i : 2 * i + 1, :] = total[:, 0:128]
        small[2 * i + 1 : 2 * i + 2, 0:64] = total[:, 128:192]
    msg[1, 18 * CH - SUMS : SUMS, :] = small[...].astype(BF16)
    copies = [
        pltpu.make_async_copy(msg.at[1 - core], send_out, sems.at[0]),
        pltpu.make_async_copy(msg.at[core], keep_out, sems.at[1]),
    ]
    for copy in copies:
        copy.start()
    for copy in copies:
        copy.wait()


SMALL_ROWS = 2 * SUMS - 18 * CH


def pair_kernel(kept, arrived, chunks, x_send, x_keep):
    core = lax.axis_index("core")
    here = lax.axis_index("xh")
    for g in range(GROUP):
        at = UNIT * g
        total = kept[at : at + UNIT, :].astype(F32) + arrived[at : at + UNIT, :].astype(F32)
        chunks[g] = total.astype(BF16)
    own = pl.ds(pl.multiple_of(SUMS + QUARTER * here, 64), QUARTER)
    other = pl.ds(pl.multiple_of(SUMS + QUARTER * (1 - here), 64), QUARTER)
    x_send[core] = kept[other, :]
    x_send[1 - core] = arrived[other, :]
    x_keep[core] = kept[own, :]
    x_keep[1 - core] = arrived[own, :]


def group_kernel(terms, total_out):
    total = terms[0].astype(F32)
    for g in range(1, GROUP):
        total = total + terms[g].astype(F32)
    total = total.astype(BF16)
    for g in range(8):
        total_out[g] = total


def column_kernel(terms, kept, arrived, total_out, near, to_lon, to_lat, to_both):
    here = lax.axis_index("xh")
    half = QUARTER // 2
    for c in range(2):
        near[2 * here + c] = kept[c, 0:half, :]
        near[2 * (1 - here) + c] = arrived[c, 0:half, :]
        to_lon[2 * here + c] = kept[c, half:QUARTER, :]
        to_lon[2 * (1 - here) + c] = arrived[c, half:QUARTER, :]
    to_lat[...] = near[3]
    to_both[...] = to_lon[3]
    total = terms[0].astype(F32)
    for g in range(1, 8):
        total = total + terms[g].astype(F32)
    total = total.astype(BF16)
    for g in range(GROUP):
        total_out[g] = total


def unpack_kernel(
    own, other, g_qkv, g_out, g_up, g_down, g_land, g_ga, g_gm, msg
):
    core = lax.axis_index("core")
    for g in range(GROUP):
        msg[core, UNIT * g : UNIT * g + UNIT, :] = own[g]
        msg[1 - core, UNIT * g : UNIT * g + UNIT, :] = other[g]

    def rows_of(start, count):
        pieces = []
        done = 0
        while done < count:
            part, row = divmod(start + done, SUMS)
            n = min(count - done, SUMS - row)
            pieces.append(msg[part, row : row + n, :].astype(F32))
            done += n
        return pieces[0] if len(pieces) == 1 else jnp.concatenate(pieces, axis=0)

    for j in range(4):
        g_qkv[:, 128 * j : 128 * j + 128] = rows_of(j * CH, CH)
    mid = rows_of(4 * CH, CH)
    tail = rows_of(5 * CH, CH)
    g_qkv[:, 512:576] = mid[:, 0:64]
    g_out[...] = jnp.concatenate([mid[:, 64:128], tail], axis=1)
    for j in range(6):
        g_up[:, 128 * j : 128 * j + 128] = rows_of((6 + j) * CH, CH)
        g_down[:, 128 * j : 128 * j + 128] = rows_of((12 + j) * CH, CH)
    little = rows_of(18 * CH, 16)
    for i, out in enumerate((g_land, g_ga, g_gm)):
        out[...] = jnp.concatenate(
            [little[2 * i : 2 * i + 1, :], little[2 * i + 1 : 2 * i + 2, 0:64]], axis=1
        )


def state_kernel(near, from_lon, from_lat, from_both, state_out):
    for first, wide, edge in ((6, near, from_lat), (0, from_lon, from_both)):
        for tile, lanes in ((0, slice(0, 128)), (1, slice(128, 192))):
            n = lanes.stop - lanes.start
            at = slice(BLOCK * tile, BLOCK * tile + BLOCK)
            before = edge[at, :].astype(F32)
            for c in range(6):
                state_out[first + c, 0:3, lanes] = before[6 * c + 3 : 6 * c + 6, 0:n]
            for k in range(4):
                block = wide[k, at, :].astype(F32)
                tall = 6 if k < 3 else 3
                for c in range(6):
                    state_out[first + c, 6 * k + 3 : 6 * k + 3 + tall, lanes] = block[
                        6 * c : 6 * c + tall, 0:n
                    ]


def hop(value, rows, cols, xh=0, cores=((0, 0), (1, 1))):
    pairs = []
    for h in range(2):
        for source, target in cores:
            for a in range(8):
                for b in range(8):
                    k = 2 * ((h + xh) % 2) + target
                    to = (k * 8 + (a + rows) % 8) * 8 + (b + cols) % 8
                    pairs.append((((2 * h + source) * 8 + a) * 8 + b, to))
    return lax.ppermute(value, AXES, pairs)


def swap(value, axis):
    return lax.ppermute(value, axis, [(0, 1), (1, 0)])


def exchange(value, axis):
    return lax.all_to_all(value, axis, 0, 0, tiled=True)


def call(kernel, name, outs, scratch=(), mib=8, from_hbm=0, placed=False):
    specs = {}
    if placed:
        specs["out_specs"] = tuple(pl.BlockSpec(memory_space=pl.ANY) for _ in outs)
    if from_hbm:
        specs["in_specs"] = [pl.BlockSpec(memory_space=pltpu.HBM)] * from_hbm
    return pl.pallas_call(
        kernel,
        out_shape=tuple(jax.ShapeDtypeStruct(dims, kind) for dims, kind in outs),
        scratch_shapes=[pltpu.VMEM(dims, kind) if kind else dims for dims, kind in scratch],
        compiler_params=pltpu.CompilerParams(vmem_limit_bytes=mib * MIB),
        name=name,
        **specs,
    )


def local(
    states, loss_grads, land_sea, land_embed, gain_attn, gain_mlp, w_qkv, w_out, w_up, w_down
):
    keep, send, edge, vectors, w_qkv = call(
        pack_kernel,
        "pack_cells",
        [((2, 2, HALF, MSG), BF16)] * 2 + [((2, HALF // 2, MSG), BF16), ((8, CH), F32)]
        + [((CH, 3 * CH), BF16)],
        [
            ((WIN_LON, ROWS, CH), BF16),
            ((WIN_LON, ROWS, CH), BF16),
            ((WIN_LON, ROWS), jnp.int32),
            ((8, CH), F32),
            ((2, 2, 2, HALF, MSG), F32),
            ((2, HALF // 2, MSG), F32),
            (pltpu.SemaphoreType.DMA((7,)), None),
        ],
        from_hbm=7,
    )(
        *(
            pltpu.with_memory_space_constraint(value, pltpu.HBM)
            for value in (
                states[0, 0].transpose(1, 0, 2), loss_grads[0, 0].transpose(1, 0, 2), land_sea.T,
                land_embed[None], gain_attn[None], gain_mlp[None], w_qkv,
            )
        )
    )
    near_own, near_x, lon_own, lon_x = call(
        sort_kernel,
        "sort_windows",
        [((2, HALF, MSG), BF16)] * 4,
        [((2, 2, 2, HALF, MSG), F32)],
    )(
        keep, swap(send, "core"),
        hop(edge, -1, 0, cores=((0, 1),)), hop(edge, -1, 0, cores=((1, 1),)),
    )
    near_x = hop(near_x, 0, 0, 1)
    lon_own = hop(lon_own, 0, -1)
    lon_x = hop(lon_x, 0, -1, 1)
    send, keep = call(
        main_kernel,
        "window_steps",
        [((SENT, 128), BF16)] * 2,
        [
            ((STEPS, WIN, MSG), F32),
            ((TOK, 3 * CH), F32),
            ((STEPS, WIN, HEADS * WIN), F32),
            ((STEPS, HEADS * WIN, CH), BF16),
            ((TOK, CH), F32),
            ((TOK, CH), F32),
            ((TOK, 1), F32),
            ((TOK, CH), F32),
            ((TOK, 1), F32),
            ((TOK, MLP), F32),
            ((TOK, MLP), BF16),
            ((TOK, CH), F32),
            ((TOK, CH), F32),
            ((TOK, CH), BF16),
            ((TOK, CH), F32),
            ((TOK, MLP), F32),
            ((TOK, CH), F32),
            ((TOK, 3 * CH), F32),
            ((WIN, 256), F32),
            ((SMALL_ROWS, 128), F32),
            ((2, SENT, 128), BF16),
            (pltpu.SemaphoreType.DMA((2,)), None),
        ],
        mib=24,
        placed=True,
    )(
        near_own, near_x, lon_own, lon_x, vectors, w_qkv, w_out, w_up, w_down.T
    )

    chunks, x_send, x_keep = call(
        pair_kernel,
        "sum_cores",
        [((GROUP, UNIT, 128), BF16)] + [((2, QUARTER, 128), BF16)] * 2,
    )(keep, swap(send, "core"))
    x_arrived = swap(x_send, "xh")
    (partial,) = call(group_kernel, "sum_group", [((8, UNIT, 128), BF16)])(
        exchange(chunks, ("xh", "lon"))
    )
    total, near, to_lon, to_lat, to_both = call(
        column_kernel,
        "sum_column",
        [((GROUP, UNIT, 128), BF16)]
        + [((4, QUARTER // 2, 128), BF16)] * 2
        + [((QUARTER // 2, 128), BF16)] * 2,
    )(exchange(partial, "lat"), x_keep, x_arrived)
    from_lon = hop(to_lon, 0, 1)
    from_lat = hop(to_lat, 1, 0)
    from_both = hop(to_both, 1, 1)
    own, from_lon, from_lat, from_both = lax.optimization_barrier(
        (exchange(total, ("xh", "lon")), from_lon, from_lat, from_both)
    )
    (state_grads,) = call(state_kernel, "unpack_states", [((WIN_LON, ROWS, CH), F32)])(
        near, from_lon, from_lat, from_both
    )
    outs = call(
        unpack_kernel,
        "unpack_sums",
        [
            ((CH, 3 * CH), F32),
            ((CH, CH), F32),
            ((CH, MLP), F32),
            ((CH, MLP), F32),
            ((1, CH), F32),
            ((1, CH), F32),
            ((1, CH), F32),
        ],
        [((2, SUMS, 128), BF16)],
        mib=16,
    )(own, swap(own, "core"))
    return (
        state_grads.transpose(1, 0, 2)[None, None],
        outs[0], outs[1], outs[2], outs[3].T, outs[4][0], outs[5][0], outs[6][0],
    )


def solution(mesh):
    halves = Mesh(mesh.devices.reshape(2, 2, *mesh.devices.shape[1:]), AXES)
    cell = P(("xh", "core"), None, "lat", "lon", None)
    return jax.shard_map(
        local,
        mesh=halves,
        in_specs=(cell, cell, P("lat", "lon"), P(), P(), P(), P(), P(), P(), P()),
        out_specs=(cell, P(), P(), P(), P(), P(), P(), P()),
        check_vma=False,
    )
```

```python
import jax
import jax.numpy as jnp
from jax import lax
from jax.experimental import pallas as pl
from jax.experimental.pallas import tpu as pltpu
from jax.sharding import Mesh
from jax.sharding import PartitionSpec as P

CH = 192
HEADS = 6
HEAD_DIM = 32
MLP = 768
ROWS = 24
WIN_LAT = 6
WIN_LON = 12
WIN = WIN_LAT * WIN_LON
HALF = WIN // 2
STEPS = 4
TOK = STEPS * WIN
MSG = 512
GROUP = 16
UNIT = 112
SUMS = GROUP * UNIT
BLOCK = 48
QUARTER = 4 * BLOCK
SENT = SUMS + 2 * QUARTER
HALF_CH = CH // 2
TILED = 18 * HALF_CH
SCALE = HEAD_DIM ** (-0.5)
EPS = 1e-05
F32 = jnp.float32
BF16 = jnp.bfloat16
AXES = ("xh", "core", "lat", "lon")
MIB = 1024 * 1024


def nn(a, b):
    return lax.dot_general(a, b, (((1,), (0,)), ((), ())), preferred_element_type=F32)


def nt(a, b):
    return lax.dot_general(a, b, (((1,), (1,)), ((), ())), preferred_element_type=F32)


def tn(a, b):
    return lax.dot_general(a, b, (((0,), (0,)), ((), ())), preferred_element_type=F32)


def mean_of(v):
    return jnp.sum(v, axis=-1, keepdims=True) * (1.0 / CH)


def pack_kernel(
    states_in, loss_in, land_in, embed_in, gain_a_in, gain_m_in, wqkv_in,
    keep_out, send_out, edge_out, vectors_out, wqkv_out,
    states, loss, land, vectors, cells, edges, sems,
):
    pairs = (
        (states_in, states), (loss_in, loss), (land_in, land),
        (embed_in, vectors.at[0:1]), (gain_a_in, vectors.at[1:2]), (gain_m_in, vectors.at[2:3]),
    )
    copies = [
        pltpu.make_async_copy(source, target, sems.at[i])
        for i, (source, target) in enumerate(pairs)
    ]
    weights = pltpu.make_async_copy(wqkv_in, wqkv_out, sems.at[6])
    for copy in copies:
        copy.start()
    weights.start()
    for copy in copies:
        copy.wait()
    core = lax.axis_index("core")
    mask = land[...].astype(F32)
    nothing = jnp.zeros((3, MSG), F32)
    for c in range(WIN_LON):
        column = jnp.broadcast_to(mask[c : c + 1, :], (64, ROWS)).T
        cell = jnp.concatenate(
            [states[c].astype(F32), column, loss[c].astype(F32), column], axis=1
        )
        part, at = (1, 6 * c) if c < 6 else (0, 6 * (c - 6))
        for k in range(3):
            cells[k % 2, k // 2, part, at : at + 6, :] = cell[6 * k + 3 : 6 * k + 9]
        cells[1, 1, part, at : at + 3, :] = cell[21:24]
        cells[1, 1, part, at + 3 : at + 6, :] = nothing
        edges[part, at // 2 : at // 2 + 3, :] = cell[0:3]
    keep_out[...] = cells[core].astype(BF16)
    send_out[...] = cells[1 - core].astype(BF16)
    edge_out[...] = edges[...].astype(BF16)
    vectors_out[...] = vectors[...]
    weights.wait()


def sort_kernel(kept, arrived, edge0, edge1, near_own, near_x, lon_own, lon_x, cells):
    core = lax.axis_index("core")
    here = lax.axis_index("xh")
    cells[core] = kept[...].astype(F32)
    cells[1 - core] = arrived[...].astype(F32)

    @pl.when(core == 1)
    def _():
        for step, edge in enumerate((edge0, edge1)):
            for part in range(2):
                rows = edge[part].astype(F32)
                for c in range(6):
                    cells[step, 1, part, 6 * c + 3 : 6 * c + 6, :] = rows[3 * c : 3 * c + 3]

    for step in range(2):
        near_own[step] = cells[step, here, 0].astype(BF16)
        near_x[step] = cells[step, 1 - here, 0].astype(BF16)
        lon_own[step] = cells[step, here, 1].astype(BF16)
        lon_x[step] = cells[step, 1 - here, 1].astype(BF16)


def main_kernel(
    near_own, near_x, lon_own, lon_x, vectors, wqkv, wout, wup, wdown_t,
    send_out, keep_out,
    x, qkv, probs, qm_all, emb, xh1, r1, hid_xh, r2, gp, act, normed_s, mixed_s, nm_s,
    cot_s, dpre_s, dproj_s, dqkv_s, dstate, small, msg,
):
    core = lax.axis_index("core")
    here = lax.axis_index("xh")
    last = jnp.logical_and(lax.axis_index("lat") == 7, jnp.logical_and(here == 1, core == 1))
    closed = jnp.where(last, 0.0, 1.0).astype(F32)
    for step in range(2):
        x[2 * here + step, 0:HALF, :] = near_own[step].astype(F32)
        x[2 * here + step, HALF:WIN, :] = lon_own[step].astype(F32)
        x[2 * (1 - here) + step, 0:HALF, :] = near_x[step].astype(F32)
        x[2 * (1 - here) + step, HALF:WIN, :] = lon_x[step].astype(F32)
    le = vectors[0:1, :]
    ga = vectors[1:2, :]
    gm = vectors[2:3, :]
    col_head = lax.broadcasted_iota(jnp.int32, (1, CH), 1) // HEAD_DIM
    masks = [(col_head == h).astype(F32) for h in range(HEADS)]
    row_half = lax.rem(lax.broadcasted_iota(jnp.int32, (WIN, WIN), 0), WIN_LAT) // 3
    key_half = lax.rem(lax.broadcasted_iota(jnp.int32, (WIN, WIN), 1), WIN_LAT) // 3
    allow1 = jnp.where(row_half == key_half, 1.0, closed).astype(F32)
    allow = jnp.concatenate([allow1] * HEADS, axis=1)

    def spread(v):
        return jnp.concatenate([v * m for m in masks], axis=0).astype(BF16)

    def gathered(v):
        total = v[0:WIN] * masks[0]
        for h in range(1, HEADS):
            total = total + v[WIN * h : WIN * h + WIN] * masks[h]
        return total

    for s in range(STEPS):
        rows = slice(WIN * s, WIN * s + WIN)
        land = x[s, :, 192:256][:, 0:1]
        e = x[s, :, 0:CH] + land * le
        emb[rows, :] = e
        off = e - mean_of(e)
        r = lax.rsqrt(mean_of(off * off) + EPS)
        xh = off * r
        xh1[rows, :] = xh
        r1[rows, :] = r
        normed_s[rows, :] = xh * ga
    normed = normed_s[...].astype(BF16)
    qkv[...] = nn(normed, wqkv[...]).astype(BF16).astype(F32)
    for s in range(STEPS):
        rows = slice(WIN * s, WIN * s + WIN)
        qm = spread(qkv[rows, 0:CH])
        qm_all[s] = qm
        keys = qkv[rows, CH : 2 * CH].astype(BF16)
        values = qkv[rows, 2 * CH : 3 * CH].astype(BF16)
        weights = jnp.exp(nt(keys, qm) * SCALE) * allow
        p = weights / jnp.sum(weights, axis=0, keepdims=True)
        probs[s] = p
        mixed_s[rows, :] = gathered(tn(p.astype(BF16), values))
    mixed = mixed_s[...].astype(BF16)
    projected = nn(mixed, wout[...]).astype(BF16).astype(F32)
    hid = emb[...] + projected
    off = hid - mean_of(hid)
    r = lax.rsqrt(mean_of(off * off) + EPS)
    xh = off * r
    hid_xh[...] = xh
    r2[...] = r
    nm_s[...] = (xh * gm).astype(BF16)
    for j in range(MLP // 256):
        cols = slice(256 * j, 256 * j + 256)
        pre = nn(nm_s[...], wup[:, cols])
        cdf = 0.5 * (1.0 + lax.erf(pre * (0.5 ** 0.5)))
        pdf = jnp.exp(pre * pre * -0.5) * 0.3989422804014327
        act[:, cols] = (pre * cdf).astype(BF16)
        gp[:, cols] = cdf + pre * pdf

    gain_m_sum = jnp.zeros((1, CH), F32)
    gain_a_sum = jnp.zeros((1, CH), F32)
    land_sum = jnp.zeros((1, CH), F32)
    incoming = None
    wq = wqkv[:, 0:CH]
    wk = wqkv[:, CH : 2 * CH]
    wv = wqkv[:, 2 * CH : 3 * CH]
    zero_rows = jnp.zeros((BLOCK - HALF, 128), F32)
    dstate[...] = jnp.zeros_like(dstate)
    for s in range(STEPS - 1, -1, -1):
        rows = slice(WIN * s, WIN * s + WIN)
        cot = x[s, :, 256:448]
        if incoming is not None:
            cot = cot + incoming
        cotb = cot.astype(BF16)
        cot_s[rows, :] = cotb.astype(F32)
        d_pre = gp[rows, :] * nn(cotb, wdown_t[...])
        dpre_b = d_pre.astype(BF16)
        dpre_s[rows, :] = dpre_b.astype(F32)
        dy = nt(dpre_b, wup[...])
        xh = hid_xh[rows, :]
        gain_m_sum = gain_m_sum + jnp.sum(dy * xh, axis=0, keepdims=True)
        dxh = dy * gm
        d_hid = cot + r2[rows, :] * (dxh - mean_of(dxh) - xh * mean_of(dxh * xh))
        dproj = d_hid.astype(BF16)
        dproj_s[rows, :] = dproj.astype(F32)
        d_mixed = nt(dproj, wout[...]).astype(BF16).astype(F32)
        dm = spread(d_mixed)
        keys = qkv[rows, CH : 2 * CH].astype(BF16)
        values = qkv[rows, 2 * CH : 3 * CH].astype(BF16)
        p = probs[s]
        dp = nt(values, dm)
        dv = nn(p.astype(BF16), dm).astype(BF16)
        ds = (p * (dp - jnp.sum(p * dp, axis=0, keepdims=True)) * SCALE).astype(BF16)
        dq = gathered(tn(ds, keys)).astype(BF16)
        dk = nn(ds, qm_all[s]).astype(BF16)
        dqkv_s[rows, 0:CH] = dq.astype(F32)
        dqkv_s[rows, CH : 2 * CH] = dk.astype(F32)
        dqkv_s[rows, 2 * CH : 3 * CH] = dv.astype(F32)
        d_rolled = nt(dq, wq) + nt(dk, wk) + nt(dv, wv)
        dy = d_rolled.astype(BF16).astype(F32)
        xh = xh1[rows, :]
        gain_a_sum = gain_a_sum + jnp.sum(dy * xh, axis=0, keepdims=True)
        dxh = dy * ga
        d_state = d_hid + r1[rows, :] * (dxh - mean_of(dxh) - xh * mean_of(dxh * xh))
        land = x[s, :, 192:256][:, 0:1]
        land_sum = land_sum + jnp.sum(d_state * land, axis=0, keepdims=True)
        incoming = d_state.astype(BF16).astype(F32)
        dstate[:, 0:CH] = incoming
        for half in range(2):
            piece = dstate[HALF * half : HALF * half + HALF, :]
            for tile in range(2):
                at = QUARTER * (s // 2) + BLOCK * (2 * half + tile)
                block = jnp.concatenate([piece[:, 128 * tile : 128 * tile + 128], zero_rows], axis=0)
                msg[s % 2, at : at + BLOCK, :] = block.astype(BF16)

    factor = float(STEPS * 192 * 96) ** (-0.5)

    def own_first(v):
        return jnp.where(core == 0, v, jnp.concatenate([v[:, HALF_CH:], v[:, :HALF_CH]], axis=1))

    def put(tile, value):
        value = (value * factor).astype(BF16)
        for j in range(value.shape[1] // 128):
            at = (tile + j) * HALF_CH
            piece = value[:, 128 * j : 128 * j + 128]
            keep_out[at : at + HALF_CH, :] = piece[:HALF_CH]
            send_out[at : at + HALF_CH, :] = piece[HALF_CH:]

    put(12, tn(own_first(cot_s[...]).astype(BF16), act[...]))
    put(6, tn(own_first(nm_s[...]), dpre_s[...].astype(BF16)))
    g_qkv = tn(own_first(normed_s[...]).astype(BF16), dqkv_s[...].astype(BF16))
    g_out = tn(own_first(mixed_s[...]).astype(BF16), dproj_s[...].astype(BF16))
    put(0, jnp.concatenate([g_qkv, g_out], axis=1))
    small[...] = jnp.zeros_like(small)
    for i, total in enumerate((land_sum, gain_a_sum, gain_m_sum)):
        total = total * factor
        small[2 * i : 2 * i + 1, :] = total[:, 0:128]
        small[2 * i + 1 : 2 * i + 2, 0:64] = total[:, 128:192]
    keep_out[TILED:SUMS, :] = jnp.where(core == 1, small[...], 0.0).astype(BF16)
    send_out[TILED:SUMS, :] = jnp.where(core == 1, 0.0, small[...]).astype(BF16)
    keep_out[SUMS:SENT, :] = msg[core]
    send_out[SUMS:SENT, :] = msg[1 - core]


def pair_kernel(kept, arrived, chunks, x_send, x_keep):
    core = lax.axis_index("core")
    here = lax.axis_index("xh")
    for g in range(GROUP):
        at = UNIT * g
        total = kept[at : at + UNIT, :].astype(F32) + arrived[at : at + UNIT, :].astype(F32)
        chunks[g] = total.astype(BF16)
    own = pl.ds(pl.multiple_of(SUMS + QUARTER * here, 64), QUARTER)
    other = pl.ds(pl.multiple_of(SUMS + QUARTER * (1 - here), 64), QUARTER)
    x_send[core] = kept[other, :]
    x_send[1 - core] = arrived[other, :]
    x_keep[core] = kept[own, :]
    x_keep[1 - core] = arrived[own, :]


def group_kernel(terms, total_out):
    total = terms[0].astype(F32)
    for g in range(1, GROUP):
        total = total + terms[g].astype(F32)
    total = total.astype(BF16)
    for g in range(8):
        total_out[g] = total


def column_kernel(terms, kept, arrived, total_out, near, to_lon, to_lat, to_both):
    here = lax.axis_index("xh")
    half = QUARTER // 2
    for c in range(2):
        near[2 * here + c] = kept[c, 0:half, :]
        near[2 * (1 - here) + c] = arrived[c, 0:half, :]
        to_lon[2 * here + c] = kept[c, half:QUARTER, :]
        to_lon[2 * (1 - here) + c] = arrived[c, half:QUARTER, :]
    to_lat[...] = near[3]
    to_both[...] = to_lon[3]
    total = terms[0].astype(F32)
    for g in range(1, 8):
        total = total + terms[g].astype(F32)
    total = total.astype(BF16)
    for g in range(GROUP):
        total_out[g] = total


def unpack_kernel(own, other, g_qkv, g_out, g_up, g_down, g_land, g_ga, g_gm):
    core = lax.axis_index("core")
    for rows, half in ((core, own), (1 - core, other)):
        to = pl.ds(pl.multiple_of(HALF_CH * rows, 32), HALF_CH)

        def tile(t):
            return half[HALF_CH * t : HALF_CH * t + HALF_CH, :].astype(F32)

        for j in range(4):
            g_qkv[to, 128 * j : 128 * j + 128] = tile(j)
        mid = tile(4)
        g_qkv[to, 512:576] = mid[:, 0:64]
        g_out[to, :] = jnp.concatenate([mid[:, 64:128], tile(5)], axis=1)
        for j in range(6):
            g_up[to, 128 * j : 128 * j + 128] = tile(6 + j)
            g_down[to, 128 * j : 128 * j + 128] = tile(12 + j)
    little = jnp.where(
        core == 1, own[TILED : TILED + 16, :].astype(F32), other[TILED : TILED + 16, :].astype(F32)
    )
    for i, out in enumerate((g_land, g_ga, g_gm)):
        out[...] = jnp.concatenate(
            [little[2 * i : 2 * i + 1, :], little[2 * i + 1 : 2 * i + 2, 0:64]], axis=1
        )


def state_kernel(near, from_lon, from_lat, from_both, state_out):
    for first, wide, edge in ((6, near, from_lat), (0, from_lon, from_both)):
        for tile, lanes in ((0, slice(0, 128)), (1, slice(128, 192))):
            n = lanes.stop - lanes.start
            at = slice(BLOCK * tile, BLOCK * tile + BLOCK)
            before = edge[at, :].astype(F32)
            for c in range(6):
                state_out[first + c, 0:3, lanes] = before[6 * c + 3 : 6 * c + 6, 0:n]
            for k in range(4):
                block = wide[k, at, :].astype(F32)
                tall = 6 if k < 3 else 3
                for c in range(6):
                    state_out[first + c, 6 * k + 3 : 6 * k + 3 + tall, lanes] = block[
                        6 * c : 6 * c + tall, 0:n
                    ]


def hop(value, rows, cols, xh=0, cores=((0, 0), (1, 1))):
    pairs = []
    for h in range(2):
        for source, target in cores:
            for a in range(8):
                for b in range(8):
                    k = 2 * ((h + xh) % 2) + target
                    to = (k * 8 + (a + rows) % 8) * 8 + (b + cols) % 8
                    pairs.append((((2 * h + source) * 8 + a) * 8 + b, to))
    return lax.ppermute(value, AXES, pairs)


def swap(value, axis):
    return lax.ppermute(value, axis, [(0, 1), (1, 0)])


def exchange(value, axis):
    return lax.all_to_all(value, axis, 0, 0, tiled=True)


def call(kernel, name, outs, scratch=(), mib=8, from_hbm=0):
    specs = {}
    if from_hbm:
        specs["in_specs"] = [pl.BlockSpec(memory_space=pltpu.HBM)] * from_hbm
    return pl.pallas_call(
        kernel,
        out_shape=tuple(jax.ShapeDtypeStruct(dims, kind) for dims, kind in outs),
        scratch_shapes=[pltpu.VMEM(dims, kind) if kind else dims for dims, kind in scratch],
        compiler_params=pltpu.CompilerParams(vmem_limit_bytes=mib * MIB),
        name=name,
        **specs,
    )


def local(
    states, loss_grads, land_sea, land_embed, gain_attn, gain_mlp, w_qkv, w_out, w_up, w_down
):
    keep, send, edge, vectors, w_qkv = call(
        pack_kernel,
        "pack_cells",
        [((2, 2, HALF, MSG), BF16)] * 2 + [((2, HALF // 2, MSG), BF16), ((8, CH), F32)]
        + [((CH, 3 * CH), BF16)],
        [
            ((WIN_LON, ROWS, CH), BF16),
            ((WIN_LON, ROWS, CH), BF16),
            ((WIN_LON, ROWS), jnp.int32),
            ((8, CH), F32),
            ((2, 2, 2, HALF, MSG), F32),
            ((2, HALF // 2, MSG), F32),
            (pltpu.SemaphoreType.DMA((7,)), None),
        ],
        from_hbm=7,
    )(
        *(
            pltpu.with_memory_space_constraint(value, pltpu.HBM)
            for value in (
                states[0, 0].transpose(1, 0, 2), loss_grads[0, 0].transpose(1, 0, 2), land_sea.T,
                land_embed[None], gain_attn[None], gain_mlp[None], w_qkv,
            )
        )
    )
    near_own, near_x, lon_own, lon_x = call(
        sort_kernel,
        "sort_windows",
        [((2, HALF, MSG), BF16)] * 4,
        [((2, 2, 2, HALF, MSG), F32)],
    )(
        keep, swap(send, "core"),
        hop(edge, -1, 0, cores=((0, 1),)), hop(edge, -1, 0, cores=((1, 1),)),
    )
    near_x = hop(near_x, 0, 0, 1)
    lon_own = hop(lon_own, 0, -1)
    lon_x = hop(lon_x, 0, -1, 1)
    send, keep = call(
        main_kernel,
        "window_steps",
        [((SENT, 128), BF16)] * 2,
        [
            ((STEPS, WIN, MSG), F32),
            ((TOK, 3 * CH), F32),
            ((STEPS, WIN, HEADS * WIN), F32),
            ((STEPS, HEADS * WIN, CH), BF16),
            ((TOK, CH), F32),
            ((TOK, CH), F32),
            ((TOK, 1), F32),
            ((TOK, CH), F32),
            ((TOK, 1), F32),
            ((TOK, MLP), F32),
            ((TOK, MLP), BF16),
            ((TOK, CH), F32),
            ((TOK, CH), F32),
            ((TOK, CH), BF16),
            ((TOK, CH), F32),
            ((TOK, MLP), F32),
            ((TOK, CH), F32),
            ((TOK, 3 * CH), F32),
            ((WIN, 256), F32),
            ((SUMS - TILED, 128), F32),
            ((2, 2 * QUARTER, 128), BF16),
        ],
        mib=24,
    )(
        near_own, near_x, lon_own, lon_x, vectors, w_qkv, w_out, w_up, w_down.T
    )

    chunks, x_send, x_keep = call(
        pair_kernel,
        "sum_cores",
        [((GROUP, UNIT, 128), BF16)] + [((2, QUARTER, 128), BF16)] * 2,
    )(keep, swap(send, "core"))
    x_arrived = swap(x_send, "xh")
    (partial,) = call(group_kernel, "sum_group", [((8, UNIT, 128), BF16)])(
        exchange(chunks, ("xh", "lon"))
    )
    total, near, to_lon, to_lat, to_both = call(
        column_kernel,
        "sum_column",
        [((GROUP, UNIT, 128), BF16)]
        + [((4, QUARTER // 2, 128), BF16)] * 2
        + [((QUARTER // 2, 128), BF16)] * 2,
    )(exchange(partial, "lat"), x_keep, x_arrived)
    from_lon = hop(to_lon, 0, 1)
    from_lat = hop(to_lat, 1, 0)
    from_both = hop(to_both, 1, 1)
    own, from_lon, from_lat, from_both = lax.optimization_barrier(
        (exchange(total, ("xh", "lon")), from_lon, from_lat, from_both)
    )
    own = own.reshape(SUMS, 128)
    (state_grads,) = call(state_kernel, "unpack_states", [((WIN_LON, ROWS, CH), F32)])(
        near, from_lon, from_lat, from_both
    )
    outs = call(
        unpack_kernel,
        "unpack_sums",
        [
            ((CH, 3 * CH), F32),
            ((CH, CH), F32),
            ((CH, MLP), F32),
            ((CH, MLP), F32),
            ((1, CH), F32),
            ((1, CH), F32),
            ((1, CH), F32),
        ],
        mib=16,
    )(own, swap(own, "core"))
    return (
        state_grads.transpose(1, 0, 2)[None, None],
        outs[0], outs[1], outs[2], outs[3].T, outs[4][0], outs[5][0], outs[6][0],
    )


def solution(mesh):
    halves = Mesh(mesh.devices.reshape(2, 2, *mesh.devices.shape[1:]), AXES)
    cell = P(("xh", "core"), None, "lat", "lon", None)
    return jax.shard_map(
        local,
        mesh=halves,
        in_specs=(cell, cell, P("lat", "lon"), P(), P(), P(), P(), P(), P(), P()),
        out_specs=(cell, P(), P(), P(), P(), P(), P(), P()),
        check_vma=False,
    )
```

```python
import jax
import jax.numpy as jnp
from jax import lax
from jax.experimental import pallas as pl
from jax.experimental.pallas import tpu as pltpu
from jax.sharding import Mesh
from jax.sharding import PartitionSpec as P

CH = 192
HEADS = 6
HEAD_DIM = 32
MLP = 768
ROWS = 24
WIN_LAT = 6
WIN_LON = 12
WIN = WIN_LAT * WIN_LON
HALF = WIN // 2
STEPS = 4
TOK = STEPS * WIN
MSG = 512
GROUP = 16
UNIT = 112
SUMS = GROUP * UNIT
BLOCK = 48
QUARTER = 4 * BLOCK
COLUMNS = QUARTER // 2
SENT = SUMS + 2 * QUARTER
HALF_CH = CH // 2
TILED = 18 * HALF_CH
SCALE = HEAD_DIM ** (-0.5)
EPS = 1e-05
F32 = jnp.float32
BF16 = jnp.bfloat16
AXES = ("xh", "core", "lat", "lon")
MIB = 1024 * 1024


def nn(a, b):
    return lax.dot_general(a, b, (((1,), (0,)), ((), ())), preferred_element_type=F32)


def nt(a, b):
    return lax.dot_general(a, b, (((1,), (1,)), ((), ())), preferred_element_type=F32)


def tn(a, b):
    return lax.dot_general(a, b, (((0,), (0,)), ((), ())), preferred_element_type=F32)


def mean_of(v):
    return jnp.sum(v, axis=-1, keepdims=True) * (1.0 / CH)


def pack_kernel(
    states_in, loss_in, land_in, embed_in, gain_a_in, gain_m_in, wqkv_in,
    keep_out, send_out, edge_out, vectors_out, wqkv_out,
    states, loss, land, vectors, cells, edges, sems,
):
    pairs = (
        (states_in, states), (loss_in, loss), (land_in, land),
        (embed_in, vectors.at[0:1]), (gain_a_in, vectors.at[1:2]), (gain_m_in, vectors.at[2:3]),
    )
    copies = [
        pltpu.make_async_copy(source, target, sems.at[i])
        for i, (source, target) in enumerate(pairs)
    ]
    weights = pltpu.make_async_copy(wqkv_in, wqkv_out, sems.at[6])
    for copy in copies:
        copy.start()
    weights.start()
    for copy in copies:
        copy.wait()
    core = lax.axis_index("core")
    mask = land[...].astype(F32)
    nothing = jnp.zeros((3, MSG), F32)
    for c in range(WIN_LON):
        column = jnp.broadcast_to(mask[c : c + 1, :], (64, ROWS)).T
        cell = jnp.concatenate(
            [states[c].astype(F32), column, loss[c].astype(F32), column], axis=1
        )
        part, at = (1, 6 * c) if c < 6 else (0, 6 * (c - 6))
        for k in range(3):
            cells[k % 2, k // 2, part, at : at + 6, :] = cell[6 * k + 3 : 6 * k + 9]
        cells[1, 1, part, at : at + 3, :] = cell[21:24]
        cells[1, 1, part, at + 3 : at + 6, :] = nothing
        edges[part, at // 2 : at // 2 + 3, :] = cell[0:3]
    keep_out[...] = cells[core].astype(BF16)
    send_out[...] = cells[1 - core].astype(BF16)
    edge_out[...] = edges[...].astype(BF16)
    vectors_out[...] = vectors[...]
    weights.wait()


def sort_kernel(kept, arrived, edge0, edge1, near_own, near_x, lon_own, lon_x, cells):
    core = lax.axis_index("core")
    here = lax.axis_index("xh")
    cells[core] = kept[...].astype(F32)
    cells[1 - core] = arrived[...].astype(F32)

    @pl.when(core == 1)
    def _():
        for step, edge in enumerate((edge0, edge1)):
            for part in range(2):
                rows = edge[part].astype(F32)
                for c in range(6):
                    cells[step, 1, part, 6 * c + 3 : 6 * c + 6, :] = rows[3 * c : 3 * c + 3]

    for step in range(2):
        near_own[step] = cells[step, here, 0].astype(BF16)
        near_x[step] = cells[step, 1 - here, 0].astype(BF16)
        lon_own[step] = cells[step, here, 1].astype(BF16)
        lon_x[step] = cells[step, 1 - here, 1].astype(BF16)


def main_kernel(
    near_own, near_x, lon_own, lon_x, vectors, wqkv, wout, wup, wdown_t,
    send_out, keep_out,
    x, qkv, probs, qm_all, emb, xh1, r1, hid_xh, r2, gp, act, normed_s, mixed_s, nm_s,
    cot_s, dpre_s, dproj_s, dqkv_s, dstate, small, msg,
):
    core = lax.axis_index("core")
    here = lax.axis_index("xh")
    last = jnp.logical_and(lax.axis_index("lat") == 7, jnp.logical_and(here == 1, core == 1))
    closed = jnp.where(last, 0.0, 1.0).astype(F32)
    for step in range(2):
        x[2 * here + step, 0:HALF, :] = near_own[step].astype(F32)
        x[2 * here + step, HALF:WIN, :] = lon_own[step].astype(F32)
        x[2 * (1 - here) + step, 0:HALF, :] = near_x[step].astype(F32)
        x[2 * (1 - here) + step, HALF:WIN, :] = lon_x[step].astype(F32)
    le = vectors[0:1, :]
    ga = vectors[1:2, :]
    gm = vectors[2:3, :]
    col_head = lax.broadcasted_iota(jnp.int32, (1, CH), 1) // HEAD_DIM
    masks = [(col_head == h).astype(F32) for h in range(HEADS)]
    row_half = lax.rem(lax.broadcasted_iota(jnp.int32, (WIN, WIN), 0), WIN_LAT) // 3
    key_half = lax.rem(lax.broadcasted_iota(jnp.int32, (WIN, WIN), 1), WIN_LAT) // 3
    allow1 = jnp.where(row_half == key_half, 1.0, closed).astype(F32)
    allow = jnp.concatenate([allow1] * HEADS, axis=1)

    def spread(v):
        return jnp.concatenate([v * m for m in masks], axis=0).astype(BF16)

    def gathered(v):
        total = v[0:WIN] * masks[0]
        for h in range(1, HEADS):
            total = total + v[WIN * h : WIN * h + WIN] * masks[h]
        return total

    for s in range(STEPS):
        rows = slice(WIN * s, WIN * s + WIN)
        land = x[s, :, 192:256][:, 0:1]
        e = x[s, :, 0:CH] + land * le
        emb[rows, :] = e
        off = e - mean_of(e)
        r = lax.rsqrt(mean_of(off * off) + EPS)
        xh = off * r
        xh1[rows, :] = xh
        r1[rows, :] = r
        normed_s[rows, :] = xh * ga
    normed = normed_s[...].astype(BF16)
    qkv[...] = nn(normed, wqkv[...]).astype(BF16).astype(F32)
    for s in range(STEPS):
        rows = slice(WIN * s, WIN * s + WIN)
        qm = spread(qkv[rows, 0:CH])
        qm_all[s] = qm
        keys = qkv[rows, CH : 2 * CH].astype(BF16)
        values = qkv[rows, 2 * CH : 3 * CH].astype(BF16)
        weights = jnp.exp(nt(keys, qm) * SCALE) * allow
        p = weights / jnp.sum(weights, axis=0, keepdims=True)
        probs[s] = p
        mixed_s[rows, :] = gathered(tn(p.astype(BF16), values))
    mixed = mixed_s[...].astype(BF16)
    projected = nn(mixed, wout[...]).astype(BF16).astype(F32)
    hid = emb[...] + projected
    off = hid - mean_of(hid)
    r = lax.rsqrt(mean_of(off * off) + EPS)
    xh = off * r
    hid_xh[...] = xh
    r2[...] = r
    nm_s[...] = (xh * gm).astype(BF16)
    for j in range(MLP // 256):
        cols = slice(256 * j, 256 * j + 256)
        pre = nn(nm_s[...], wup[:, cols])
        cdf = 0.5 * (1.0 + lax.erf(pre * (0.5 ** 0.5)))
        pdf = jnp.exp(pre * pre * -0.5) * 0.3989422804014327
        act[:, cols] = (pre * cdf).astype(BF16)
        gp[:, cols] = cdf + pre * pdf

    gain_m_sum = jnp.zeros((1, CH), F32)
    gain_a_sum = jnp.zeros((1, CH), F32)
    land_sum = jnp.zeros((1, CH), F32)
    incoming = None
    wq = wqkv[:, 0:CH]
    wk = wqkv[:, CH : 2 * CH]
    wv = wqkv[:, 2 * CH : 3 * CH]
    zero_rows = jnp.zeros((BLOCK - HALF, 128), F32)
    dstate[...] = jnp.zeros_like(dstate)
    for s in range(STEPS - 1, -1, -1):
        rows = slice(WIN * s, WIN * s + WIN)
        cot = x[s, :, 256:448]
        if incoming is not None:
            cot = cot + incoming
        cotb = cot.astype(BF16)
        cot_s[rows, :] = cotb.astype(F32)
        d_pre = gp[rows, :] * nn(cotb, wdown_t[...])
        dpre_b = d_pre.astype(BF16)
        dpre_s[rows, :] = dpre_b.astype(F32)
        dy = nt(dpre_b, wup[...])
        xh = hid_xh[rows, :]
        gain_m_sum = gain_m_sum + jnp.sum(dy * xh, axis=0, keepdims=True)
        dxh = dy * gm
        d_hid = cot + r2[rows, :] * (dxh - mean_of(dxh) - xh * mean_of(dxh * xh))
        dproj = d_hid.astype(BF16)
        dproj_s[rows, :] = dproj.astype(F32)
        d_mixed = nt(dproj, wout[...]).astype(BF16).astype(F32)
        dm = spread(d_mixed)
        keys = qkv[rows, CH : 2 * CH].astype(BF16)
        values = qkv[rows, 2 * CH : 3 * CH].astype(BF16)
        p = probs[s]
        dp = nt(values, dm)
        dv = nn(p.astype(BF16), dm).astype(BF16)
        ds = (p * (dp - jnp.sum(p * dp, axis=0, keepdims=True)) * SCALE).astype(BF16)
        dq = gathered(tn(ds, keys)).astype(BF16)
        dk = nn(ds, qm_all[s]).astype(BF16)
        dqkv_s[rows, 0:CH] = dq.astype(F32)
        dqkv_s[rows, CH : 2 * CH] = dk.astype(F32)
        dqkv_s[rows, 2 * CH : 3 * CH] = dv.astype(F32)
        d_rolled = nt(dq, wq) + nt(dk, wk) + nt(dv, wv)
        dy = d_rolled.astype(BF16).astype(F32)
        xh = xh1[rows, :]
        gain_a_sum = gain_a_sum + jnp.sum(dy * xh, axis=0, keepdims=True)
        dxh = dy * ga
        d_state = d_hid + r1[rows, :] * (dxh - mean_of(dxh) - xh * mean_of(dxh * xh))
        land = x[s, :, 192:256][:, 0:1]
        land_sum = land_sum + jnp.sum(d_state * land, axis=0, keepdims=True)
        incoming = d_state.astype(BF16).astype(F32)
        dstate[:, 0:CH] = incoming
        for half in range(2):
            piece = dstate[HALF * half : HALF * half + HALF, :]
            for tile in range(2):
                at = QUARTER * (s // 2) + BLOCK * (2 * half + tile)
                block = jnp.concatenate([piece[:, 128 * tile : 128 * tile + 128], zero_rows], axis=0)
                msg[s % 2, at : at + BLOCK, :] = block.astype(BF16)

    factor = float(STEPS * 192 * 96) ** (-0.5)

    def own_first(v):
        return jnp.where(core == 0, v, jnp.concatenate([v[:, HALF_CH:], v[:, :HALF_CH]], axis=1))

    def put(tile, value):
        value = (value * factor).astype(BF16)
        for j in range(value.shape[1] // 128):
            at = (tile + j) * HALF_CH
            piece = value[:, 128 * j : 128 * j + 128]
            keep_out[at : at + HALF_CH, :] = piece[:HALF_CH]
            send_out[at : at + HALF_CH, :] = piece[HALF_CH:]

    put(12, tn(own_first(cot_s[...]).astype(BF16), act[...]))
    put(6, tn(own_first(nm_s[...]), dpre_s[...].astype(BF16)))
    g_qkv = tn(own_first(normed_s[...]).astype(BF16), dqkv_s[...].astype(BF16))
    g_out = tn(own_first(mixed_s[...]).astype(BF16), dproj_s[...].astype(BF16))
    put(0, jnp.concatenate([g_qkv, g_out], axis=1))
    small[...] = jnp.zeros_like(small)
    for i, total in enumerate((land_sum, gain_a_sum, gain_m_sum)):
        total = total * factor
        small[2 * i : 2 * i + 1, :] = total[:, 0:128]
        small[2 * i + 1 : 2 * i + 2, 0:64] = total[:, 128:192]
    keep_out[TILED:SUMS, :] = jnp.where(core == 1, small[...], 0.0).astype(BF16)
    send_out[TILED:SUMS, :] = jnp.where(core == 1, 0.0, small[...]).astype(BF16)
    keep_out[SUMS:SENT, :] = msg[core]
    send_out[SUMS:SENT, :] = msg[1 - core]


def pair_kernel(kept, arrived, chunks, near_own, near_x, lon_own, lon_x):
    core = lax.axis_index("core")
    here = lax.axis_index("xh")
    for g in range(GROUP):
        at = UNIT * g
        total = kept[at : at + UNIT, :].astype(F32) + arrived[at : at + UNIT, :].astype(F32)
        chunks[g] = total.astype(BF16)
    for half, near, lon in ((here, near_own, lon_own), (1 - here, near_x, lon_x)):
        first = pl.ds(pl.multiple_of(SUMS + QUARTER * half, 64), COLUMNS)
        second = pl.ds(pl.multiple_of(SUMS + QUARTER * half + COLUMNS, 32), COLUMNS)
        near[core] = kept[first, :]
        near[1 - core] = arrived[first, :]
        lon[core] = kept[second, :]
        lon[1 - core] = arrived[second, :]


def group_kernel(terms, total_out):
    total = terms[0].astype(F32)
    for g in range(1, GROUP):
        total = total + terms[g].astype(F32)
    total = total.astype(BF16)
    for g in range(8):
        total_out[g] = total


def column_kernel(terms, near_own, near_x, lon_own, lon_x, total_out, near, lon, to_lat):
    here = lax.axis_index("xh")
    for c in range(2):
        near[2 * here + c] = near_own[c]
        near[2 * (1 - here) + c] = near_x[c]
        lon[2 * here + c] = lon_own[c]
        lon[2 * (1 - here) + c] = lon_x[c]
    to_lat[0] = near[3]
    to_lat[1] = lon[3]
    total = terms[0].astype(F32)
    for g in range(1, 8):
        total = total + terms[g].astype(F32)
    total = total.astype(BF16)
    for g in range(GROUP):
        total_out[g] = total


def unpack_kernel(own, other, g_qkv, g_out, g_up, g_down, g_land, g_ga, g_gm):
    core = lax.axis_index("core")
    for rows, half in ((core, own), (1 - core, other)):
        to = pl.ds(pl.multiple_of(HALF_CH * rows, 32), HALF_CH)

        def tile(t):
            return half[HALF_CH * t : HALF_CH * t + HALF_CH, :].astype(F32)

        for j in range(4):
            g_qkv[to, 128 * j : 128 * j + 128] = tile(j)
        mid = tile(4)
        g_qkv[to, 512:576] = mid[:, 0:64]
        g_out[to, :] = jnp.concatenate([mid[:, 64:128], tile(5)], axis=1)
        for j in range(6):
            g_up[to, 128 * j : 128 * j + 128] = tile(6 + j)
            g_down[to, 128 * j : 128 * j + 128] = tile(12 + j)
    little = jnp.where(
        core == 1, own[TILED : TILED + 16, :].astype(F32), other[TILED : TILED + 16, :].astype(F32)
    )
    for i, out in enumerate((g_land, g_ga, g_gm)):
        out[...] = jnp.concatenate(
            [little[2 * i : 2 * i + 1, :], little[2 * i + 1 : 2 * i + 2, 0:64]], axis=1
        )


def state_kernel(near, lon, edges, state_out):
    for part, first, wide in ((0, 6, near), (1, 0, lon)):
        for tile, lanes in ((0, slice(0, 128)), (1, slice(128, 192))):
            n = lanes.stop - lanes.start
            at = slice(BLOCK * tile, BLOCK * tile + BLOCK)
            before = edges[part, at, :].astype(F32)
            for c in range(6):
                state_out[first + c, 0:3, lanes] = before[6 * c + 3 : 6 * c + 6, 0:n]
            for k in range(4):
                block = wide[k, at, :].astype(F32)
                tall = 6 if k < 3 else 3
                for c in range(6):
                    state_out[first + c, 6 * k + 3 : 6 * k + 3 + tall, lanes] = block[
                        6 * c : 6 * c + tall, 0:n
                    ]


def hop(value, rows, cols, xh=0, cores=((0, 0), (1, 1))):
    pairs = []
    for h in range(2):
        for source, target in cores:
            for a in range(8):
                for b in range(8):
                    k = 2 * ((h + xh) % 2) + target
                    to = (k * 8 + (a + rows) % 8) * 8 + (b + cols) % 8
                    pairs.append((((2 * h + source) * 8 + a) * 8 + b, to))
    return lax.ppermute(value, AXES, pairs)


def swap(value, axis):
    return lax.ppermute(value, axis, [(0, 1), (1, 0)])


def exchange(value, axis):
    return lax.all_to_all(value, axis, 0, 0, tiled=True)


def call(kernel, name, outs, scratch=(), mib=8, from_hbm=0):
    specs = {}
    if from_hbm:
        specs["in_specs"] = [pl.BlockSpec(memory_space=pltpu.HBM)] * from_hbm
    return pl.pallas_call(
        kernel,
        out_shape=tuple(jax.ShapeDtypeStruct(dims, kind) for dims, kind in outs),
        scratch_shapes=[pltpu.VMEM(dims, kind) if kind else dims for dims, kind in scratch],
        compiler_params=pltpu.CompilerParams(vmem_limit_bytes=mib * MIB),
        name=name,
        **specs,
    )


def local(
    states, loss_grads, land_sea, land_embed, gain_attn, gain_mlp, w_qkv, w_out, w_up, w_down
):
    keep, send, edge, vectors, w_qkv = call(
        pack_kernel,
        "pack_cells",
        [((2, 2, HALF, MSG), BF16)] * 2 + [((2, HALF // 2, MSG), BF16), ((8, CH), F32)]
        + [((CH, 3 * CH), BF16)],
        [
            ((WIN_LON, ROWS, CH), BF16),
            ((WIN_LON, ROWS, CH), BF16),
            ((WIN_LON, ROWS), jnp.int32),
            ((8, CH), F32),
            ((2, 2, 2, HALF, MSG), F32),
            ((2, HALF // 2, MSG), F32),
            (pltpu.SemaphoreType.DMA((7,)), None),
        ],
        from_hbm=7,
    )(
        *(
            pltpu.with_memory_space_constraint(value, pltpu.HBM)
            for value in (
                states[0, 0].transpose(1, 0, 2), loss_grads[0, 0].transpose(1, 0, 2), land_sea.T,
                land_embed[None], gain_attn[None], gain_mlp[None], w_qkv,
            )
        )
    )
    near_own, near_x, lon_own, lon_x = call(
        sort_kernel,
        "sort_windows",
        [((2, HALF, MSG), BF16)] * 4,
        [((2, 2, 2, HALF, MSG), F32)],
    )(
        keep, swap(send, "core"),
        hop(edge, -1, 0, cores=((0, 1),)), hop(edge, -1, 0, cores=((1, 1),)),
    )
    near_x = hop(near_x, 0, 0, 1)
    lon_own = hop(lon_own, 0, -1)
    lon_x = hop(lon_x, 0, -1, 1)
    send, keep = call(
        main_kernel,
        "window_steps",
        [((SENT, 128), BF16)] * 2,
        [
            ((STEPS, WIN, MSG), F32),
            ((TOK, 3 * CH), F32),
            ((STEPS, WIN, HEADS * WIN), F32),
            ((STEPS, HEADS * WIN, CH), BF16),
            ((TOK, CH), F32),
            ((TOK, CH), F32),
            ((TOK, 1), F32),
            ((TOK, CH), F32),
            ((TOK, 1), F32),
            ((TOK, MLP), F32),
            ((TOK, MLP), BF16),
            ((TOK, CH), F32),
            ((TOK, CH), F32),
            ((TOK, CH), BF16),
            ((TOK, CH), F32),
            ((TOK, MLP), F32),
            ((TOK, CH), F32),
            ((TOK, 3 * CH), F32),
            ((WIN, 256), F32),
            ((SUMS - TILED, 128), F32),
            ((2, 2 * QUARTER, 128), BF16),
        ],
        mib=24,
    )(
        near_own, near_x, lon_own, lon_x, vectors, w_qkv, w_out, w_up, w_down.T
    )

    chunks, near_own, near_x, lon_own, lon_x = call(
        pair_kernel,
        "sum_cores",
        [((GROUP, UNIT, 128), BF16)] + [((2, COLUMNS, 128), BF16)] * 4,
    )(keep, swap(send, "core"))
    near_x = hop(near_x, 0, 0, 1)
    lon_own = hop(lon_own, 0, 1)
    lon_x = hop(lon_x, 0, 1, 1)
    (partial,) = call(group_kernel, "sum_group", [((8, UNIT, 128), BF16)])(
        exchange(chunks, ("xh", "lon"))
    )
    total, near, lon, to_lat = call(
        column_kernel,
        "sum_column",
        [((GROUP, UNIT, 128), BF16)]
        + [((4, COLUMNS, 128), BF16)] * 2
        + [((2, COLUMNS, 128), BF16)],
    )(exchange(partial, "lat"), near_own, near_x, lon_own, lon_x)
    own, edges = lax.optimization_barrier((exchange(total, ("xh", "lon")), hop(to_lat, 1, 0)))
    own = own.reshape(SUMS, 128)
    (state_grads,) = call(state_kernel, "unpack_states", [((WIN_LON, ROWS, CH), F32)])(
        near, lon, edges
    )
    outs = call(
        unpack_kernel,
        "unpack_sums",
        [
            ((CH, 3 * CH), F32),
            ((CH, CH), F32),
            ((CH, MLP), F32),
            ((CH, MLP), F32),
            ((1, CH), F32),
            ((1, CH), F32),
            ((1, CH), F32),
        ],
        mib=16,
    )(own, swap(own, "core"))
    return (
        state_grads.transpose(1, 0, 2)[None, None],
        outs[0], outs[1], outs[2], outs[3].T, outs[4][0], outs[5][0], outs[6][0],
    )


def solution(mesh):
    halves = Mesh(mesh.devices.reshape(2, 2, *mesh.devices.shape[1:]), AXES)
    cell = P(("xh", "core"), None, "lat", "lon", None)
    return jax.shard_map(
        local,
        mesh=halves,
        in_specs=(cell, cell, P("lat", "lon"), P(), P(), P(), P(), P(), P(), P()),
        out_specs=(cell, P(), P(), P(), P(), P(), P(), P()),
        check_vma=False,
    )
```

```python
import jax
import jax.numpy as jnp
from jax import lax
from jax.experimental import pallas as pl
from jax.experimental.pallas import tpu as pltpu
from jax.sharding import Mesh
from jax.sharding import PartitionSpec as P

CH = 192
HEADS = 6
HEAD_DIM = 32
MLP = 768
ROWS = 24
WIN_LAT = 6
WIN_LON = 12
WIN = WIN_LAT * WIN_LON
HALF = WIN // 2
STEPS = 4
TOK = STEPS * WIN
MSG = 384
TALL = 40
GROUP = 16
UNIT = 112
SUMS = GROUP * UNIT
BLOCK = 48
QUARTER = 4 * BLOCK
COLUMNS = QUARTER // 2
SENT = SUMS + 2 * QUARTER
HALF_CH = CH // 2
TILED = 18 * HALF_CH
SCALE = HEAD_DIM ** (-0.5)
EPS = 1e-05
F32 = jnp.float32
BF16 = jnp.bfloat16
AXES = ("xh", "core", "lat", "lon")
MIB = 1024 * 1024


def nn(a, b):
    return lax.dot_general(a, b, (((1,), (0,)), ((), ())), preferred_element_type=F32)


def nt(a, b):
    return lax.dot_general(a, b, (((1,), (1,)), ((), ())), preferred_element_type=F32)


def tn(a, b):
    return lax.dot_general(a, b, (((0,), (0,)), ((), ())), preferred_element_type=F32)


def mean_of(v):
    return jnp.sum(v, axis=-1, keepdims=True) * (1.0 / CH)


def pack_kernel(
    states_in, loss_in, land_in, embed_in, gain_a_in, gain_m_in, wqkv_in,
    keep_out, send_out, edge_out, vectors_out, wqkv_out,
    states, loss, land, vectors, cells, edges, sems,
):
    pairs = (
        (states_in, states), (loss_in, loss), (land_in, land),
        (embed_in, vectors.at[0:1]), (gain_a_in, vectors.at[1:2]), (gain_m_in, vectors.at[2:3]),
    )
    copies = [
        pltpu.make_async_copy(source, target, sems.at[i])
        for i, (source, target) in enumerate(pairs)
    ]
    weights = pltpu.make_async_copy(wqkv_in, wqkv_out, sems.at[6])
    for copy in copies:
        copy.start()
    weights.start()
    for copy in copies:
        copy.wait()
    core = lax.axis_index("core")
    nothing = jnp.zeros((3, MSG), F32)
    cells[:, :, :, HALF:TALL, :] = jnp.zeros((2, 2, 2, TALL - HALF, MSG), F32)
    edges[:, HALF // 2 : 24, :] = jnp.zeros((2, 24 - HALF // 2, MSG), F32)
    for c in range(WIN_LON):
        cell = jnp.concatenate([states[c].astype(F32), loss[c].astype(F32)], axis=1)
        part, at = (1, 6 * c) if c < 6 else (0, 6 * (c - 6))
        for k in range(3):
            cells[k % 2, k // 2, part, at : at + 6, :] = cell[6 * k + 3 : 6 * k + 9]
        cells[1, 1, part, at : at + 3, :] = cell[21:24]
        cells[1, 1, part, at + 3 : at + 6, :] = nothing
        edges[part, at // 2 : at // 2 + 3, :] = cell[0:3]
    lanes = lax.broadcasted_iota(jnp.int32, (ROWS, 640), 1)
    row = lax.broadcasted_iota(jnp.int32, (ROWS, 640), 0)
    window = lanes // 128
    inner = lax.rem(lax.rem(lanes, 128), WIN_LAT)
    wanted = jnp.where(window == 4, inner - 3, 6 * window + 3 + inner)
    picked = nn(land[...].astype(BF16), (row == wanted).astype(BF16))
    token = lax.rem(lax.broadcasted_iota(jnp.int32, (6, 640), 1), 128)
    column = lax.broadcasted_iota(jnp.int32, (6, 640), 0)
    here = (token // WIN_LAT == column).astype(F32)
    for part in range(2):
        first = 6 - 6 * part
        line = jnp.sum(picked[first : first + 6] * here, axis=0, keepdims=True)
        for k in range(4):
            cells[k % 2, k // 2, part, HALF : HALF + 1, 0:128] = line[:, 128 * k : 128 * k + 128]
        edges[part, HALF // 2 : HALF // 2 + 1, 0:128] = line[:, 512:640]
    keep_out[...] = cells[core].astype(BF16)
    send_out[...] = cells[1 - core].astype(BF16)
    edge_out[...] = edges[...].astype(BF16)
    vectors_out[...] = vectors[...]
    weights.wait()


def sort_kernel(kept, arrived, edge0, edge1, near_own, near_x, lon_own, lon_x, cells):
    core = lax.axis_index("core")
    here = lax.axis_index("xh")
    cells[core] = kept[...].astype(F32)
    cells[1 - core] = arrived[...].astype(F32)

    @pl.when(core == 1)
    def _():
        for step, edge in enumerate((edge0, edge1)):
            for part in range(2):
                rows = edge[part].astype(F32)
                for c in range(6):
                    cells[step, 1, part, 6 * c + 3 : 6 * c + 6, :] = rows[3 * c : 3 * c + 3]
                line = rows[HALF // 2 : HALF // 2 + 1]
                cells[step, 1, part, HALF : HALF + 1, :] = (
                    cells[step, 1, part, HALF : HALF + 1, :] + line
                )

    for step in range(2):
        near_own[step] = cells[step, here, 0].astype(BF16)
        near_x[step] = cells[step, 1 - here, 0].astype(BF16)
        lon_own[step] = cells[step, here, 1].astype(BF16)
        lon_x[step] = cells[step, 1 - here, 1].astype(BF16)


def main_kernel(
    near_own, near_x, lon_own, lon_x, vectors, wqkv, wout, wup, wdown_t,
    send_out, keep_out,
    x, land_s, qkv, probs, qm_all, emb, xh1, r1, hid_xh, r2, gp, act, normed_s, mixed_s, nm_s,
    cot_s, dpre_s, dproj_s, dqkv_s, dstate, small, msg,
):
    core = lax.axis_index("core")
    here = lax.axis_index("xh")
    last = jnp.logical_and(lax.axis_index("lat") == 7, jnp.logical_and(here == 1, core == 1))
    closed = jnp.where(last, 0.0, 1.0).astype(F32)
    for step in range(2):
        x[2 * here + step, 0:HALF, :] = near_own[step].astype(F32)[0:HALF]
        x[2 * here + step, HALF:WIN, :] = lon_own[step].astype(F32)[0:HALF]
        x[2 * (1 - here) + step, 0:HALF, :] = near_x[step].astype(F32)[0:HALF]
        x[2 * (1 - here) + step, HALF:WIN, :] = lon_x[step].astype(F32)[0:HALF]
    for part, cells in ((0, near_own), (1, lon_own)):
        line = cells[0].astype(F32)[HALF : HALF + 1, 0:128]
        column = jnp.broadcast_to(line, (8, 128)).T
        land_s[HALF * part : HALF * part + HALF, :] = column[0:HALF, 0:1]
    le = vectors[0:1, :]
    ga = vectors[1:2, :]
    gm = vectors[2:3, :]
    col_head = lax.broadcasted_iota(jnp.int32, (1, CH), 1) // HEAD_DIM
    masks = [(col_head == h).astype(F32) for h in range(HEADS)]
    row_half = lax.rem(lax.broadcasted_iota(jnp.int32, (WIN, WIN), 0), WIN_LAT) // 3
    key_half = lax.rem(lax.broadcasted_iota(jnp.int32, (WIN, WIN), 1), WIN_LAT) // 3
    allow1 = jnp.where(row_half == key_half, 1.0, closed).astype(F32)
    allow = jnp.concatenate([allow1] * HEADS, axis=1)

    def spread(v):
        return jnp.concatenate([v * m for m in masks], axis=0).astype(BF16)

    def gathered(v):
        total = v[0:WIN] * masks[0]
        for h in range(1, HEADS):
            total = total + v[WIN * h : WIN * h + WIN] * masks[h]
        return total

    for s in range(STEPS):
        rows = slice(WIN * s, WIN * s + WIN)
        land = land_s[...]
        e = x[s, :, 0:CH] + land * le
        emb[rows, :] = e
        off = e - mean_of(e)
        r = lax.rsqrt(mean_of(off * off) + EPS)
        xh = off * r
        xh1[rows, :] = xh
        r1[rows, :] = r
        normed_s[rows, :] = xh * ga
    normed = normed_s[...].astype(BF16)
    qkv[...] = nn(normed, wqkv[...]).astype(BF16).astype(F32)
    for s in range(STEPS):
        rows = slice(WIN * s, WIN * s + WIN)
        qm = spread(qkv[rows, 0:CH])
        qm_all[s] = qm
        keys = qkv[rows, CH : 2 * CH].astype(BF16)
        values = qkv[rows, 2 * CH : 3 * CH].astype(BF16)
        weights = jnp.exp(nt(keys, qm) * SCALE) * allow
        p = weights / jnp.sum(weights, axis=0, keepdims=True)
        probs[s] = p
        mixed_s[rows, :] = gathered(tn(p.astype(BF16), values))
    mixed = mixed_s[...].astype(BF16)
    projected = nn(mixed, wout[...]).astype(BF16).astype(F32)
    hid = emb[...] + projected
    off = hid - mean_of(hid)
    r = lax.rsqrt(mean_of(off * off) + EPS)
    xh = off * r
    hid_xh[...] = xh
    r2[...] = r
    nm_s[...] = (xh * gm).astype(BF16)
    for j in range(MLP // 256):
        cols = slice(256 * j, 256 * j + 256)
        pre = nn(nm_s[...], wup[:, cols])
        cdf = 0.5 * (1.0 + lax.erf(pre * (0.5 ** 0.5)))
        pdf = jnp.exp(pre * pre * -0.5) * 0.3989422804014327
        act[:, cols] = (pre * cdf).astype(BF16)
        gp[:, cols] = cdf + pre * pdf

    gain_m_sum = jnp.zeros((1, CH), F32)
    gain_a_sum = jnp.zeros((1, CH), F32)
    land_sum = jnp.zeros((1, CH), F32)
    incoming = None
    wq = wqkv[:, 0:CH]
    wk = wqkv[:, CH : 2 * CH]
    wv = wqkv[:, 2 * CH : 3 * CH]
    zero_rows = jnp.zeros((BLOCK - HALF, 128), F32)
    dstate[...] = jnp.zeros_like(dstate)
    for s in range(STEPS - 1, -1, -1):
        rows = slice(WIN * s, WIN * s + WIN)
        cot = x[s, :, CH:MSG]
        if incoming is not None:
            cot = cot + incoming
        cotb = cot.astype(BF16)
        cot_s[rows, :] = cotb.astype(F32)
        d_pre = gp[rows, :] * nn(cotb, wdown_t[...])
        dpre_b = d_pre.astype(BF16)
        dpre_s[rows, :] = dpre_b.astype(F32)
        dy = nt(dpre_b, wup[...])
        xh = hid_xh[rows, :]
        gain_m_sum = gain_m_sum + jnp.sum(dy * xh, axis=0, keepdims=True)
        dxh = dy * gm
        d_hid = cot + r2[rows, :] * (dxh - mean_of(dxh) - xh * mean_of(dxh * xh))
        dproj = d_hid.astype(BF16)
        dproj_s[rows, :] = dproj.astype(F32)
        d_mixed = nt(dproj, wout[...]).astype(BF16).astype(F32)
        dm = spread(d_mixed)
        keys = qkv[rows, CH : 2 * CH].astype(BF16)
        values = qkv[rows, 2 * CH : 3 * CH].astype(BF16)
        p = probs[s]
        dp = nt(values, dm)
        dv = nn(p.astype(BF16), dm).astype(BF16)
        ds = (p * (dp - jnp.sum(p * dp, axis=0, keepdims=True)) * SCALE).astype(BF16)
        dq = gathered(tn(ds, keys)).astype(BF16)
        dk = nn(ds, qm_all[s]).astype(BF16)
        dqkv_s[rows, 0:CH] = dq.astype(F32)
        dqkv_s[rows, CH : 2 * CH] = dk.astype(F32)
        dqkv_s[rows, 2 * CH : 3 * CH] = dv.astype(F32)
        d_rolled = nt(dq, wq) + nt(dk, wk) + nt(dv, wv)
        dy = d_rolled.astype(BF16).astype(F32)
        xh = xh1[rows, :]
        gain_a_sum = gain_a_sum + jnp.sum(dy * xh, axis=0, keepdims=True)
        dxh = dy * ga
        d_state = d_hid + r1[rows, :] * (dxh - mean_of(dxh) - xh * mean_of(dxh * xh))
        land = land_s[...]
        land_sum = land_sum + jnp.sum(d_state * land, axis=0, keepdims=True)
        incoming = d_state.astype(BF16).astype(F32)
        dstate[:, 0:CH] = incoming
        for half in range(2):
            piece = dstate[HALF * half : HALF * half + HALF, :]
            for tile in range(2):
                at = QUARTER * (s // 2) + BLOCK * (2 * half + tile)
                block = jnp.concatenate([piece[:, 128 * tile : 128 * tile + 128], zero_rows], axis=0)
                msg[s % 2, at : at + BLOCK, :] = block.astype(BF16)

    factor = float(STEPS * 192 * 96) ** (-0.5)

    def own_first(v):
        return jnp.where(core == 0, v, jnp.concatenate([v[:, HALF_CH:], v[:, :HALF_CH]], axis=1))

    def put(tile, value):
        value = (value * factor).astype(BF16)
        for j in range(value.shape[1] // 128):
            at = (tile + j) * HALF_CH
            piece = value[:, 128 * j : 128 * j + 128]
            keep_out[at : at + HALF_CH, :] = piece[:HALF_CH]
            send_out[at : at + HALF_CH, :] = piece[HALF_CH:]

    put(12, tn(own_first(cot_s[...]).astype(BF16), act[...]))
    put(6, tn(own_first(nm_s[...]), dpre_s[...].astype(BF16)))
    g_qkv = tn(own_first(normed_s[...]).astype(BF16), dqkv_s[...].astype(BF16))
    g_out = tn(own_first(mixed_s[...]).astype(BF16), dproj_s[...].astype(BF16))
    put(0, jnp.concatenate([g_qkv, g_out], axis=1))
    small[...] = jnp.zeros_like(small)
    for i, total in enumerate((land_sum, gain_a_sum, gain_m_sum)):
        total = total * factor
        small[2 * i : 2 * i + 1, :] = total[:, 0:128]
        small[2 * i + 1 : 2 * i + 2, 0:64] = total[:, 128:192]
    keep_out[TILED:SUMS, :] = jnp.where(core == 1, small[...], 0.0).astype(BF16)
    send_out[TILED:SUMS, :] = jnp.where(core == 1, 0.0, small[...]).astype(BF16)
    keep_out[SUMS:SENT, :] = msg[core]
    send_out[SUMS:SENT, :] = msg[1 - core]


def pair_kernel(kept, arrived, chunks, near_own, near_x, lon_own, lon_x):
    core = lax.axis_index("core")
    here = lax.axis_index("xh")
    for g in range(GROUP):
        at = UNIT * g
        total = kept[at : at + UNIT, :].astype(F32) + arrived[at : at + UNIT, :].astype(F32)
        chunks[g] = total.astype(BF16)
    for half, near, lon in ((here, near_own, lon_own), (1 - here, near_x, lon_x)):
        first = pl.ds(pl.multiple_of(SUMS + QUARTER * half, 64), COLUMNS)
        second = pl.ds(pl.multiple_of(SUMS + QUARTER * half + COLUMNS, 32), COLUMNS)
        near[core] = kept[first, :]
        near[1 - core] = arrived[first, :]
        lon[core] = kept[second, :]
        lon[1 - core] = arrived[second, :]


def group_kernel(terms, total_out):
    total = terms[0].astype(F32)
    for g in range(1, GROUP):
        total = total + terms[g].astype(F32)
    total = total.astype(BF16)
    for g in range(8):
        total_out[g] = total


def column_kernel(terms, near_own, near_x, lon_own, lon_x, total_out, near, lon, to_lat):
    here = lax.axis_index("xh")
    for c in range(2):
        near[2 * here + c] = near_own[c]
        near[2 * (1 - here) + c] = near_x[c]
        lon[2 * here + c] = lon_own[c]
        lon[2 * (1 - here) + c] = lon_x[c]
    to_lat[0] = near[3]
    to_lat[1] = lon[3]
    total = terms[0].astype(F32)
    for g in range(1, 8):
        total = total + terms[g].astype(F32)
    total = total.astype(BF16)
    for g in range(GROUP):
        total_out[g] = total


def unpack_kernel(own, other, g_qkv, g_out, g_up, g_down, g_land, g_ga, g_gm):
    core = lax.axis_index("core")
    for rows, half in ((core, own), (1 - core, other)):
        to = pl.ds(pl.multiple_of(HALF_CH * rows, 32), HALF_CH)

        def tile(t):
            return half[HALF_CH * t : HALF_CH * t + HALF_CH, :].astype(F32)

        for j in range(4):
            g_qkv[to, 128 * j : 128 * j + 128] = tile(j)
        mid = tile(4)
        g_qkv[to, 512:576] = mid[:, 0:64]
        g_out[to, :] = jnp.concatenate([mid[:, 64:128], tile(5)], axis=1)
        for j in range(6):
            g_up[to, 128 * j : 128 * j + 128] = tile(6 + j)
            g_down[to, 128 * j : 128 * j + 128] = tile(12 + j)
    little = jnp.where(
        core == 1, own[TILED : TILED + 16, :].astype(F32), other[TILED : TILED + 16, :].astype(F32)
    )
    for i, out in enumerate((g_land, g_ga, g_gm)):
        out[...] = jnp.concatenate(
            [little[2 * i : 2 * i + 1, :], little[2 * i + 1 : 2 * i + 2, 0:64]], axis=1
        )


def state_kernel(near, lon, edges, state_out):
    for part, first, wide in ((0, 6, near), (1, 0, lon)):
        for tile, lanes in ((0, slice(0, 128)), (1, slice(128, 192))):
            n = lanes.stop - lanes.start
            at = slice(BLOCK * tile, BLOCK * tile + BLOCK)
            before = edges[part, at, :].astype(F32)
            for c in range(6):
                state_out[first + c, 0:3, lanes] = before[6 * c + 3 : 6 * c + 6, 0:n]
            for k in range(4):
                block = wide[k, at, :].astype(F32)
                tall = 6 if k < 3 else 3
                for c in range(6):
                    state_out[first + c, 6 * k + 3 : 6 * k + 3 + tall, lanes] = block[
                        6 * c : 6 * c + tall, 0:n
                    ]


def hop(value, rows, cols, xh=0, cores=((0, 0), (1, 1))):
    pairs = []
    for h in range(2):
        for source, target in cores:
            for a in range(8):
                for b in range(8):
                    k = 2 * ((h + xh) % 2) + target
                    to = (k * 8 + (a + rows) % 8) * 8 + (b + cols) % 8
                    pairs.append((((2 * h + source) * 8 + a) * 8 + b, to))
    return lax.ppermute(value, AXES, pairs)


def swap(value, axis):
    return lax.ppermute(value, axis, [(0, 1), (1, 0)])


def exchange(value, axis):
    return lax.all_to_all(value, axis, 0, 0, tiled=True)


def call(kernel, name, outs, scratch=(), mib=8, from_hbm=0):
    specs = {}
    if from_hbm:
        specs["in_specs"] = [pl.BlockSpec(memory_space=pltpu.HBM)] * from_hbm
    return pl.pallas_call(
        kernel,
        out_shape=tuple(jax.ShapeDtypeStruct(dims, kind) for dims, kind in outs),
        scratch_shapes=[pltpu.VMEM(dims, kind) if kind else dims for dims, kind in scratch],
        compiler_params=pltpu.CompilerParams(vmem_limit_bytes=mib * MIB),
        name=name,
        **specs,
    )


def local(
    states, loss_grads, land_sea, land_embed, gain_attn, gain_mlp, w_qkv, w_out, w_up, w_down
):
    keep, send, edge, vectors, w_qkv = call(
        pack_kernel,
        "pack_cells",
        [((2, 2, TALL, MSG), BF16)] * 2 + [((2, 24, MSG), BF16), ((8, CH), F32)]
        + [((CH, 3 * CH), BF16)],
        [
            ((WIN_LON, ROWS, CH), BF16),
            ((WIN_LON, ROWS, CH), BF16),
            ((WIN_LON, ROWS), jnp.int32),
            ((8, CH), F32),
            ((2, 2, 2, TALL, MSG), F32),
            ((2, 24, MSG), F32),
            (pltpu.SemaphoreType.DMA((7,)), None),
        ],
        from_hbm=7,
    )(
        *(
            pltpu.with_memory_space_constraint(value, pltpu.HBM)
            for value in (
                states[0, 0].transpose(1, 0, 2), loss_grads[0, 0].transpose(1, 0, 2), land_sea.T,
                land_embed[None], gain_attn[None], gain_mlp[None], w_qkv,
            )
        )
    )
    near_own, near_x, lon_own, lon_x = call(
        sort_kernel,
        "sort_windows",
        [((2, TALL, MSG), BF16)] * 4,
        [((2, 2, 2, TALL, MSG), F32)],
    )(
        keep, swap(send, "core"),
        hop(edge, -1, 0, cores=((0, 1),)), hop(edge, -1, 0, cores=((1, 1),)),
    )
    near_x = hop(near_x, 0, 0, 1)
    lon_own = hop(lon_own, 0, -1)
    lon_x = hop(lon_x, 0, -1, 1)
    send, keep = call(
        main_kernel,
        "window_steps",
        [((SENT, 128), BF16)] * 2,
        [
            ((STEPS, WIN, MSG), F32),
            ((WIN, 1), F32),
            ((TOK, 3 * CH), F32),
            ((STEPS, WIN, HEADS * WIN), F32),
            ((STEPS, HEADS * WIN, CH), BF16),
            ((TOK, CH), F32),
            ((TOK, CH), F32),
            ((TOK, 1), F32),
            ((TOK, CH), F32),
            ((TOK, 1), F32),
            ((TOK, MLP), F32),
            ((TOK, MLP), BF16),
            ((TOK, CH), F32),
            ((TOK, CH), F32),
            ((TOK, CH), BF16),
            ((TOK, CH), F32),
            ((TOK, MLP), F32),
            ((TOK, CH), F32),
            ((TOK, 3 * CH), F32),
            ((WIN, 256), F32),
            ((SUMS - TILED, 128), F32),
            ((2, 2 * QUARTER, 128), BF16),
        ],
        mib=24,
    )(
        near_own, near_x, lon_own, lon_x, vectors, w_qkv, w_out, w_up, w_down.T
    )

    chunks, near_own, near_x, lon_own, lon_x = call(
        pair_kernel,
        "sum_cores",
        [((GROUP, UNIT, 128), BF16)] + [((2, COLUMNS, 128), BF16)] * 4,
    )(keep, swap(send, "core"))
    near_x = hop(near_x, 0, 0, 1)
    lon_own = hop(lon_own, 0, 1)
    lon_x = hop(lon_x, 0, 1, 1)
    (partial,) = call(group_kernel, "sum_group", [((8, UNIT, 128), BF16)])(
        exchange(chunks, ("xh", "lon"))
    )
    total, near, lon, to_lat = call(
        column_kernel,
        "sum_column",
        [((GROUP, UNIT, 128), BF16)]
        + [((4, COLUMNS, 128), BF16)] * 2
        + [((2, COLUMNS, 128), BF16)],
    )(exchange(partial, "lat"), near_own, near_x, lon_own, lon_x)
    own, edges = lax.optimization_barrier((exchange(total, ("xh", "lon")), hop(to_lat, 1, 0)))
    own = own.reshape(SUMS, 128)
    (state_grads,) = call(state_kernel, "unpack_states", [((WIN_LON, ROWS, CH), F32)])(
        near, lon, edges
    )
    outs = call(
        unpack_kernel,
        "unpack_sums",
        [
            ((CH, 3 * CH), F32),
            ((CH, CH), F32),
            ((CH, MLP), F32),
            ((CH, MLP), F32),
            ((1, CH), F32),
            ((1, CH), F32),
            ((1, CH), F32),
        ],
        mib=16,
    )(own, swap(own, "core"))
    return (
        state_grads.transpose(1, 0, 2)[None, None],
        outs[0], outs[1], outs[2], outs[3].T, outs[4][0], outs[5][0], outs[6][0],
    )


def solution(mesh):
    halves = Mesh(mesh.devices.reshape(2, 2, *mesh.devices.shape[1:]), AXES)
    cell = P(("xh", "core"), None, "lat", "lon", None)
    return jax.shard_map(
        local,
        mesh=halves,
        in_specs=(cell, cell, P("lat", "lon"), P(), P(), P(), P(), P(), P(), P()),
        out_specs=(cell, P(), P(), P(), P(), P(), P(), P()),
        check_vma=False,
    )
```

```python
import jax
import jax.numpy as jnp
from jax import lax
from jax.experimental import pallas as pl
from jax.experimental.pallas import tpu as pltpu
from jax.sharding import Mesh
from jax.sharding import PartitionSpec as P

CH = 192
HEADS = 6
HEAD_DIM = 32
MLP = 768
ROWS = 24
WIN_LAT = 6
WIN_LON = 12
WIN = WIN_LAT * WIN_LON
HALF = WIN // 2
STEPS = 4
TOK = STEPS * WIN
MSG = 384
TALL = 40
GROUP = 16
UNIT = 112
SUMS = GROUP * UNIT
BLOCK = 48
QUARTER = 4 * BLOCK
COLUMNS = QUARTER // 2
SENT = SUMS + 2 * QUARTER
HALF_CH = CH // 2
TILED = 18 * HALF_CH
SCALE = HEAD_DIM ** (-0.5)
EPS = 1e-05
F32 = jnp.float32
BF16 = jnp.bfloat16
AXES = ("xh", "core", "lat", "lon")
MIB = 1024 * 1024


def nn(a, b):
    return lax.dot_general(a, b, (((1,), (0,)), ((), ())), preferred_element_type=F32)


def nt(a, b):
    return lax.dot_general(a, b, (((1,), (1,)), ((), ())), preferred_element_type=F32)


def tn(a, b):
    return lax.dot_general(a, b, (((0,), (0,)), ((), ())), preferred_element_type=F32)


def mean_of(v):
    return jnp.sum(v, axis=-1, keepdims=True) * (1.0 / CH)


def pack_kernel(
    states_in, loss_in, land_in, embed_in, gain_a_in, gain_m_in, wqkv_in,
    keep_out, send_out, edge_out, vectors_out, wqkv_out,
    states, loss, land, vectors, cells, edges, sems,
):
    pairs = (
        (states_in, states), (loss_in, loss), (land_in, land),
        (embed_in, vectors.at[0:1]), (gain_a_in, vectors.at[1:2]), (gain_m_in, vectors.at[2:3]),
    )
    copies = [
        pltpu.make_async_copy(source, target, sems.at[i])
        for i, (source, target) in enumerate(pairs)
    ]
    weights = pltpu.make_async_copy(wqkv_in, wqkv_out, sems.at[6])
    for copy in copies:
        copy.start()
    weights.start()
    for copy in copies:
        copy.wait()
    core = lax.axis_index("core")
    nothing = jnp.zeros((3, MSG), F32)
    cells[:, :, :, HALF:TALL, :] = jnp.zeros((2, 2, 2, TALL - HALF, MSG), F32)
    edges[:, HALF // 2 : 24, :] = jnp.zeros((2, 24 - HALF // 2, MSG), F32)
    for c in range(WIN_LON):
        cell = jnp.concatenate([states[c].astype(F32), loss[c].astype(F32)], axis=1)
        part, at = (1, 6 * c) if c < 6 else (0, 6 * (c - 6))
        for k in range(3):
            cells[k % 2, k // 2, part, at : at + 6, :] = cell[6 * k + 3 : 6 * k + 9]
        cells[1, 1, part, at : at + 3, :] = cell[21:24]
        cells[1, 1, part, at + 3 : at + 6, :] = nothing
        edges[part, at // 2 : at // 2 + 3, :] = cell[0:3]
    lanes = lax.broadcasted_iota(jnp.int32, (ROWS, 640), 1)
    row = lax.broadcasted_iota(jnp.int32, (ROWS, 640), 0)
    window = lanes // 128
    inner = lax.rem(lax.rem(lanes, 128), WIN_LAT)
    wanted = jnp.where(window == 4, inner - 3, 6 * window + 3 + inner)
    picked = nn(land[...].astype(BF16), (row == wanted).astype(BF16))
    token = lax.rem(lax.broadcasted_iota(jnp.int32, (6, 640), 1), 128)
    column = lax.broadcasted_iota(jnp.int32, (6, 640), 0)
    here = (token // WIN_LAT == column).astype(F32)
    for part in range(2):
        first = 6 - 6 * part
        line = jnp.sum(picked[first : first + 6] * here, axis=0, keepdims=True)
        for k in range(4):
            cells[k % 2, k // 2, part, HALF : HALF + 1, 0:128] = line[:, 128 * k : 128 * k + 128]
        edges[part, HALF // 2 : HALF // 2 + 1, 0:128] = line[:, 512:640]
    keep_out[...] = cells[core].astype(BF16)
    send_out[...] = cells[1 - core].astype(BF16)
    edge_out[...] = edges[...].astype(BF16)
    vectors_out[...] = vectors[...]
    weights.wait()


def sort_kernel(kept, arrived, edge0, edge1, near_own, near_x, lon_own, lon_x, cells):
    core = lax.axis_index("core")
    here = lax.axis_index("xh")
    cells[core] = kept[...].astype(F32)
    cells[1 - core] = arrived[...].astype(F32)

    @pl.when(core == 1)
    def _():
        for step, edge in enumerate((edge0, edge1)):
            for part in range(2):
                rows = edge[part].astype(F32)
                for c in range(6):
                    cells[step, 1, part, 6 * c + 3 : 6 * c + 6, :] = rows[3 * c : 3 * c + 3]
                line = rows[HALF // 2 : HALF // 2 + 1]
                cells[step, 1, part, HALF : HALF + 1, :] = (
                    cells[step, 1, part, HALF : HALF + 1, :] + line
                )

    for step in range(2):
        near_own[step] = cells[step, here, 0].astype(BF16)
        near_x[step] = cells[step, 1 - here, 0].astype(BF16)
        lon_own[step] = cells[step, here, 1].astype(BF16)
        lon_x[step] = cells[step, 1 - here, 1].astype(BF16)


def main_kernel(
    near_own, near_x, lon_own, lon_x, vectors, wqkv, wout, wup, wdown_t,
    send_out, keep_out,
    x, loss, land_s, qkv, probs, qm_all, emb, xh1, r1, hid_xh, r2, gp, act, normed_s, mixed_s, nm_s,
    cot_s, dpre_s, dproj_s, dqkv_s, dstate, small, msg,
):
    core = lax.axis_index("core")
    here = lax.axis_index("xh")
    last = jnp.logical_and(lax.axis_index("lat") == 7, jnp.logical_and(here == 1, core == 1))
    closed = jnp.where(last, 0.0, 1.0).astype(F32)
    for step in range(2):
        for half, part, cells in (
            (here, 0, near_own), (here, 1, lon_own), (1 - here, 0, near_x), (1 - here, 1, lon_x)
        ):
            rows = slice(HALF * part, HALF * part + HALF)
            block = cells[step].astype(F32)[0:HALF]
            x[2 * half + step, rows, :] = block[:, 0:CH]
            loss[2 * half + step, rows, :] = block[:, CH:MSG]
    for part, cells in ((0, near_own), (1, lon_own)):
        line = cells[0].astype(F32)[HALF : HALF + 1, 0:128]
        column = jnp.broadcast_to(line, (128, 128)).T[0:HALF]
        land_s[HALF * part : HALF * part + HALF, 0:128] = column
        land_s[HALF * part : HALF * part + HALF, 128:CH] = column[:, 0 : CH - 128]
    le = vectors[0:1, :]
    ga = vectors[1:2, :]
    gm = vectors[2:3, :]
    col_head = lax.broadcasted_iota(jnp.int32, (1, CH), 1) // HEAD_DIM
    masks = [(col_head == h).astype(F32) for h in range(HEADS)]
    row_half = lax.rem(lax.broadcasted_iota(jnp.int32, (WIN, WIN), 0), WIN_LAT) // 3
    key_half = lax.rem(lax.broadcasted_iota(jnp.int32, (WIN, WIN), 1), WIN_LAT) // 3
    allow1 = jnp.where(row_half == key_half, 1.0, closed).astype(F32)
    allow = jnp.concatenate([allow1] * HEADS, axis=1)

    def spread(v):
        return jnp.concatenate([v * m for m in masks], axis=0).astype(BF16)

    def gathered(v):
        total = v[0:WIN] * masks[0]
        for h in range(1, HEADS):
            total = total + v[WIN * h : WIN * h + WIN] * masks[h]
        return total

    for s in range(STEPS):
        rows = slice(WIN * s, WIN * s + WIN)
        land = land_s[...]
        e = x[s] + land * le
        emb[rows, :] = e
        off = e - mean_of(e)
        r = lax.rsqrt(mean_of(off * off) + EPS)
        xh = off * r
        xh1[rows, :] = xh
        r1[rows, :] = r
        normed_s[rows, :] = xh * ga
    normed = normed_s[...].astype(BF16)
    qkv[...] = nn(normed, wqkv[...]).astype(BF16).astype(F32)
    for s in range(STEPS):
        rows = slice(WIN * s, WIN * s + WIN)
        qm = spread(qkv[rows, 0:CH])
        qm_all[s] = qm
        keys = qkv[rows, CH : 2 * CH].astype(BF16)
        values = qkv[rows, 2 * CH : 3 * CH].astype(BF16)
        weights = jnp.exp(nt(keys, qm) * SCALE) * allow
        p = weights / jnp.sum(weights, axis=0, keepdims=True)
        probs[s] = p
        mixed_s[rows, :] = gathered(tn(p.astype(BF16), values))
    mixed = mixed_s[...].astype(BF16)
    projected = nn(mixed, wout[...]).astype(BF16).astype(F32)
    hid = emb[...] + projected
    off = hid - mean_of(hid)
    r = lax.rsqrt(mean_of(off * off) + EPS)
    xh = off * r
    hid_xh[...] = xh
    r2[...] = r
    nm_s[...] = (xh * gm).astype(BF16)
    for j in range(MLP // 256):
        cols = slice(256 * j, 256 * j + 256)
        pre = nn(nm_s[...], wup[:, cols])
        cdf = 0.5 * (1.0 + lax.erf(pre * (0.5 ** 0.5)))
        pdf = jnp.exp(pre * pre * -0.5) * 0.3989422804014327
        act[:, cols] = (pre * cdf).astype(BF16)
        gp[:, cols] = cdf + pre * pdf

    gain_m_sum = jnp.zeros((1, CH), F32)
    gain_a_sum = jnp.zeros((1, CH), F32)
    land_sum = jnp.zeros((1, CH), F32)
    incoming = None
    wq = wqkv[:, 0:CH]
    wk = wqkv[:, CH : 2 * CH]
    wv = wqkv[:, 2 * CH : 3 * CH]
    zero_rows = jnp.zeros((BLOCK - HALF, 128), F32)
    dstate[...] = jnp.zeros_like(dstate)
    for s in range(STEPS - 1, -1, -1):
        rows = slice(WIN * s, WIN * s + WIN)
        cot = loss[s]
        if incoming is not None:
            cot = cot + incoming
        cotb = cot.astype(BF16)
        cot_s[rows, :] = cotb.astype(F32)
        d_pre = gp[rows, :] * nn(cotb, wdown_t[...])
        dpre_b = d_pre.astype(BF16)
        dpre_s[rows, :] = dpre_b.astype(F32)
        dy = nt(dpre_b, wup[...])
        xh = hid_xh[rows, :]
        gain_m_sum = gain_m_sum + jnp.sum(dy * xh, axis=0, keepdims=True)
        dxh = dy * gm
        d_hid = cot + r2[rows, :] * (dxh - mean_of(dxh) - xh * mean_of(dxh * xh))
        dproj = d_hid.astype(BF16)
        dproj_s[rows, :] = dproj.astype(F32)
        d_mixed = nt(dproj, wout[...]).astype(BF16).astype(F32)
        dm = spread(d_mixed)
        keys = qkv[rows, CH : 2 * CH].astype(BF16)
        values = qkv[rows, 2 * CH : 3 * CH].astype(BF16)
        p = probs[s]
        dp = nt(values, dm)
        dv = nn(p.astype(BF16), dm).astype(BF16)
        ds = (p * (dp - jnp.sum(p * dp, axis=0, keepdims=True)) * SCALE).astype(BF16)
        dq = gathered(tn(ds, keys)).astype(BF16)
        dk = nn(ds, qm_all[s]).astype(BF16)
        dqkv_s[rows, 0:CH] = dq.astype(F32)
        dqkv_s[rows, CH : 2 * CH] = dk.astype(F32)
        dqkv_s[rows, 2 * CH : 3 * CH] = dv.astype(F32)
        d_rolled = nt(dq, wq) + nt(dk, wk) + nt(dv, wv)
        dy = d_rolled.astype(BF16).astype(F32)
        xh = xh1[rows, :]
        gain_a_sum = gain_a_sum + jnp.sum(dy * xh, axis=0, keepdims=True)
        dxh = dy * ga
        d_state = d_hid + r1[rows, :] * (dxh - mean_of(dxh) - xh * mean_of(dxh * xh))
        land = land_s[...]
        land_sum = land_sum + jnp.sum(d_state * land, axis=0, keepdims=True)
        incoming = d_state.astype(BF16).astype(F32)
        dstate[:, 0:CH] = incoming
        for half in range(2):
            piece = dstate[HALF * half : HALF * half + HALF, :]
            for tile in range(2):
                at = QUARTER * (s // 2) + BLOCK * (2 * half + tile)
                block = jnp.concatenate([piece[:, 128 * tile : 128 * tile + 128], zero_rows], axis=0)
                msg[s % 2, at : at + BLOCK, :] = block.astype(BF16)

    factor = float(STEPS * 192 * 96) ** (-0.5)

    def own_first(v):
        return jnp.where(core == 0, v, jnp.concatenate([v[:, HALF_CH:], v[:, :HALF_CH]], axis=1))

    def put(tile, value):
        value = (value * factor).astype(BF16)
        for j in range(value.shape[1] // 128):
            at = (tile + j) * HALF_CH
            piece = value[:, 128 * j : 128 * j + 128]
            keep_out[at : at + HALF_CH, :] = piece[:HALF_CH]
            send_out[at : at + HALF_CH, :] = piece[HALF_CH:]

    put(12, tn(own_first(cot_s[...]).astype(BF16), act[...]))
    put(6, tn(own_first(nm_s[...]), dpre_s[...].astype(BF16)))
    g_qkv = tn(own_first(normed_s[...]).astype(BF16), dqkv_s[...].astype(BF16))
    g_out = tn(own_first(mixed_s[...]).astype(BF16), dproj_s[...].astype(BF16))
    put(0, jnp.concatenate([g_qkv, g_out], axis=1))
    small[...] = jnp.zeros_like(small)
    for i, total in enumerate((land_sum, gain_a_sum, gain_m_sum)):
        total = total * factor
        small[2 * i : 2 * i + 1, :] = total[:, 0:128]
        small[2 * i + 1 : 2 * i + 2, 0:64] = total[:, 128:192]
    keep_out[TILED:SUMS, :] = jnp.where(core == 1, small[...], 0.0).astype(BF16)
    send_out[TILED:SUMS, :] = jnp.where(core == 1, 0.0, small[...]).astype(BF16)
    keep_out[SUMS:SENT, :] = msg[core]
    send_out[SUMS:SENT, :] = msg[1 - core]


def pair_kernel(kept, arrived, chunks, near_own, near_x, lon_own, lon_x):
    core = lax.axis_index("core")
    here = lax.axis_index("xh")
    for g in range(GROUP):
        at = UNIT * g
        total = kept[at : at + UNIT, :].astype(F32) + arrived[at : at + UNIT, :].astype(F32)
        chunks[g] = total.astype(BF16)
    for half, near, lon in ((here, near_own, lon_own), (1 - here, near_x, lon_x)):
        first = pl.ds(pl.multiple_of(SUMS + QUARTER * half, 64), COLUMNS)
        second = pl.ds(pl.multiple_of(SUMS + QUARTER * half + COLUMNS, 32), COLUMNS)
        near[core] = kept[first, :]
        near[1 - core] = arrived[first, :]
        lon[core] = kept[second, :]
        lon[1 - core] = arrived[second, :]


def group_kernel(terms, total_out):
    total = terms[0].astype(F32)
    for g in range(1, GROUP):
        total = total + terms[g].astype(F32)
    total = total.astype(BF16)
    for g in range(8):
        total_out[g] = total


def column_kernel(terms, near_own, near_x, lon_own, lon_x, total_out, near, lon, to_lat):
    here = lax.axis_index("xh")
    for c in range(2):
        near[2 * here + c] = near_own[c]
        near[2 * (1 - here) + c] = near_x[c]
        lon[2 * here + c] = lon_own[c]
        lon[2 * (1 - here) + c] = lon_x[c]
    to_lat[0] = near[3]
    to_lat[1] = lon[3]
    total = terms[0].astype(F32)
    for g in range(1, 8):
        total = total + terms[g].astype(F32)
    total = total.astype(BF16)
    for g in range(GROUP):
        total_out[g] = total


def unpack_kernel(own, other, g_qkv, g_out, g_up, g_down, g_land, g_ga, g_gm):
    core = lax.axis_index("core")
    for rows, half in ((core, own), (1 - core, other)):
        to = pl.ds(pl.multiple_of(HALF_CH * rows, 32), HALF_CH)

        def tile(t):
            return half[HALF_CH * t : HALF_CH * t + HALF_CH, :].astype(F32)

        for j in range(4):
            g_qkv[to, 128 * j : 128 * j + 128] = tile(j)
        mid = tile(4)
        g_qkv[to, 512:576] = mid[:, 0:64]
        g_out[to, :] = jnp.concatenate([mid[:, 64:128], tile(5)], axis=1)
        for j in range(6):
            g_up[to, 128 * j : 128 * j + 128] = tile(6 + j)
            g_down[to, 128 * j : 128 * j + 128] = tile(12 + j)
    little = jnp.where(
        core == 1, own[TILED : TILED + 16, :].astype(F32), other[TILED : TILED + 16, :].astype(F32)
    )
    for i, out in enumerate((g_land, g_ga, g_gm)):
        out[...] = jnp.concatenate(
            [little[2 * i : 2 * i + 1, :], little[2 * i + 1 : 2 * i + 2, 0:64]], axis=1
        )


def state_kernel(near, lon, edges, state_out):
    for part, first, wide in ((0, 6, near), (1, 0, lon)):
        for tile, lanes in ((0, slice(0, 128)), (1, slice(128, 192))):
            n = lanes.stop - lanes.start
            at = slice(BLOCK * tile, BLOCK * tile + BLOCK)
            before = edges[part, at, :].astype(F32)
            for c in range(6):
                state_out[first + c, 0:3, lanes] = before[6 * c + 3 : 6 * c + 6, 0:n]
            for k in range(4):
                block = wide[k, at, :].astype(F32)
                tall = 6 if k < 3 else 3
                for c in range(6):
                    state_out[first + c, 6 * k + 3 : 6 * k + 3 + tall, lanes] = block[
                        6 * c : 6 * c + tall, 0:n
                    ]


def hop(value, rows, cols, xh=0, cores=((0, 0), (1, 1))):
    pairs = []
    for h in range(2):
        for source, target in cores:
            for a in range(8):
                for b in range(8):
                    k = 2 * ((h + xh) % 2) + target
                    to = (k * 8 + (a + rows) % 8) * 8 + (b + cols) % 8
                    pairs.append((((2 * h + source) * 8 + a) * 8 + b, to))
    return lax.ppermute(value, AXES, pairs)


def swap(value, axis):
    return lax.ppermute(value, axis, [(0, 1), (1, 0)])


def exchange(value, axis):
    return lax.all_to_all(value, axis, 0, 0, tiled=True)


def call(kernel, name, outs, scratch=(), mib=8, from_hbm=0):
    specs = {}
    if from_hbm:
        specs["in_specs"] = [pl.BlockSpec(memory_space=pltpu.HBM)] * from_hbm
    return pl.pallas_call(
        kernel,
        out_shape=tuple(jax.ShapeDtypeStruct(dims, kind) for dims, kind in outs),
        scratch_shapes=[pltpu.VMEM(dims, kind) if kind else dims for dims, kind in scratch],
        compiler_params=pltpu.CompilerParams(vmem_limit_bytes=mib * MIB),
        name=name,
        **specs,
    )


def local(
    states, loss_grads, land_sea, land_embed, gain_attn, gain_mlp, w_qkv, w_out, w_up, w_down
):
    keep, send, edge, vectors, w_qkv = call(
        pack_kernel,
        "pack_cells",
        [((2, 2, TALL, MSG), BF16)] * 2 + [((2, 24, MSG), BF16), ((8, CH), F32)]
        + [((CH, 3 * CH), BF16)],
        [
            ((WIN_LON, ROWS, CH), BF16),
            ((WIN_LON, ROWS, CH), BF16),
            ((WIN_LON, ROWS), jnp.int32),
            ((8, CH), F32),
            ((2, 2, 2, TALL, MSG), F32),
            ((2, 24, MSG), F32),
            (pltpu.SemaphoreType.DMA((7,)), None),
        ],
        from_hbm=7,
    )(
        *(
            pltpu.with_memory_space_constraint(value, pltpu.HBM)
            for value in (
                states[0, 0].transpose(1, 0, 2), loss_grads[0, 0].transpose(1, 0, 2), land_sea.T,
                land_embed[None], gain_attn[None], gain_mlp[None], w_qkv,
            )
        )
    )
    near_own, near_x, lon_own, lon_x = call(
        sort_kernel,
        "sort_windows",
        [((2, TALL, MSG), BF16)] * 4,
        [((2, 2, 2, TALL, MSG), F32)],
    )(
        keep, swap(send, "core"),
        hop(edge, -1, 0, cores=((0, 1),)), hop(edge, -1, 0, cores=((1, 1),)),
    )
    near_x = hop(near_x, 0, 0, 1)
    lon_own = hop(lon_own, 0, -1)
    lon_x = hop(lon_x, 0, -1, 1)
    send, keep = call(
        main_kernel,
        "window_steps",
        [((SENT, 128), BF16)] * 2,
        [
            ((STEPS, WIN, CH), F32),
            ((STEPS, WIN, CH), F32),
            ((WIN, CH), F32),
            ((TOK, 3 * CH), F32),
            ((STEPS, WIN, HEADS * WIN), F32),
            ((STEPS, HEADS * WIN, CH), BF16),
            ((TOK, CH), F32),
            ((TOK, CH), F32),
            ((TOK, 1), F32),
            ((TOK, CH), F32),
            ((TOK, 1), F32),
            ((TOK, MLP), F32),
            ((TOK, MLP), BF16),
            ((TOK, CH), F32),
            ((TOK, CH), F32),
            ((TOK, CH), BF16),
            ((TOK, CH), F32),
            ((TOK, MLP), F32),
            ((TOK, CH), F32),
            ((TOK, 3 * CH), F32),
            ((WIN, 256), F32),
            ((SUMS - TILED, 128), F32),
            ((2, 2 * QUARTER, 128), BF16),
        ],
        mib=24,
    )(
        near_own, near_x, lon_own, lon_x, vectors, w_qkv, w_out, w_up, w_down.T
    )

    chunks, near_own, near_x, lon_own, lon_x = call(
        pair_kernel,
        "sum_cores",
        [((GROUP, UNIT, 128), BF16)] + [((2, COLUMNS, 128), BF16)] * 4,
    )(keep, swap(send, "core"))
    near_x = hop(near_x, 0, 0, 1)
    lon_own = hop(lon_own, 0, 1)
    lon_x = hop(lon_x, 0, 1, 1)
    (partial,) = call(group_kernel, "sum_group", [((8, UNIT, 128), BF16)])(
        exchange(chunks, ("xh", "lon"))
    )
    total, near, lon, to_lat = call(
        column_kernel,
        "sum_column",
        [((GROUP, UNIT, 128), BF16)]
        + [((4, COLUMNS, 128), BF16)] * 2
        + [((2, COLUMNS, 128), BF16)],
    )(exchange(partial, "lat"), near_own, near_x, lon_own, lon_x)
    own, edges = lax.optimization_barrier((exchange(total, ("xh", "lon")), hop(to_lat, 1, 0)))
    own = own.reshape(SUMS, 128)
    (state_grads,) = call(state_kernel, "unpack_states", [((WIN_LON, ROWS, CH), F32)])(
        near, lon, edges
    )
    outs = call(
        unpack_kernel,
        "unpack_sums",
        [
            ((CH, 3 * CH), F32),
            ((CH, CH), F32),
            ((CH, MLP), F32),
            ((CH, MLP), F32),
            ((1, CH), F32),
            ((1, CH), F32),
            ((1, CH), F32),
        ],
        mib=16,
    )(own, swap(own, "core"))
    return (
        state_grads.transpose(1, 0, 2)[None, None],
        outs[0], outs[1], outs[2], outs[3].T, outs[4][0], outs[5][0], outs[6][0],
    )


def solution(mesh):
    halves = Mesh(mesh.devices.reshape(2, 2, *mesh.devices.shape[1:]), AXES)
    cell = P(("xh", "core"), None, "lat", "lon", None)
    return jax.shard_map(
        local,
        mesh=halves,
        in_specs=(cell, cell, P("lat", "lon"), P(), P(), P(), P(), P(), P(), P()),
        out_specs=(cell, P(), P(), P(), P(), P(), P(), P()),
        check_vma=False,
    )
```

```python
import jax
import jax.numpy as jnp
from jax import lax
from jax.experimental import pallas as pl
from jax.experimental.pallas import tpu as pltpu
from jax.sharding import Mesh
from jax.sharding import PartitionSpec as P

CH = 192
HEADS = 6
HEAD_DIM = 32
MLP = 768
ROWS = 24
WIN_LAT = 6
WIN_LON = 12
WIN = WIN_LAT * WIN_LON
HALF = WIN // 2
STEPS = 4
TOK = STEPS * WIN
MSG = 384
TALL = 40
GROUP = 16
UNIT = 112
SUMS = GROUP * UNIT
BLOCK = 48
QUARTER = 4 * BLOCK
COLUMNS = QUARTER // 2
SENT = SUMS + 2 * QUARTER
HALF_CH = CH // 2
TILED = 18 * HALF_CH
SCALE = HEAD_DIM ** (-0.5)
EPS = 1e-05
F32 = jnp.float32
BF16 = jnp.bfloat16
AXES = ("xh", "core", "lat", "lon")
MIB = 1024 * 1024


def nn(a, b):
    return lax.dot_general(a, b, (((1,), (0,)), ((), ())), preferred_element_type=F32)


def nt(a, b):
    return lax.dot_general(a, b, (((1,), (1,)), ((), ())), preferred_element_type=F32)


def tn(a, b):
    return lax.dot_general(a, b, (((0,), (0,)), ((), ())), preferred_element_type=F32)


def mean_of(v):
    return jnp.sum(v, axis=-1, keepdims=True) * (1.0 / CH)


def pack_kernel(
    states_in, loss_in, land_in, embed_in, gain_a_in, gain_m_in, wqkv_in,
    keep_out, send_out, edge_out, vectors_out, wqkv_out,
    states, loss, land, vectors, cells, edges, sems,
):
    pairs = (
        (states_in, states), (loss_in, loss), (land_in, land),
        (embed_in, vectors.at[0:1]), (gain_a_in, vectors.at[1:2]), (gain_m_in, vectors.at[2:3]),
    )
    copies = [
        pltpu.make_async_copy(source, target, sems.at[i])
        for i, (source, target) in enumerate(pairs)
    ]
    weights = pltpu.make_async_copy(wqkv_in, wqkv_out, sems.at[6])
    for copy in copies:
        copy.start()
    weights.start()
    for copy in copies:
        copy.wait()
    core = lax.axis_index("core")
    nothing = jnp.zeros((3, MSG), F32)
    cells[:, :, :, HALF:TALL, :] = jnp.zeros((2, 2, 2, TALL - HALF, MSG), F32)
    edges[:, HALF // 2 : 24, :] = jnp.zeros((2, 24 - HALF // 2, MSG), F32)
    for c in range(WIN_LON):
        cell = jnp.concatenate([states[c].astype(F32), loss[c].astype(F32)], axis=1)
        part, at = (1, 6 * c) if c < 6 else (0, 6 * (c - 6))
        for k in range(3):
            cells[k % 2, k // 2, part, at : at + 6, :] = cell[6 * k + 3 : 6 * k + 9]
        cells[1, 1, part, at : at + 3, :] = cell[21:24]
        cells[1, 1, part, at + 3 : at + 6, :] = nothing
        edges[part, at // 2 : at // 2 + 3, :] = cell[0:3]
    lanes = lax.broadcasted_iota(jnp.int32, (ROWS, 640), 1)
    row = lax.broadcasted_iota(jnp.int32, (ROWS, 640), 0)
    window = lanes // 128
    inner = lax.rem(lax.rem(lanes, 128), WIN_LAT)
    wanted = jnp.where(window == 4, inner - 3, 6 * window + 3 + inner)
    picked = nn(land[...].astype(BF16), (row == wanted).astype(BF16))
    token = lax.rem(lax.broadcasted_iota(jnp.int32, (6, 640), 1), 128)
    column = lax.broadcasted_iota(jnp.int32, (6, 640), 0)
    here = (token // WIN_LAT == column).astype(F32)
    for part in range(2):
        first = 6 - 6 * part
        line = jnp.sum(picked[first : first + 6] * here, axis=0, keepdims=True)
        for k in range(4):
            cells[k % 2, k // 2, part, HALF : HALF + 1, 0:128] = line[:, 128 * k : 128 * k + 128]
        edges[part, HALF // 2 : HALF // 2 + 1, 0:128] = line[:, 512:640]
    keep_out[...] = cells[core].astype(BF16)
    send_out[...] = cells[1 - core].astype(BF16)
    edge_out[...] = edges[...].astype(BF16)
    vectors_out[...] = vectors[...]
    weights.wait()


def sort_kernel(kept, arrived, edge0, edge1, near_own, near_x, lon_own, lon_x, cells):
    core = lax.axis_index("core")
    here = lax.axis_index("xh")
    cells[core] = kept[...].astype(F32)
    cells[1 - core] = arrived[...].astype(F32)

    @pl.when(core == 1)
    def _():
        for step, edge in enumerate((edge0, edge1)):
            for part in range(2):
                rows = edge[part].astype(F32)
                for c in range(6):
                    cells[step, 1, part, 6 * c + 3 : 6 * c + 6, :] = rows[3 * c : 3 * c + 3]
                line = rows[HALF // 2 : HALF // 2 + 1]
                cells[step, 1, part, HALF : HALF + 1, :] = (
                    cells[step, 1, part, HALF : HALF + 1, :] + line
                )

    for step in range(2):
        near_own[step] = cells[step, here, 0].astype(BF16)
        near_x[step] = cells[step, 1 - here, 0].astype(BF16)
        lon_own[step] = cells[step, here, 1].astype(BF16)
        lon_x[step] = cells[step, 1 - here, 1].astype(BF16)


def main_kernel(
    lon_x, near_x, lon_own, near_own, vectors, wqkv, wout, wup, wdown_t,
    send_out, keep_out,
    x, loss, land_s, qkv, probs, qm_all, emb, xh1, r1, hid_xh, r2, gp, act, normed_s, mixed_s, nm_s,
    cot_s, dpre_s, dproj_s, dqkv_s, dstate, small, msg,
):
    core = lax.axis_index("core")
    here = lax.axis_index("xh")
    last = jnp.logical_and(lax.axis_index("lat") == 7, jnp.logical_and(here == 1, core == 1))
    closed = jnp.where(last, 0.0, 1.0).astype(F32)
    for step in range(2):
        for half, part, cells in (
            (here, 0, near_own), (here, 1, lon_own), (1 - here, 0, near_x), (1 - here, 1, lon_x)
        ):
            rows = slice(HALF * part, HALF * part + HALF)
            block = cells[step].astype(F32)[0:HALF]
            x[2 * half + step, rows, :] = block[:, 0:CH]
            loss[2 * half + step, rows, :] = block[:, CH:MSG]
    for part, cells in ((0, near_own), (1, lon_own)):
        line = cells[0].astype(F32)[HALF : HALF + 1, 0:128]
        column = jnp.broadcast_to(line, (128, 128)).T[0:HALF]
        land_s[HALF * part : HALF * part + HALF, 0:128] = column
        land_s[HALF * part : HALF * part + HALF, 128:CH] = column[:, 0 : CH - 128]
    le = vectors[0:1, :]
    ga = vectors[1:2, :]
    gm = vectors[2:3, :]
    col_head = lax.broadcasted_iota(jnp.int32, (1, CH), 1) // HEAD_DIM
    masks = [(col_head == h).astype(F32) for h in range(HEADS)]
    row_half = lax.rem(lax.broadcasted_iota(jnp.int32, (WIN, WIN), 0), WIN_LAT) // 3
    key_half = lax.rem(lax.broadcasted_iota(jnp.int32, (WIN, WIN), 1), WIN_LAT) // 3
    allow1 = jnp.where(row_half == key_half, 1.0, closed).astype(F32)
    allow = jnp.concatenate([allow1] * HEADS, axis=1)

    def spread(v):
        return jnp.concatenate([v * m for m in masks], axis=0).astype(BF16)

    def gathered(v):
        total = v[0:WIN] * masks[0]
        for h in range(1, HEADS):
            total = total + v[WIN * h : WIN * h + WIN] * masks[h]
        return total

    for s in range(STEPS):
        rows = slice(WIN * s, WIN * s + WIN)
        land = land_s[...]
        e = x[s] + land * le
        emb[rows, :] = e
        off = e - mean_of(e)
        r = lax.rsqrt(mean_of(off * off) + EPS)
        xh = off * r
        xh1[rows, :] = xh
        r1[rows, :] = r
        normed_s[rows, :] = xh * ga
    normed = normed_s[...].astype(BF16)
    qkv[...] = nn(normed, wqkv[...]).astype(BF16).astype(F32)
    for s in range(STEPS):
        rows = slice(WIN * s, WIN * s + WIN)
        qm = spread(qkv[rows, 0:CH])
        qm_all[s] = qm
        keys = qkv[rows, CH : 2 * CH].astype(BF16)
        values = qkv[rows, 2 * CH : 3 * CH].astype(BF16)
        weights = jnp.exp(nt(keys, qm) * SCALE) * allow
        p = weights / jnp.sum(weights, axis=0, keepdims=True)
        probs[s] = p
        mixed_s[rows, :] = gathered(tn(p.astype(BF16), values))
    mixed = mixed_s[...].astype(BF16)
    projected = nn(mixed, wout[...]).astype(BF16).astype(F32)
    hid = emb[...] + projected
    off = hid - mean_of(hid)
    r = lax.rsqrt(mean_of(off * off) + EPS)
    xh = off * r
    hid_xh[...] = xh
    r2[...] = r
    nm_s[...] = (xh * gm).astype(BF16)
    for j in range(MLP // 256):
        cols = slice(256 * j, 256 * j + 256)
        pre = nn(nm_s[...], wup[:, cols])
        cdf = 0.5 * (1.0 + lax.erf(pre * (0.5 ** 0.5)))
        pdf = jnp.exp(pre * pre * -0.5) * 0.3989422804014327
        act[:, cols] = (pre * cdf).astype(BF16)
        gp[:, cols] = cdf + pre * pdf

    gain_m_sum = jnp.zeros((1, CH), F32)
    gain_a_sum = jnp.zeros((1, CH), F32)
    land_sum = jnp.zeros((1, CH), F32)
    incoming = None
    wq = wqkv[:, 0:CH]
    wk = wqkv[:, CH : 2 * CH]
    wv = wqkv[:, 2 * CH : 3 * CH]
    zero_rows = jnp.zeros((BLOCK - HALF, 128), F32)
    dstate[...] = jnp.zeros_like(dstate)
    for s in range(STEPS - 1, -1, -1):
        rows = slice(WIN * s, WIN * s + WIN)
        cot = loss[s]
        if incoming is not None:
            cot = cot + incoming
        cotb = cot.astype(BF16)
        cot_s[rows, :] = cotb.astype(F32)
        d_pre = gp[rows, :] * nn(cotb, wdown_t[...])
        dpre_b = d_pre.astype(BF16)
        dpre_s[rows, :] = dpre_b.astype(F32)
        dy = nt(dpre_b, wup[...])
        xh = hid_xh[rows, :]
        gain_m_sum = gain_m_sum + jnp.sum(dy * xh, axis=0, keepdims=True)
        dxh = dy * gm
        d_hid = cot + r2[rows, :] * (dxh - mean_of(dxh) - xh * mean_of(dxh * xh))
        dproj = d_hid.astype(BF16)
        dproj_s[rows, :] = dproj.astype(F32)
        d_mixed = nt(dproj, wout[...]).astype(BF16).astype(F32)
        dm = spread(d_mixed)
        keys = qkv[rows, CH : 2 * CH].astype(BF16)
        values = qkv[rows, 2 * CH : 3 * CH].astype(BF16)
        p = probs[s]
        dp = nt(values, dm)
        dv = nn(p.astype(BF16), dm).astype(BF16)
        ds = (p * (dp - jnp.sum(p * dp, axis=0, keepdims=True)) * SCALE).astype(BF16)
        dq = gathered(tn(ds, keys)).astype(BF16)
        dk = nn(ds, qm_all[s]).astype(BF16)
        dqkv_s[rows, 0:CH] = dq.astype(F32)
        dqkv_s[rows, CH : 2 * CH] = dk.astype(F32)
        dqkv_s[rows, 2 * CH : 3 * CH] = dv.astype(F32)
        d_rolled = nt(dq, wq) + nt(dk, wk) + nt(dv, wv)
        dy = d_rolled.astype(BF16).astype(F32)
        xh = xh1[rows, :]
        gain_a_sum = gain_a_sum + jnp.sum(dy * xh, axis=0, keepdims=True)
        dxh = dy * ga
        d_state = d_hid + r1[rows, :] * (dxh - mean_of(dxh) - xh * mean_of(dxh * xh))
        land = land_s[...]
        land_sum = land_sum + jnp.sum(d_state * land, axis=0, keepdims=True)
        incoming = d_state.astype(BF16).astype(F32)
        dstate[:, 0:CH] = incoming
        for half in range(2):
            piece = dstate[HALF * half : HALF * half + HALF, :]
            for tile in range(2):
                at = QUARTER * (s // 2) + BLOCK * (2 * half + tile)
                block = jnp.concatenate([piece[:, 128 * tile : 128 * tile + 128], zero_rows], axis=0)
                msg[s % 2, at : at + BLOCK, :] = block.astype(BF16)

    factor = float(STEPS * 192 * 96) ** (-0.5)

    def own_first(v):
        return jnp.where(core == 0, v, jnp.concatenate([v[:, HALF_CH:], v[:, :HALF_CH]], axis=1))

    def put(tile, value):
        value = (value * factor).astype(BF16)
        for j in range(value.shape[1] // 128):
            at = (tile + j) * HALF_CH
            piece = value[:, 128 * j : 128 * j + 128]
            keep_out[at : at + HALF_CH, :] = piece[:HALF_CH]
            send_out[at : at + HALF_CH, :] = piece[HALF_CH:]

    put(12, tn(own_first(cot_s[...]).astype(BF16), act[...]))
    put(6, tn(own_first(nm_s[...]), dpre_s[...].astype(BF16)))
    g_qkv = tn(own_first(normed_s[...]).astype(BF16), dqkv_s[...].astype(BF16))
    g_out = tn(own_first(mixed_s[...]).astype(BF16), dproj_s[...].astype(BF16))
    put(0, jnp.concatenate([g_qkv, g_out], axis=1))
    small[...] = jnp.zeros_like(small)
    for i, total in enumerate((land_sum, gain_a_sum, gain_m_sum)):
        total = total * factor
        small[2 * i : 2 * i + 1, :] = total[:, 0:128]
        small[2 * i + 1 : 2 * i + 2, 0:64] = total[:, 128:192]
    keep_out[TILED:SUMS, :] = jnp.where(core == 1, small[...], 0.0).astype(BF16)
    send_out[TILED:SUMS, :] = jnp.where(core == 1, 0.0, small[...]).astype(BF16)
    keep_out[SUMS:SENT, :] = msg[core]
    send_out[SUMS:SENT, :] = msg[1 - core]


def pair_kernel(kept, arrived, chunks, near_own, near_x, lon_own, lon_x):
    core = lax.axis_index("core")
    here = lax.axis_index("xh")
    for g in range(GROUP):
        at = UNIT * g
        total = kept[at : at + UNIT, :].astype(F32) + arrived[at : at + UNIT, :].astype(F32)
        chunks[g] = total.astype(BF16)
    for half, near, lon in ((here, near_own, lon_own), (1 - here, near_x, lon_x)):
        first = pl.ds(pl.multiple_of(SUMS + QUARTER * half, 64), COLUMNS)
        second = pl.ds(pl.multiple_of(SUMS + QUARTER * half + COLUMNS, 32), COLUMNS)
        near[core] = kept[first, :]
        near[1 - core] = arrived[first, :]
        lon[core] = kept[second, :]
        lon[1 - core] = arrived[second, :]


def group_kernel(terms, total_out):
    total = terms[0].astype(F32)
    for g in range(1, GROUP):
        total = total + terms[g].astype(F32)
    total = total.astype(BF16)
    for g in range(8):
        total_out[g] = total


def column_kernel(terms, lon_x, near_x, lon_own, near_own, total_out, near, lon, to_lat):
    here = lax.axis_index("xh")
    for c in range(2):
        near[2 * here + c] = near_own[c]
        near[2 * (1 - here) + c] = near_x[c]
        lon[2 * here + c] = lon_own[c]
        lon[2 * (1 - here) + c] = lon_x[c]
    to_lat[0] = near[3]
    to_lat[1] = lon[3]
    total = terms[0].astype(F32)
    for g in range(1, 8):
        total = total + terms[g].astype(F32)
    total = total.astype(BF16)
    for g in range(GROUP):
        total_out[g] = total


def unpack_kernel(own, other, g_qkv, g_out, g_up, g_down, g_land, g_ga, g_gm):
    core = lax.axis_index("core")
    for rows, half in ((core, own), (1 - core, other)):
        to = pl.ds(pl.multiple_of(HALF_CH * rows, 32), HALF_CH)

        def tile(t):
            return half[HALF_CH * t : HALF_CH * t + HALF_CH, :].astype(F32)

        for j in range(4):
            g_qkv[to, 128 * j : 128 * j + 128] = tile(j)
        mid = tile(4)
        g_qkv[to, 512:576] = mid[:, 0:64]
        g_out[to, :] = jnp.concatenate([mid[:, 64:128], tile(5)], axis=1)
        for j in range(6):
            g_up[to, 128 * j : 128 * j + 128] = tile(6 + j)
            g_down[to, 128 * j : 128 * j + 128] = tile(12 + j)
    little = jnp.where(
        core == 1, own[TILED : TILED + 16, :].astype(F32), other[TILED : TILED + 16, :].astype(F32)
    )
    for i, out in enumerate((g_land, g_ga, g_gm)):
        out[...] = jnp.concatenate(
            [little[2 * i : 2 * i + 1, :], little[2 * i + 1 : 2 * i + 2, 0:64]], axis=1
        )


def state_kernel(near, lon, edges, state_out):
    for part, first, wide in ((0, 6, near), (1, 0, lon)):
        for tile, lanes in ((0, slice(0, 128)), (1, slice(128, 192))):
            n = lanes.stop - lanes.start
            at = slice(BLOCK * tile, BLOCK * tile + BLOCK)
            before = edges[part, at, :].astype(F32)
            for c in range(6):
                state_out[first + c, 0:3, lanes] = before[6 * c + 3 : 6 * c + 6, 0:n]
            for k in range(4):
                block = wide[k, at, :].astype(F32)
                tall = 6 if k < 3 else 3
                for c in range(6):
                    state_out[first + c, 6 * k + 3 : 6 * k + 3 + tall, lanes] = block[
                        6 * c : 6 * c + tall, 0:n
                    ]


def hop(value, rows, cols, xh=0, cores=((0, 0), (1, 1))):
    pairs = []
    for h in range(2):
        for source, target in cores:
            for a in range(8):
                for b in range(8):
                    k = 2 * ((h + xh) % 2) + target
                    to = (k * 8 + (a + rows) % 8) * 8 + (b + cols) % 8
                    pairs.append((((2 * h + source) * 8 + a) * 8 + b, to))
    return lax.ppermute(value, AXES, pairs)


def swap(value, axis):
    return lax.ppermute(value, axis, [(0, 1), (1, 0)])


def exchange(value, axis):
    return lax.all_to_all(value, axis, 0, 0, tiled=True)


def call(kernel, name, outs, scratch=(), mib=8, from_hbm=0):
    specs = {}
    if from_hbm:
        specs["in_specs"] = [pl.BlockSpec(memory_space=pltpu.HBM)] * from_hbm
    return pl.pallas_call(
        kernel,
        out_shape=tuple(jax.ShapeDtypeStruct(dims, kind) for dims, kind in outs),
        scratch_shapes=[pltpu.VMEM(dims, kind) if kind else dims for dims, kind in scratch],
        compiler_params=pltpu.CompilerParams(vmem_limit_bytes=mib * MIB),
        name=name,
        **specs,
    )


def local(
    states, loss_grads, land_sea, land_embed, gain_attn, gain_mlp, w_qkv, w_out, w_up, w_down
):
    keep, send, edge, vectors, w_qkv = call(
        pack_kernel,
        "pack_cells",
        [((2, 2, TALL, MSG), BF16)] * 2 + [((2, 24, MSG), BF16), ((8, CH), F32)]
        + [((CH, 3 * CH), BF16)],
        [
            ((WIN_LON, ROWS, CH), BF16),
            ((WIN_LON, ROWS, CH), BF16),
            ((WIN_LON, ROWS), jnp.int32),
            ((8, CH), F32),
            ((2, 2, 2, TALL, MSG), F32),
            ((2, 24, MSG), F32),
            (pltpu.SemaphoreType.DMA((7,)), None),
        ],
        from_hbm=7,
    )(
        *(
            pltpu.with_memory_space_constraint(value, pltpu.HBM)
            for value in (
                states[0, 0].transpose(1, 0, 2), loss_grads[0, 0].transpose(1, 0, 2), land_sea.T,
                land_embed[None], gain_attn[None], gain_mlp[None], w_qkv,
            )
        )
    )
    near_own, near_x, lon_own, lon_x = call(
        sort_kernel,
        "sort_windows",
        [((2, TALL, MSG), BF16)] * 4,
        [((2, 2, 2, TALL, MSG), F32)],
    )(
        keep, swap(send, "core"),
        hop(edge, -1, 0, cores=((0, 1),)), hop(edge, -1, 0, cores=((1, 1),)),
    )
    lon_x = hop(lon_x, 0, -1, 1)
    near_x = hop(near_x, 0, 0, 1)
    lon_own = hop(lon_own, 0, -1)
    send, keep = call(
        main_kernel,
        "window_steps",
        [((SENT, 128), BF16)] * 2,
        [
            ((STEPS, WIN, CH), F32),
            ((STEPS, WIN, CH), F32),
            ((WIN, CH), F32),
            ((TOK, 3 * CH), F32),
            ((STEPS, WIN, HEADS * WIN), F32),
            ((STEPS, HEADS * WIN, CH), BF16),
            ((TOK, CH), F32),
            ((TOK, CH), F32),
            ((TOK, 1), F32),
            ((TOK, CH), F32),
            ((TOK, 1), F32),
            ((TOK, MLP), F32),
            ((TOK, MLP), BF16),
            ((TOK, CH), F32),
            ((TOK, CH), F32),
            ((TOK, CH), BF16),
            ((TOK, CH), F32),
            ((TOK, MLP), F32),
            ((TOK, CH), F32),
            ((TOK, 3 * CH), F32),
            ((WIN, 256), F32),
            ((SUMS - TILED, 128), F32),
            ((2, 2 * QUARTER, 128), BF16),
        ],
        mib=24,
    )(
        lon_x, near_x, lon_own, near_own, vectors, w_qkv, w_out, w_up, w_down.T
    )

    chunks, near_own, near_x, lon_own, lon_x = call(
        pair_kernel,
        "sum_cores",
        [((GROUP, UNIT, 128), BF16)] + [((2, COLUMNS, 128), BF16)] * 4,
    )(keep, swap(send, "core"))
    lon_x = hop(lon_x, 0, 1, 1)
    near_x = hop(near_x, 0, 0, 1)
    lon_own = hop(lon_own, 0, 1)
    (partial,) = call(group_kernel, "sum_group", [((8, UNIT, 128), BF16)])(
        exchange(chunks, ("xh", "lon"))
    )
    total, near, lon, to_lat = call(
        column_kernel,
        "sum_column",
        [((GROUP, UNIT, 128), BF16)]
        + [((4, COLUMNS, 128), BF16)] * 2
        + [((2, COLUMNS, 128), BF16)],
    )(exchange(partial, "lat"), lon_x, near_x, lon_own, near_own)
    own, edges = lax.optimization_barrier((exchange(total, ("xh", "lon")), hop(to_lat, 1, 0)))
    own = own.reshape(SUMS, 128)
    (state_grads,) = call(state_kernel, "unpack_states", [((WIN_LON, ROWS, CH), F32)])(
        near, lon, edges
    )
    outs = call(
        unpack_kernel,
        "unpack_sums",
        [
            ((CH, 3 * CH), F32),
            ((CH, CH), F32),
            ((CH, MLP), F32),
            ((CH, MLP), F32),
            ((1, CH), F32),
            ((1, CH), F32),
            ((1, CH), F32),
        ],
        mib=16,
    )(own, swap(own, "core"))
    return (
        state_grads.transpose(1, 0, 2)[None, None],
        outs[0], outs[1], outs[2], outs[3].T, outs[4][0], outs[5][0], outs[6][0],
    )


def solution(mesh):
    halves = Mesh(mesh.devices.reshape(2, 2, *mesh.devices.shape[1:]), AXES)
    cell = P(("xh", "core"), None, "lat", "lon", None)
    return jax.shard_map(
        local,
        mesh=halves,
        in_specs=(cell, cell, P("lat", "lon"), P(), P(), P(), P(), P(), P(), P()),
        out_specs=(cell, P(), P(), P(), P(), P(), P(), P()),
        check_vma=False,
    )
```

```python
import jax
import jax.numpy as jnp
from jax import lax
from jax.experimental import pallas as pl
from jax.experimental.pallas import tpu as pltpu
from jax.sharding import Mesh
from jax.sharding import PartitionSpec as P

CH = 192
HEADS = 6
HEAD_DIM = 32
MLP = 768
ROWS = 24
WIN_LAT = 6
WIN_LON = 12
WIN = WIN_LAT * WIN_LON
HALF = WIN // 2
STEPS = 4
TOK = STEPS * WIN
MSG = 384
TALL = 40
GROUP = 16
UNIT = 112
SUMS = GROUP * UNIT
BLOCK = 48
QUARTER = 4 * BLOCK
SENT = SUMS + 2 * QUARTER
HALF_CH = CH // 2
TILED = 18 * HALF_CH
SCALE = HEAD_DIM ** (-0.5)
EPS = 1e-05
F32 = jnp.float32
BF16 = jnp.bfloat16
AXES = ("xh", "core", "lat", "lon")
MIB = 1024 * 1024


def nn(a, b):
    return lax.dot_general(a, b, (((1,), (0,)), ((), ())), preferred_element_type=F32)


def nt(a, b):
    return lax.dot_general(a, b, (((1,), (1,)), ((), ())), preferred_element_type=F32)


def tn(a, b):
    return lax.dot_general(a, b, (((0,), (0,)), ((), ())), preferred_element_type=F32)


def mean_of(v):
    return jnp.sum(v, axis=-1, keepdims=True) * (1.0 / CH)


def pack_kernel(
    states_in, loss_in, land_in, embed_in, gain_a_in, gain_m_in, wqkv_in,
    keep_out, send_out, edge_out, vectors_out, wqkv_out,
    states, loss, land, vectors, cells, edges, sems,
):
    pairs = (
        (states_in, states), (loss_in, loss), (land_in, land),
        (embed_in, vectors.at[0:1]), (gain_a_in, vectors.at[1:2]), (gain_m_in, vectors.at[2:3]),
    )
    copies = [
        pltpu.make_async_copy(source, target, sems.at[i])
        for i, (source, target) in enumerate(pairs)
    ]
    weights = pltpu.make_async_copy(wqkv_in, wqkv_out, sems.at[6])
    for copy in copies:
        copy.start()
    weights.start()
    for copy in copies:
        copy.wait()
    core = lax.axis_index("core")
    nothing = jnp.zeros((3, MSG), F32)
    cells[:, :, :, HALF:TALL, :] = jnp.zeros((2, 2, 2, TALL - HALF, MSG), F32)
    edges[:, HALF // 2 : 24, :] = jnp.zeros((2, 24 - HALF // 2, MSG), F32)
    for c in range(WIN_LON):
        cell = jnp.concatenate([states[c].astype(F32), loss[c].astype(F32)], axis=1)
        part, at = (1, 6 * c) if c < 6 else (0, 6 * (c - 6))
        for k in range(3):
            cells[k % 2, k // 2, part, at : at + 6, :] = cell[6 * k + 3 : 6 * k + 9]
        cells[1, 1, part, at : at + 3, :] = cell[21:24]
        cells[1, 1, part, at + 3 : at + 6, :] = nothing
        edges[part, at // 2 : at // 2 + 3, :] = cell[0:3]
    lanes = lax.broadcasted_iota(jnp.int32, (ROWS, 640), 1)
    row = lax.broadcasted_iota(jnp.int32, (ROWS, 640), 0)
    window = lanes // 128
    inner = lax.rem(lax.rem(lanes, 128), WIN_LAT)
    wanted = jnp.where(window == 4, inner - 3, 6 * window + 3 + inner)
    picked = nn(land[...].astype(BF16), (row == wanted).astype(BF16))
    token = lax.rem(lax.broadcasted_iota(jnp.int32, (6, 640), 1), 128)
    column = lax.broadcasted_iota(jnp.int32, (6, 640), 0)
    here = (token // WIN_LAT == column).astype(F32)
    for part in range(2):
        first = 6 - 6 * part
        line = jnp.sum(picked[first : first + 6] * here, axis=0, keepdims=True)
        for k in range(4):
            cells[k % 2, k // 2, part, HALF : HALF + 1, 0:128] = line[:, 128 * k : 128 * k + 128]
        edges[part, HALF // 2 : HALF // 2 + 1, 0:128] = line[:, 512:640]
    keep_out[...] = cells[core].astype(BF16)
    send_out[...] = cells[1 - core].astype(BF16)
    edge_out[...] = edges[...].astype(BF16)
    vectors_out[...] = vectors[...]
    weights.wait()


def sort_kernel(kept, arrived, edge0, edge1, near_own, near_x, lon_own, lon_x, cells):
    core = lax.axis_index("core")
    here = lax.axis_index("xh")
    cells[core] = kept[...].astype(F32)
    cells[1 - core] = arrived[...].astype(F32)

    @pl.when(core == 1)
    def _():
        for step, edge in enumerate((edge0, edge1)):
            for part in range(2):
                rows = edge[part].astype(F32)
                for c in range(6):
                    cells[step, 1, part, 6 * c + 3 : 6 * c + 6, :] = rows[3 * c : 3 * c + 3]
                line = rows[HALF // 2 : HALF // 2 + 1]
                cells[step, 1, part, HALF : HALF + 1, :] = (
                    cells[step, 1, part, HALF : HALF + 1, :] + line
                )

    for step in range(2):
        near_own[step] = cells[step, here, 0].astype(BF16)
        near_x[step] = cells[step, 1 - here, 0].astype(BF16)
        lon_own[step] = cells[step, here, 1].astype(BF16)
        lon_x[step] = cells[step, 1 - here, 1].astype(BF16)


def main_kernel(
    lon_x, near_x, lon_own, near_own, vectors, wqkv, wout, wup, wdown_t,
    send_out, keep_out,
    x, loss, land_s, qkv, probs, qm_all, emb, xh1, r1, hid_xh, r2, gp, act, normed_s, mixed_s, nm_s,
    cot_s, dpre_s, dproj_s, dqkv_s, dstate, small, msg,
):
    core = lax.axis_index("core")
    here = lax.axis_index("xh")
    last = jnp.logical_and(lax.axis_index("lat") == 7, jnp.logical_and(here == 1, core == 1))
    closed = jnp.where(last, 0.0, 1.0).astype(F32)
    for step in range(2):
        for half, part, cells in (
            (here, 0, near_own), (here, 1, lon_own), (1 - here, 0, near_x), (1 - here, 1, lon_x)
        ):
            rows = slice(HALF * part, HALF * part + HALF)
            block = cells[step].astype(F32)[0:HALF]
            x[2 * half + step, rows, :] = block[:, 0:CH]
            loss[2 * half + step, rows, :] = block[:, CH:MSG]
    for part, cells in ((0, near_own), (1, lon_own)):
        line = cells[0].astype(F32)[HALF : HALF + 1, 0:128]
        column = jnp.broadcast_to(line, (128, 128)).T[0:HALF]
        land_s[HALF * part : HALF * part + HALF, 0:128] = column
        land_s[HALF * part : HALF * part + HALF, 128:CH] = column[:, 0 : CH - 128]
    le = vectors[0:1, :]
    ga = vectors[1:2, :]
    gm = vectors[2:3, :]
    col_head = lax.broadcasted_iota(jnp.int32, (1, CH), 1) // HEAD_DIM
    masks = [(col_head == h).astype(F32) for h in range(HEADS)]
    row_half = lax.rem(lax.broadcasted_iota(jnp.int32, (WIN, WIN), 0), WIN_LAT) // 3
    key_half = lax.rem(lax.broadcasted_iota(jnp.int32, (WIN, WIN), 1), WIN_LAT) // 3
    allow1 = jnp.where(row_half == key_half, 1.0, closed).astype(F32)
    allow = jnp.concatenate([allow1] * HEADS, axis=1)

    def spread(v):
        return jnp.concatenate([v * m for m in masks], axis=0).astype(BF16)

    def gathered(v):
        total = v[0:WIN] * masks[0]
        for h in range(1, HEADS):
            total = total + v[WIN * h : WIN * h + WIN] * masks[h]
        return total

    for s in range(STEPS):
        rows = slice(WIN * s, WIN * s + WIN)
        land = land_s[...]
        e = x[s] + land * le
        emb[rows, :] = e
        off = e - mean_of(e)
        r = lax.rsqrt(mean_of(off * off) + EPS)
        xh = off * r
        xh1[rows, :] = xh
        r1[rows, :] = r
        normed_s[rows, :] = xh * ga
    normed = normed_s[...].astype(BF16)
    qkv[...] = nn(normed, wqkv[...]).astype(BF16).astype(F32)
    for s in range(STEPS):
        rows = slice(WIN * s, WIN * s + WIN)
        qm = spread(qkv[rows, 0:CH])
        qm_all[s] = qm
        keys = qkv[rows, CH : 2 * CH].astype(BF16)
        values = qkv[rows, 2 * CH : 3 * CH].astype(BF16)
        weights = jnp.exp(nt(keys, qm) * SCALE) * allow
        p = weights / jnp.sum(weights, axis=0, keepdims=True)
        probs[s] = p
        mixed_s[rows, :] = gathered(tn(p.astype(BF16), values))
    mixed = mixed_s[...].astype(BF16)
    projected = nn(mixed, wout[...]).astype(BF16).astype(F32)
    hid = emb[...] + projected
    off = hid - mean_of(hid)
    r = lax.rsqrt(mean_of(off * off) + EPS)
    xh = off * r
    hid_xh[...] = xh
    r2[...] = r
    nm_s[...] = (xh * gm).astype(BF16)
    for j in range(MLP // 256):
        cols = slice(256 * j, 256 * j + 256)
        pre = nn(nm_s[...], wup[:, cols])
        cdf = 0.5 * (1.0 + lax.erf(pre * (0.5 ** 0.5)))
        pdf = jnp.exp(pre * pre * -0.5) * 0.3989422804014327
        act[:, cols] = (pre * cdf).astype(BF16)
        gp[:, cols] = cdf + pre * pdf

    gain_m_sum = jnp.zeros((1, CH), F32)
    gain_a_sum = jnp.zeros((1, CH), F32)
    land_sum = jnp.zeros((1, CH), F32)
    incoming = None
    wq = wqkv[:, 0:CH]
    wk = wqkv[:, CH : 2 * CH]
    wv = wqkv[:, 2 * CH : 3 * CH]
    zero_rows = jnp.zeros((BLOCK - HALF, 128), F32)
    dstate[...] = jnp.zeros_like(dstate)
    for s in range(STEPS - 1, -1, -1):
        rows = slice(WIN * s, WIN * s + WIN)
        cot = loss[s]
        if incoming is not None:
            cot = cot + incoming
        cotb = cot.astype(BF16)
        cot_s[rows, :] = cotb.astype(F32)
        d_pre = gp[rows, :] * nn(cotb, wdown_t[...])
        dpre_b = d_pre.astype(BF16)
        dpre_s[rows, :] = dpre_b.astype(F32)
        dy = nt(dpre_b, wup[...])
        xh = hid_xh[rows, :]
        gain_m_sum = gain_m_sum + jnp.sum(dy * xh, axis=0, keepdims=True)
        dxh = dy * gm
        d_hid = cot + r2[rows, :] * (dxh - mean_of(dxh) - xh * mean_of(dxh * xh))
        dproj = d_hid.astype(BF16)
        dproj_s[rows, :] = dproj.astype(F32)
        d_mixed = nt(dproj, wout[...]).astype(BF16).astype(F32)
        dm = spread(d_mixed)
        keys = qkv[rows, CH : 2 * CH].astype(BF16)
        values = qkv[rows, 2 * CH : 3 * CH].astype(BF16)
        p = probs[s]
        dp = nt(values, dm)
        dv = nn(p.astype(BF16), dm).astype(BF16)
        ds = (p * (dp - jnp.sum(p * dp, axis=0, keepdims=True)) * SCALE).astype(BF16)
        dq = gathered(tn(ds, keys)).astype(BF16)
        dk = nn(ds, qm_all[s]).astype(BF16)
        dqkv_s[rows, 0:CH] = dq.astype(F32)
        dqkv_s[rows, CH : 2 * CH] = dk.astype(F32)
        dqkv_s[rows, 2 * CH : 3 * CH] = dv.astype(F32)
        d_rolled = nt(dq, wq) + nt(dk, wk) + nt(dv, wv)
        dy = d_rolled.astype(BF16).astype(F32)
        xh = xh1[rows, :]
        gain_a_sum = gain_a_sum + jnp.sum(dy * xh, axis=0, keepdims=True)
        dxh = dy * ga
        d_state = d_hid + r1[rows, :] * (dxh - mean_of(dxh) - xh * mean_of(dxh * xh))
        land = land_s[...]
        land_sum = land_sum + jnp.sum(d_state * land, axis=0, keepdims=True)
        incoming = d_state.astype(BF16).astype(F32)
        dstate[:, 0:CH] = incoming
        for half in range(2):
            piece = dstate[HALF * half : HALF * half + HALF, :]
            for tile in range(2):
                at = QUARTER * (s // 2) + BLOCK * (2 * half + tile)
                block = jnp.concatenate([piece[:, 128 * tile : 128 * tile + 128], zero_rows], axis=0)
                msg[s % 2, at : at + BLOCK, :] = block.astype(BF16)

    factor = float(STEPS * 192 * 96) ** (-0.5)

    def own_first(v):
        return jnp.where(core == 0, v, jnp.concatenate([v[:, HALF_CH:], v[:, :HALF_CH]], axis=1))

    def put(tile, value):
        value = (value * factor).astype(BF16)
        for j in range(value.shape[1] // 128):
            at = (tile + j) * HALF_CH
            piece = value[:, 128 * j : 128 * j + 128]
            keep_out[at : at + HALF_CH, :] = piece[:HALF_CH]
            send_out[at : at + HALF_CH, :] = piece[HALF_CH:]

    put(12, tn(own_first(cot_s[...]).astype(BF16), act[...]))
    put(6, tn(own_first(nm_s[...]), dpre_s[...].astype(BF16)))
    g_qkv = tn(own_first(normed_s[...]).astype(BF16), dqkv_s[...].astype(BF16))
    g_out = tn(own_first(mixed_s[...]).astype(BF16), dproj_s[...].astype(BF16))
    put(0, jnp.concatenate([g_qkv, g_out], axis=1))
    small[...] = jnp.zeros_like(small)
    for i, total in enumerate((land_sum, gain_a_sum, gain_m_sum)):
        total = total * factor
        small[2 * i : 2 * i + 1, :] = total[:, 0:128]
        small[2 * i + 1 : 2 * i + 2, 0:64] = total[:, 128:192]
    keep_out[TILED:SUMS, :] = jnp.where(core == 1, small[...], 0.0).astype(BF16)
    send_out[TILED:SUMS, :] = jnp.where(core == 1, 0.0, small[...]).astype(BF16)
    keep_out[SUMS:SENT, :] = msg[core]
    send_out[SUMS:SENT, :] = msg[1 - core]


def pair_kernel(kept, arrived, chunks, x_send, x_keep):
    core = lax.axis_index("core")
    here = lax.axis_index("xh")
    for g in range(GROUP):
        at = UNIT * g
        total = kept[at : at + UNIT, :].astype(F32) + arrived[at : at + UNIT, :].astype(F32)
        chunks[g] = total.astype(BF16)
    own = pl.ds(pl.multiple_of(SUMS + QUARTER * here, 64), QUARTER)
    other = pl.ds(pl.multiple_of(SUMS + QUARTER * (1 - here), 64), QUARTER)
    x_send[core] = kept[other, :]
    x_send[1 - core] = arrived[other, :]
    x_keep[core] = kept[own, :]
    x_keep[1 - core] = arrived[own, :]


def group_kernel(terms, total_out):
    total = terms[0].astype(F32)
    for g in range(1, GROUP):
        total = total + terms[g].astype(F32)
    total = total.astype(BF16)
    for g in range(8):
        total_out[g] = total


def column_kernel(terms, kept, arrived, total_out, near, to_lon, to_lat, to_both):
    here = lax.axis_index("xh")
    half = QUARTER // 2
    for c in range(2):
        near[2 * here + c] = kept[c, 0:half, :]
        near[2 * (1 - here) + c] = arrived[c, 0:half, :]
        to_lon[2 * here + c] = kept[c, half:QUARTER, :]
        to_lon[2 * (1 - here) + c] = arrived[c, half:QUARTER, :]
    to_lat[...] = near[3]
    to_both[...] = to_lon[3]
    total = terms[0].astype(F32)
    for g in range(1, 8):
        total = total + terms[g].astype(F32)
    total = total.astype(BF16)
    for g in range(GROUP):
        total_out[g] = total


def unpack_kernel(own, other, g_qkv, g_out, g_up, g_down, g_land, g_ga, g_gm):
    core = lax.axis_index("core")
    for rows, half in ((core, own), (1 - core, other)):
        to = pl.ds(pl.multiple_of(HALF_CH * rows, 32), HALF_CH)

        def tile(t):
            return half[HALF_CH * t : HALF_CH * t + HALF_CH, :].astype(F32)

        for j in range(4):
            g_qkv[to, 128 * j : 128 * j + 128] = tile(j)
        mid = tile(4)
        g_qkv[to, 512:576] = mid[:, 0:64]
        g_out[to, :] = jnp.concatenate([mid[:, 64:128], tile(5)], axis=1)
        for j in range(6):
            g_up[to, 128 * j : 128 * j + 128] = tile(6 + j)
            g_down[to, 128 * j : 128 * j + 128] = tile(12 + j)
    little = jnp.where(
        core == 1, own[TILED : TILED + 16, :].astype(F32), other[TILED : TILED + 16, :].astype(F32)
    )
    for i, out in enumerate((g_land, g_ga, g_gm)):
        out[...] = jnp.concatenate(
            [little[2 * i : 2 * i + 1, :], little[2 * i + 1 : 2 * i + 2, 0:64]], axis=1
        )


def state_kernel(near, from_lon, from_lat, from_both, state_out):
    for first, wide, edge in ((6, near, from_lat), (0, from_lon, from_both)):
        for tile, lanes in ((0, slice(0, 128)), (1, slice(128, 192))):
            n = lanes.stop - lanes.start
            at = slice(BLOCK * tile, BLOCK * tile + BLOCK)
            before = edge[at, :].astype(F32)
            for c in range(6):
                state_out[first + c, 0:3, lanes] = before[6 * c + 3 : 6 * c + 6, 0:n]
            for k in range(4):
                block = wide[k, at, :].astype(F32)
                tall = 6 if k < 3 else 3
                for c in range(6):
                    state_out[first + c, 6 * k + 3 : 6 * k + 3 + tall, lanes] = block[
                        6 * c : 6 * c + tall, 0:n
                    ]


def hop(value, rows, cols, xh=0, cores=((0, 0), (1, 1))):
    pairs = []
    for h in range(2):
        for source, target in cores:
            for a in range(8):
                for b in range(8):
                    k = 2 * ((h + xh) % 2) + target
                    to = (k * 8 + (a + rows) % 8) * 8 + (b + cols) % 8
                    pairs.append((((2 * h + source) * 8 + a) * 8 + b, to))
    return lax.ppermute(value, AXES, pairs)


def swap(value, axis):
    return lax.ppermute(value, axis, [(0, 1), (1, 0)])


def exchange(value, axis):
    return lax.all_to_all(value, axis, 0, 0, tiled=True)


def call(kernel, name, outs, scratch=(), mib=8, from_hbm=0):
    specs = {}
    if from_hbm:
        specs["in_specs"] = [pl.BlockSpec(memory_space=pltpu.HBM)] * from_hbm
    return pl.pallas_call(
        kernel,
        out_shape=tuple(jax.ShapeDtypeStruct(dims, kind) for dims, kind in outs),
        scratch_shapes=[pltpu.VMEM(dims, kind) if kind else dims for dims, kind in scratch],
        compiler_params=pltpu.CompilerParams(vmem_limit_bytes=mib * MIB),
        name=name,
        **specs,
    )


def local(
    states, loss_grads, land_sea, land_embed, gain_attn, gain_mlp, w_qkv, w_out, w_up, w_down
):
    keep, send, edge, vectors, w_qkv = call(
        pack_kernel,
        "pack_cells",
        [((2, 2, TALL, MSG), BF16)] * 2 + [((2, 24, MSG), BF16), ((8, CH), F32)]
        + [((CH, 3 * CH), BF16)],
        [
            ((WIN_LON, ROWS, CH), BF16),
            ((WIN_LON, ROWS, CH), BF16),
            ((WIN_LON, ROWS), jnp.int32),
            ((8, CH), F32),
            ((2, 2, 2, TALL, MSG), F32),
            ((2, 24, MSG), F32),
            (pltpu.SemaphoreType.DMA((7,)), None),
        ],
        from_hbm=7,
    )(
        *(
            pltpu.with_memory_space_constraint(value, pltpu.HBM)
            for value in (
                states[0, 0].transpose(1, 0, 2), loss_grads[0, 0].transpose(1, 0, 2), land_sea.T,
                land_embed[None], gain_attn[None], gain_mlp[None], w_qkv,
            )
        )
    )
    near_own, near_x, lon_own, lon_x = call(
        sort_kernel,
        "sort_windows",
        [((2, TALL, MSG), BF16)] * 4,
        [((2, 2, 2, TALL, MSG), F32)],
    )(
        keep, swap(send, "core"),
        hop(edge, -1, 0, cores=((0, 1),)), hop(edge, -1, 0, cores=((1, 1),)),
    )
    lon_x = hop(lon_x, 0, -1, 1)
    near_x = hop(near_x, 0, 0, 1)
    lon_own = hop(lon_own, 0, -1)
    send, keep = call(
        main_kernel,
        "window_steps",
        [((SENT, 128), BF16)] * 2,
        [
            ((STEPS, WIN, CH), F32),
            ((STEPS, WIN, CH), F32),
            ((WIN, CH), F32),
            ((TOK, 3 * CH), F32),
            ((STEPS, WIN, HEADS * WIN), F32),
            ((STEPS, HEADS * WIN, CH), BF16),
            ((TOK, CH), F32),
            ((TOK, CH), F32),
            ((TOK, 1), F32),
            ((TOK, CH), F32),
            ((TOK, 1), F32),
            ((TOK, MLP), F32),
            ((TOK, MLP), BF16),
            ((TOK, CH), F32),
            ((TOK, CH), F32),
            ((TOK, CH), BF16),
            ((TOK, CH), F32),
            ((TOK, MLP), F32),
            ((TOK, CH), F32),
            ((TOK, 3 * CH), F32),
            ((WIN, 256), F32),
            ((SUMS - TILED, 128), F32),
            ((2, 2 * QUARTER, 128), BF16),
        ],
        mib=24,
    )(
        lon_x, near_x, lon_own, near_own, vectors, w_qkv, w_out, w_up, w_down.T
    )

    chunks, x_send, x_keep = call(
        pair_kernel,
        "sum_cores",
        [((GROUP, UNIT, 128), BF16)] + [((2, QUARTER, 128), BF16)] * 2,
    )(keep, swap(send, "core"))
    x_arrived = swap(x_send, "xh")
    (partial,) = call(group_kernel, "sum_group", [((8, UNIT, 128), BF16)])(
        exchange(chunks, ("xh", "lon"))
    )
    total, near, to_lon, to_lat, to_both = call(
        column_kernel,
        "sum_column",
        [((GROUP, UNIT, 128), BF16)]
        + [((4, QUARTER // 2, 128), BF16)] * 2
        + [((QUARTER // 2, 128), BF16)] * 2,
    )(exchange(partial, "lat"), x_keep, x_arrived)
    from_lon = hop(to_lon, 0, 1)
    from_lat = hop(to_lat, 1, 0)
    from_both = hop(to_both, 1, 1)
    own, from_lon, from_lat, from_both = lax.optimization_barrier(
        (exchange(total, ("xh", "lon")), from_lon, from_lat, from_both)
    )
    own = own.reshape(SUMS, 128)
    (state_grads,) = call(state_kernel, "unpack_states", [((WIN_LON, ROWS, CH), F32)])(
        near, from_lon, from_lat, from_both
    )
    outs = call(
        unpack_kernel,
        "unpack_sums",
        [
            ((CH, 3 * CH), F32),
            ((CH, CH), F32),
            ((CH, MLP), F32),
            ((CH, MLP), F32),
            ((1, CH), F32),
            ((1, CH), F32),
            ((1, CH), F32),
        ],
        mib=16,
    )(own, swap(own, "core"))
    return (
        state_grads.transpose(1, 0, 2)[None, None],
        outs[0], outs[1], outs[2], outs[3].T, outs[4][0], outs[5][0], outs[6][0],
    )


def solution(mesh):
    halves = Mesh(mesh.devices.reshape(2, 2, *mesh.devices.shape[1:]), AXES)
    cell = P(("xh", "core"), None, "lat", "lon", None)
    return jax.shard_map(
        local,
        mesh=halves,
        in_specs=(cell, cell, P("lat", "lon"), P(), P(), P(), P(), P(), P(), P()),
        out_specs=(cell, P(), P(), P(), P(), P(), P(), P()),
        check_vma=False,
    )
```
